32 devices in a mesh: seq: 8 (over z, y), tp: 4 (over x, core).
Axes of the slice: x: 2, y: 2, z: 4, core: 2. Of those that a mesh axis runs over, the one named last changes fastest.
Arguments:
- tokens: bfloat16 [4, 2048, 2048], P(None, 'seq'), may hold values from -6 to 6
- norm1_gain: bfloat16 [2048], P('seq'), may hold values from 0.5 to 1.5
- in_weight: bfloat16 [2048, 2, 2816], P('seq', None, 'tp'), may hold values from -0.125 to 0.125
- conv_weight: bfloat16 [4, 2816], P(None, 'tp'), may hold values from -3 to 3
- conv_bias: bfloat16 [2816], P('tp'), may hold values from -1.5 to 1.5
- gate_matrix: bfloat16 [2, 16, 176, 176], P(None, 'tp'), may hold values from -0.4375 to 0.4375
- gate_bias: bfloat16 [2, 2816], P(None, 'tp'), may hold values from -4 to 4
- decay_rate: bfloat16 [2816], P('tp'), may hold values from 0.00012207031 to 0.019897461
- out_weight: bfloat16 [2816, 2048], P('tp', 'seq'), may hold values from -0.3125 to 0.3125
- norm2_gain: bfloat16 [2048], P('seq'), may hold values from 0.5 to 1.5
- mlp_weight: bfloat16 [2048, 2, 6144], P('seq', None, 'tp'), may hold values from -0.125 to 0.125
- down_weight: bfloat16 [6144, 2048], P('tp', 'seq'), may hold values from -0.15625 to 0.15625
- cotangent: bfloat16 [4, 2048, 2048], P(None, 'seq'), may hold values from -6 to 6
Outputs:
- output: bfloat16 [4, 2048, 2048], P(None, 'seq')
- grad_tokens: float32 [4, 2048, 2048], P(None, 'seq')
- grad_norm1_gain: float32 [2048], P('seq')
- grad_in_weight: float32 [2048, 2, 2816], P('seq', None, 'tp')
- grad_conv_weight: float32 [4, 2816], P(None, 'tp')
- grad_conv_bias: float32 [2816], P('tp')
- grad_gate_weight: float32 [2, 16, 176, 176], P(None, 'tp')
- grad_gate_bias: float32 [2, 2816], P(None, 'tp')
- grad_decay_rate: float32 [2816], P('tp')
- grad_out_weight: float32 [2816, 2048], P('tp', 'seq')
- grad_norm2_gain: float32 [2048], P('seq')
- grad_mlp_weight: float32 [2048, 2, 6144], P('seq', None, 'tp')
- grad_down_weight: float32 [6144, 2048], P('tp', 'seq')
The draws below stay inside these ranges and needn't reach their ends.
All inputs are finite; a program needn't handle non-finite values.
Results may differ from the reference program's by a relative error of at most 0.018.
Values may be sent and summed in bfloat16 or wider, within the bound.
No kernel may reach another device: no remote copies, remote signals or barrier semaphores. Data moves between devices by JAX's collectives and lax.ppermute only.
A program may use at most 320 MiB of HBM per device.

```python
import math
import jax
import jax.numpy as jnp
from jax import lax

D = 2048
RNN = 2816
HEADS = 16
FF = 6144
CONV = 4
SEQS = 4
HEAD_WIDTH = 176
LEN = 2048


def block_levels(stream_key, shape, cuts, low, largest):
    def one(position, parts):
        heights = jax.random.uniform(jax.random.fold_in(jax.random.fold_in(stream_key, 6), position), (parts,), jnp.float32, low / len(cuts), largest / len(cuts))
        return jnp.repeat(jnp.exp(heights), shape[position] // parts).reshape((-1,) + (1,) * (len(shape) - position - 1))

    factor_of = one(*cuts[0])
    for cut in cuts[1:]:
        factor_of = factor_of * one(*cut)
    return factor_of


def normal_values(own_key, shape, width, reach, cuts=(), dtype=jnp.bfloat16):
    values = width * jax.random.normal(own_key, shape, jnp.float32)
    if cuts:
        values = values * block_levels(own_key, shape, cuts, -0.22, 0.18)
    return jnp.clip(values, -reach, reach).astype(dtype)


def setup_inputs(seed: int = 0) -> dict:
    streams_of = jax.random.split(jax.random.key(seed), 14)
    tokens = normal_values(streams_of[0], (SEQS, LEN, D), 1.0, 6.0, ((1, 8),))
    norm1_gain = jnp.clip(1.0 + 0.1 * jax.random.normal(streams_of[1], (D,), jnp.float32), 0.5, 1.5).astype(jnp.bfloat16)
    in_weight = normal_values(streams_of[2], (D, 2, RNN), D ** -0.5, 0.125, ((0, 8), (2, 4)))
    conv_weight = normal_values(streams_of[3], (CONV, RNN), CONV ** -0.5, 3.0, ((1, 4),))
    conv_bias = normal_values(streams_of[4], (RNN,), 0.3, 1.5, ((0, 4),))
    gate_matrix = normal_values(streams_of[5], (2, HEADS, HEAD_WIDTH, HEAD_WIDTH), HEAD_WIDTH ** -0.5, 0.4375, ((1, 4),))
    gate_bias = normal_values(streams_of[6], (2, RNN), 1.0, 4.0, ((1, 4),))
    decay_rate = jnp.clip(jnp.exp(math.log(0.019897461) - 5.09375 * jax.random.uniform(streams_of[7], (RNN,), jnp.float32) ** block_levels(streams_of[7], (RNN,), ((0, 4),), -0.2, 0.2)), 0.00012207031, 0.019897461).astype(jnp.bfloat16)
    out_weight = normal_values(streams_of[8], (RNN, D), (RNN // 8) ** -0.5, 0.3125, ((0, 4), (1, 8)))
    norm2_gain = jnp.clip(1.0 + 0.1 * jax.random.normal(streams_of[9], (D,), jnp.float32), 0.5, 1.5).astype(jnp.bfloat16)
    mlp_weight = normal_values(streams_of[10], (D, 2, FF), D ** -0.5, 0.125, ((0, 8), (2, 4)))
    down_weight = normal_values(streams_of[11], (FF, D), (FF // 4) ** -0.5, 0.15625, ((0, 4), (1, 8)))
    cotangent = normal_values(streams_of[12], (SEQS, LEN, D), 1.0, 6.0, ((1, 8),))
    return dict(tokens=tokens, norm1_gain=norm1_gain, in_weight=in_weight, conv_weight=conv_weight, conv_bias=conv_bias, gate_matrix=gate_matrix, gate_bias=gate_bias, decay_rate=decay_rate, out_weight=out_weight, norm2_gain=norm2_gain, mlp_weight=mlp_weight, down_weight=down_weight, cotangent=cotangent)


eps = 1e-06
highest = lax.Precision.HIGHEST

@jax.custom_vjp
def low(v):
    return lax.optimization_barrier(v.astype(jnp.bfloat16)).astype(jnp.float32)

@jax.custom_vjp
def low_back(v):
    return v

def low_keep(v):
    return (low(v), None)

def low_pass(kept, grad):
    return (grad,)

def back_keep(v):
    return (v, None)

def back_low(kept, grad):
    return (low(grad),)
low.defvjp(low_keep, low_pass)
low_back.defvjp(back_keep, back_low)

def root_norm(values, gain):
    inverse = lax.rsqrt(lax.optimization_barrier(jnp.mean(values * values, axis=-1, keepdims=True)) + eps)
    return values * inverse * gain

def layer(start, params):
    norm1_gain, in_weight, conv_weight, conv_bias, gate_matrix, gate_bias, decay_rate, out_weight, norm2_gain, mlp_weight, down_weight = params
    length = start.shape[0]
    lanes = in_weight.shape[2]
    taps = conv_weight.shape[0]
    heads = gate_matrix.shape[1]
    head_width = gate_matrix.shape[2]
    normed1 = low(root_norm(start, norm1_gain))
    branches = low(low_back(jnp.einsum('td,dkr->tkr', normed1, in_weight, precision=highest)))
    inner = branches[:, 0]
    gate_in = branches[:, 1]
    padded = jnp.concatenate([jnp.zeros((taps - 1, lanes), jnp.float32), inner], axis=0)
    conv_total = jnp.zeros((length, lanes), jnp.float32)
    for lag in range(taps):
        conv_total = conv_total + conv_weight[lag] * padded[taps - 1 - lag:taps - 1 - lag + length]
    mixed = low_back(conv_bias + conv_total)
    heads_in = low(mixed).reshape(length, heads, head_width)
    gates = jnp.einsum('thi,khij->kthj', heads_in, gate_matrix, precision=highest).reshape(2, length, lanes)
    gates = low_back(gates + gate_bias[:, None, :])
    recur = jax.nn.sigmoid(gates[0])
    admit = jax.nn.sigmoid(gates[1])
    log_decay = -8.0 * recur * decay_rate
    decay = jnp.exp(log_decay)
    drive = jnp.sqrt(-jnp.expm1(2.0 * log_decay)) * admit * mixed

    def advance(state, pair):
        state = pair[0] * state + pair[1]
        return (state, state)
    _, states = lax.scan(advance, jnp.zeros((lanes,), jnp.float32), (decay, drive))
    product = low(states * jax.nn.gelu(gate_in))
    recurrent = low_back(jnp.dot(product, out_weight, precision=highest))
    middle = start + recurrent
    normed2 = low(root_norm(middle, norm2_gain))
    both = low(low_back(jnp.einsum('td,dkf->tkf', normed2, mlp_weight, precision=highest)))
    hidden = low(jax.nn.gelu(both[:, 0]) * both[:, 1])
    return middle + low_back(jnp.dot(hidden, down_weight, precision=highest))

def reference(tokens, norm1_gain, in_weight, conv_weight, conv_bias, gate_matrix, gate_bias, decay_rate, out_weight, norm2_gain, mlp_weight, down_weight, cotangent):
    params = (norm1_gain.astype(jnp.float32), in_weight.astype(jnp.float32), conv_weight.astype(jnp.float32), conv_bias.astype(jnp.float32), gate_matrix.astype(jnp.float32), gate_bias.astype(jnp.float32), decay_rate.astype(jnp.float32), out_weight.astype(jnp.float32), norm2_gain.astype(jnp.float32), mlp_weight.astype(jnp.float32), down_weight.astype(jnp.float32))

    def one_sequence(total, pair):
        seq_in, seq_cot = pair
        result, pull = jax.vjp(layer, seq_in.astype(jnp.float32), params)
        grad_in, parameter_gradients = pull(seq_cot.astype(jnp.float32))
        total = jax.tree.map(lambda first, second: first + second, total, parameter_gradients)
        return (total, (result.astype(jnp.bfloat16), grad_in))
    zeros = jax.tree.map(jnp.zeros_like, params)
    total, (outputs, grad_tokens) = lax.scan(one_sequence, zeros, (tokens, cotangent))
    return (outputs, grad_tokens, total[0], total[1], total[2], total[3], total[4], total[5], total[6], total[7], total[8], total[9], total[10])
```

```python
import functools
import math

import jax
import jax.numpy as jnp
from jax import lax
from jax.experimental import pallas as pl
from jax.experimental.pallas import tpu as pltpu
from jax.sharding import PartitionSpec as P

f32 = jnp.float32
bf16 = jnp.bfloat16
eps = 1e-06
gelu_scale = math.sqrt(2.0 / math.pi)
step_rows = 16
pad_rows = 8
vmem_bytes = 48 * 2**20
ring_most = 8
lane_depth = 2
norm_rows = 128


def ring_order(n):
    return [*range(0, n, 2), *range(n - 1 - n % 2, 0, -2)]


class Lane:
    def __init__(self, order, by, depth):
        n = len(order)
        self.pairs = [(order[i], order[(i + by) % n]) for i in range(n)]
        self.depth = depth
        self.sent = []

    def send(self, message):
        if len(self.sent) >= self.depth:
            message = lax.optimization_barrier((message, self.sent[-self.depth]))[0]
        arrived = lax.ppermute(message, "seq", self.pairs)
        self.sent.append(arrived)
        return arrived


def gather(first, second, right, left, n, chunk):
    half = n // 2
    if n > ring_most:
        both = [lax.all_gather(p, "seq")[chunk] for p in (first, second)]
        return [[p[k] for k in range(n)] for p in both]
    ra, la, rb, lb = [first], [first], [second], [second]
    for _ in range(half - 1):
        ra.append(right.send(ra[-1]))
        la.append(left.send(la[-1]))
        rb.append(right.send(rb[-1]))
        lb.append(left.send(lb[-1]))
    far_a = right.send(ra[-1])
    far_b = left.send(lb[-1])
    return ra + [far_a] + la[:0:-1], rb + [far_b] + lb[:0:-1]


def scatter(first, second, right, left, n, chunk):
    half = n // 2
    if n > ring_most:
        slot = jnp.argsort(chunk)
        both = [jnp.stack([p(k).astype(bf16) for k in range(n)])[slot] for p in (first, second)]
        return [lax.psum_scatter(p, "seq", scatter_dimension=0).astype(f32) for p in both]
    chains = [
        (first, right, list(range(half, n))),
        (second, left, list(range(half, 0, -1))),
        (second, right, list(range(half + 1, n))),
        (first, left, list(range(half - 1, 0, -1))),
    ]
    arrived = [None] * 4
    for step in range(half):
        for i, (part, lane, slots) in enumerate(chains):
            if step < len(slots):
                total = part(slots[step])
                if arrived[i] is not None:
                    total = total + arrived[i].astype(f32)
                arrived[i] = lane.send(total.astype(bf16))
    total_a, total_b = first(0), second(0)
    for i in (0, 3):
        if arrived[i] is not None:
            total_a = total_a + arrived[i].astype(f32)
    for i in (1, 2):
        if arrived[i] is not None:
            total_b = total_b + arrived[i].astype(f32)
    return total_a, total_b


def core_swap(values):
    size = lax.axis_size("tp")
    return lax.ppermute(values, "tp", [(i, i ^ 1) for i in range(size)])


def chip_swap(values):
    size = lax.axis_size("tp")
    return lax.ppermute(values, "tp", [(i, i ^ 2) for i in range(size)])


def tp_sum(part, cuts):
    got = [core_swap(part(1, q).astype(bf16)) for q in range(cuts)]
    chip = [(part(0, q) + got[q].astype(f32)).astype(bf16) for q in range(cuts)]
    total = [(c.astype(f32) + chip_swap(c).astype(f32)).astype(bf16) for c in chip]
    other = [core_swap(t) for t in total]
    return jnp.concatenate(total + other, axis=0)


def gelu_parts(x):
    t = jnp.tanh(gelu_scale * (x + 0.044715 * x * x * x))
    value = 0.5 * x * (1.0 + t)
    slope = 0.5 * (1.0 + t) + 0.5 * x * (1.0 - t * t) * gelu_scale * (1.0 + 3 * 0.044715 * x * x)
    return value, slope


def drive_square(log_decay, decay):
    y = -2.0 * log_decay
    series = 1.0 - y * (1.0 / 9.0)
    for k in range(8, 1, -1):
        series = 1.0 - y * (1.0 / k) * series
    return jnp.where(y < 0.5, y * series, 1.0 - decay * decay)


def scan_block(a, b, rows, reverse):
    count = a.shape[0]
    by = 1
    while by < count:
        turn = count - by if reverse else by
        pa = pltpu.roll(a, turn, 0)
        pb = pltpu.roll(b, turn, 0)
        inside = rows < count - by if reverse else rows >= by
        b = jnp.where(inside, a * pb + b, b)
        a = jnp.where(inside, a * pa, a)
        by *= 2
    return a, b


def forward_kernel(
    inner, before, conv_w, conv_b, gate_m, gate_b, rate,
    mixed, recur, admit, decay, cum, local, ends, ext, gates,
):
    length, lanes = inner.shape
    ext[:pad_rows] = before[...]
    ext[pad_rows:] = inner[...].astype(f32)
    taps = conv_w.shape[0]
    total = jnp.broadcast_to(conv_b[...], (length, lanes))
    for lag in range(taps):
        total = total + conv_w[lag : lag + 1] * ext[pad_rows - lag : pad_rows - lag + length]
    mixed[...] = total
    low = total.astype(bf16)
    for k in range(2):
        gates[k] = jnp.dot(low, gate_m[k], preferred_element_type=f32) + gate_b[k : k + 1]
    rows = lax.broadcasted_iota(jnp.int32, (step_rows, lanes), 0)

    def step(i, carry):
        at = pl.ds(pl.multiple_of(i * step_rows, step_rows), step_rows)
        r = jax.nn.sigmoid(gates[0, at])
        g = jax.nn.sigmoid(gates[1, at])
        log_decay = -8.0 * r * rate[...]
        d = jnp.exp(log_decay)
        drive = jnp.sqrt(drive_square(log_decay, d)) * g * mixed[at]
        recur[at] = r
        admit[at] = g
        decay[at] = d
        a, b = scan_block(d, drive, rows, False)
        b = b + a * carry[1]
        a = a * carry[0]
        cum[at] = a
        local[at] = b
        return a[step_rows - 1 :], b[step_rows - 1 :]

    a, b = lax.fori_loop(
        0, length // step_rows, step, (jnp.ones((1, lanes), f32), jnp.zeros((1, lanes), f32))
    )
    ends[0:1] = a
    ends[1:2] = b
    ends[2:] = jnp.zeros((pad_rows - 2, lanes), f32)


def reverse_kernel(grad_product, gate_in, decay, tail, grad, first, nexts):
    length, lanes = gate_in.shape
    nexts[...] = pltpu.roll(decay[...], length - 1, 0)
    nexts[length - 1 :] = jnp.ones((1, lanes), f32)
    rows = lax.broadcasted_iota(jnp.int32, (step_rows, lanes), 0)
    steps = length // step_rows

    def step(i, carry):
        at = pl.ds(pl.multiple_of((steps - 1 - i) * step_rows, step_rows), step_rows)
        x = gate_in[at].astype(f32)
        direct = grad_product[at] * gelu_parts(x)[0]
        a, b = scan_block(nexts[at], direct, rows, True)
        b = b + a * carry[1]
        a = a * carry[0]
        tail[at] = a
        grad[at] = b
        return a[:1], b[:1]

    a, b = lax.fori_loop(0, steps, step, (jnp.ones((1, lanes), f32), jnp.zeros((1, lanes), f32)))
    first[0:1] = decay[0:1] * a
    first[1:2] = decay[0:1] * b
    first[2:] = jnp.zeros((pad_rows - 2, lanes), f32)


def gates_back_kernel(
    grad_product, gate_in, tail, grad, incoming, cum, local, entry, recur, admit, decay, mixed, gate_m, rate,
    grad_gates, grad_mixed, grad_gate_in, sums, previous, grad_mix,
):
    length, lanes = gate_in.shape
    enter = entry[0:1]
    later = incoming[0:1]
    previous[0:pad_rows] = jnp.broadcast_to(enter, (pad_rows, lanes))
    previous[pad_rows:] = local[...] + cum[...] * enter

    def step(i, carry):
        row = pl.multiple_of(i * step_rows, step_rows)
        at = pl.ds(row, step_rows)
        x = gate_in[at].astype(f32)
        slope = gelu_parts(x)[1]
        states = previous[pl.ds(row + pad_rows, step_rows)]
        head = previous[pl.ds(row, pad_rows)]
        rows = lax.broadcasted_iota(jnp.int32, (step_rows, lanes), 0)
        before = jnp.where(rows == 0, head[pad_rows - 1 :], pltpu.roll(states, 1, 0))
        grad_gate_in[at] = (slope * (grad_product[at] * states)).astype(bf16)
        total = grad[at] + tail[at] * later
        r, g, d, mix = recur[at], admit[at], decay[at], mixed[at]
        root = jnp.sqrt(drive_square(-8.0 * r * rate[...], d))
        grad_mix[at] = total * root * g
        both = total * mix
        gate1 = both * root * g * (1.0 - g)
        grad_log = total * before * d - both * g * d * d / root
        gate0 = -8.0 * rate[...] * grad_log * r * (1.0 - r)
        low0 = gate0.astype(bf16)
        low1 = gate1.astype(bf16)
        grad_gates[0, at] = low0
        grad_gates[1, at] = low1
        return (
            carry[0] - 8.0 * (grad_log * r),
            carry[1] + low0.astype(f32),
            carry[2] + low1.astype(f32),
        )

    zero = jnp.zeros((step_rows, lanes), f32)
    totals = lax.fori_loop(0, length // step_rows, step, (zero, zero, zero))
    back = grad_mix[...]
    for k in range(2):
        back = back + lax.dot_general(
            grad_gates[k], gate_m[k], (((1,), (1,)), ((), ())), preferred_element_type=f32
        )
    low = back.astype(bf16)
    grad_mixed[...] = low

    @pl.when(pl.program_id(0) == 0)
    def _():
        sums[...] = jnp.zeros_like(sums)

    for k in range(3):
        sums[k : k + 1] += jnp.sum(totals[k], axis=0, keepdims=True)
    sums[3:4] += jnp.sum(low.astype(f32), axis=0, keepdims=True)


def conv_back_kernel(grad_mixed, after, inner, before, conv_w, grad_inner, sums, grad_ext, ext):
    length, lanes = inner.shape
    taps = conv_w.shape[0]
    ext[:pad_rows] = before[...]
    ext[pad_rows:] = inner[...].astype(f32)
    grad_ext[length:] = after[...]
    grad = grad_mixed[...].astype(f32)
    grad_ext[:length] = grad

    @pl.when(pl.program_id(0) == 0)
    def _():
        sums[...] = jnp.zeros_like(sums)

    total = jnp.zeros((length, lanes), f32)
    for lag in range(taps):
        total = total + conv_w[lag : lag + 1] * grad_ext[lag : lag + length]
        term = grad * ext[pad_rows - lag : pad_rows - lag + length]
        sums[lag : lag + 1] += jnp.sum(term, axis=0, keepdims=True)
    grad_inner[...] = total.astype(bf16)


def per_sequence(kernel, seqs, inputs, outputs, scratch, flops):
    def spec(shape, kind):
        if kind == "whole":
            return pl.BlockSpec(shape, lambda s: (0,) * len(shape))
        if kind == "pair":
            return pl.BlockSpec((shape[0], None) + shape[2:], lambda s: (0, s, 0, 0))
        return pl.BlockSpec((None,) + shape[1:], lambda s: (s,) + (0,) * (len(shape) - 1))

    moved = sum(a.size * a.dtype.itemsize for a, _ in inputs)
    moved += sum(math.prod(shape) * jnp.dtype(t).itemsize for shape, t, _ in outputs)
    return pl.pallas_call(
        kernel,
        grid=(seqs,),
        in_specs=[spec(a.shape, kind) for a, kind in inputs],
        out_specs=[spec(shape, kind) for shape, _, kind in outputs],
        out_shape=[jax.ShapeDtypeStruct(shape, t) for shape, t, _ in outputs],
        scratch_shapes=scratch,
        compiler_params=pltpu.CompilerParams(vmem_limit_bytes=vmem_bytes),
        cost_estimate=pl.CostEstimate(flops=flops, bytes_accessed=moved, transcendentals=0),
    )(*[a for a, _ in inputs])


def moved_bytes(*arrays):
    return sum(math.prod(a.shape) * jnp.dtype(a.dtype).itemsize for a in arrays)


def by_rows(kernel, arrays, whole, outputs, sums, order=None, back=False):
    seqs, length, width = arrays[0].shape
    block = min(norm_rows, length)
    near = pl.BlockSpec((None, block, width), lambda s, r, *_: (s, r, 0))
    far = pl.BlockSpec((None, block, width), lambda s, r, sequence, chunk: (sequence[s], r, 0))
    moves = order is not None
    total = pl.BlockSpec((pad_rows, width), lambda s, r, *_: (0, 0))
    out_shape = [jax.ShapeDtypeStruct((seqs, length, width), t) for t in outputs]
    out_shape += [jax.ShapeDtypeStruct((pad_rows, width), f32)] * sums
    return pl.pallas_call(
        kernel,
        grid_spec=pltpu.PrefetchScalarGridSpec(
            num_scalar_prefetch=2 if moves else 0,
            grid=(seqs, length // block),
            in_specs=[far if moves and not back else near] * len(arrays)
            + [pl.BlockSpec(w.shape, lambda s, r, *_: (0, 0)) for w in whole],
            out_specs=[far if moves and back else near] * len(outputs) + [total] * sums,
        ),
        out_shape=out_shape,
        compiler_params=pltpu.CompilerParams(vmem_limit_bytes=vmem_bytes),
        cost_estimate=pl.CostEstimate(
            flops=8 * seqs * length * width,
            bytes_accessed=moved_bytes(*arrays, *out_shape),
            transcendentals=0,
        ),
    )(*(order if moves else ()), *arrays, *whole)


def enter_kernel(sequence, chunk, *refs):
    count = len(refs) // 2
    part = refs[0].shape[1] // chunk.shape[0]
    for k in range(chunk.shape[0]):
        at = pl.ds(pl.multiple_of(chunk[k] * part, part), part)
        for i in range(count):
            refs[count + i][:, k * part : (k + 1) * part] = refs[i][:, at]


def norm_kernel(x, added, gain, middle, normed):
    total = x[...].astype(f32) + added[...].astype(f32)
    middle[...] = total
    inverse = lax.rsqrt(jnp.mean(total * total, axis=-1, keepdims=True) + eps)
    normed[...] = (total * inverse * gain[...]).astype(bf16)


def norm_back(values, grad, gain):
    inverse = lax.rsqrt(jnp.mean(values * values, axis=-1, keepdims=True) + eps)
    scaled = values * inverse
    weighted = grad * gain
    inner = jnp.mean(weighted * scaled, axis=-1, keepdims=True)
    return inverse * (weighted - scaled * inner), grad * scaled


def add_rows(total, values):
    @pl.when((pl.program_id(0) == 0) & (pl.program_id(1) == 0))
    def _():
        total[...] = jnp.zeros_like(total)

    rows, width = values.shape
    total[...] += jnp.sum(values.reshape(rows // pad_rows, pad_rows, width), axis=0)


def middle_back_kernel(middle, grad_normed, cot, gain, grad_middle, grad_low, total):
    grad, terms = norm_back(middle[...], grad_normed[...].astype(f32), gain[...])
    grad = grad + cot[...].astype(f32)
    grad_middle[...] = grad
    grad_low[...] = grad.astype(bf16)
    add_rows(total, terms)


def put_chunks(chunk, target, values):
    part = values.shape[1] // chunk.shape[0]
    for k in range(chunk.shape[0]):
        at = pl.ds(pl.multiple_of(chunk[k] * part, part), part)
        target[:, at] = values[:, k * part : (k + 1) * part]


def start_back_kernel(sequence, chunk, x, grad_normed, grad_middle, gain, grad_tokens, total):
    grad, terms = norm_back(x[...].astype(f32), grad_normed[...].astype(f32), gain[...])
    put_chunks(chunk, grad_tokens, grad + grad_middle[...])
    add_rows(total, terms)


def output_kernel(sequence, chunk, middle, added, output):
    put_chunks(chunk, output, (middle[...] + added[...].astype(f32)).astype(bf16))


def own_order(array, order, back=False):
    sequence, chunk = order
    if back:
        sequence, chunk = jnp.argsort(sequence), jnp.argsort(chunk)
    seqs, length, width = array.shape
    chunks = chunk.shape[0]
    split = array[sequence].reshape(seqs, length, chunks, width // chunks)
    return split[:, :, chunk].reshape(array.shape)


def carried(ends, way, n):
    def shifted(values, by):
        pairs = [(i, i + way * by) for i in range(n) if 0 <= i + way * by < n]
        return lax.ppermute(values, "seq", pairs)

    ends = ends[:, :2]
    by = 1
    while 2 * by < n:
        earlier = shifted(ends, by)
        ends = ends[:, :1] * earlier + jnp.concatenate(
            [jnp.zeros_like(ends[:, 1:]), ends[:, 1:]], axis=1
        )
        by *= 2
    near, far = shifted(ends, 1), shifted(ends, 1 + by)
    state = near[:, :1] * far[:, 1:] + near[:, 1:]
    return jnp.pad(state, ((0, 0), (0, pad_rows - 1), (0, 0)))


def seq_sum(values, n):
    by = 1
    while by < n:
        values = values + lax.ppermute(values, "seq", [(i, i ^ by) for i in range(n)])
        by *= 2
    return values


def dense_heads(matrix):
    kinds, heads, width, _ = matrix.shape
    rows = [
        jnp.pad(matrix[:, h], ((0, 0), (0, 0), (h * width, (heads - 1 - h) * width)))
        for h in range(heads)
    ]
    return jnp.concatenate(rows, axis=1)


def across(a, b):
    return lax.dot_general(a, b, (((1,), (1,)), ((), ())), preferred_element_type=f32)


def down(a, b):
    return lax.dot_general(a, b, (((0,), (0,)), ((), ())), preferred_element_type=f32)


def dot(a, b):
    return jnp.dot(a, b, preferred_element_type=f32)


def shards(
    tokens,
    norm1_gain,
    in_weight,
    conv_weight,
    conv_bias,
    gate_matrix,
    gate_bias,
    decay_rate,
    out_weight,
    norm2_gain,
    mlp_weight,
    down_weight,
    cotangent,
):
    seqs, piece, width = tokens.shape
    rows = seqs * piece
    lanes = in_weight.shape[2]
    units = mlp_weight.shape[2]
    heads, head_width = gate_matrix.shape[1:3]
    taps = conv_weight.shape[0]
    n = lax.axis_size("seq")
    part = width // n
    order = ring_order(n)
    place = [order.index(i) for i in range(n)]
    me = jnp.asarray(place, jnp.int32)[lax.axis_index("seq")]
    chunk = jnp.asarray(order, jnp.int32)[(me - jnp.arange(n, dtype=jnp.int32)) % n]
    odd = lax.axis_index("tp") % 2
    sequence = (jnp.arange(seqs, dtype=jnp.int32) + odd * (seqs // 2)) % seqs
    move = (sequence, chunk)
    right, left = Lane(order, 1, lane_depth), Lane(order, -1, lane_depth)
    tiled = part % 128 == 0

    def sl(a, k):
        return a[:, k * part : (k + 1) * part]

    w_in = jnp.transpose(in_weight, (1, 2, 0))
    half_lanes = lanes // 2
    half_units = units // 2
    own_gain = jnp.pad(jnp.stack([norm1_gain, norm2_gain]), ((0, 14), (0, 0)))
    first, second = gather(
        jnp.concatenate([w_in[0], out_weight[:half_lanes]], axis=0),
        jnp.concatenate([w_in[1], out_weight[half_lanes:], own_gain], axis=0),
        right,
        left,
        n,
        chunk,
    )
    mlp0, mlp1 = gather(mlp_weight[:, 0], mlp_weight[:, 1], right, left, n, chunk)
    down0, down1 = gather(
        down_weight[:half_units], down_weight[half_units:], right, left, n, chunk
    )
    in0 = [p[:lanes] for p in first]
    in1 = [p[:lanes] for p in second]
    gains = [p[lanes + half_lanes : lanes + half_lanes + 2] for p in second]
    gain1, gain2 = (
        jnp.concatenate([g[i : i + 1] for g in gains], axis=1).astype(f32) for i in range(2)
    )

    if tiled:
        x, cot = by_rows(enter_kernel, [tokens, cotangent], [], [bf16, bf16], 0, move)
    else:
        x, cot = own_order(tokens, move), own_order(cotangent, move)
    full = x.shape
    grad_low = cot.reshape(rows, width)
    start = x.reshape(rows, width).astype(f32)
    inverse1 = lax.rsqrt(jnp.mean(start * start, axis=-1, keepdims=True) + eps)
    normed1 = [
        (sl(start, k) * inverse1 * gains[k][:1].astype(f32)).astype(bf16) for k in range(n)
    ]
    inner = sum(across(normed1[k], in0[k]) for k in range(n)).astype(bf16)
    gate_in = sum(across(normed1[k], in1[k]) for k in range(n)).astype(bf16)
    inner = inner.reshape(seqs, piece, lanes)
    gate_in = gate_in.reshape(seqs, piece, lanes)
    before = lax.ppermute(
        inner[:, piece - taps + 1 :], "seq", [(i, i + 1) for i in range(n - 1)]
    ).astype(f32)
    before = jnp.pad(before, ((0, 0), (pad_rows - taps + 1, 0), (0, 0)))
    conv_w = conv_weight.astype(f32)
    rate = decay_rate.astype(f32)[None]
    gate_m = dense_heads(gate_matrix)
    wide = (seqs, piece, lanes)
    edge = (seqs, pad_rows, lanes)
    gate_flops = 4 * rows * lanes * lanes
    mixed, recur, admit, decay, cum, local, ends = per_sequence(
        forward_kernel,
        seqs,
        [
            (inner, "seq"),
            (before, "seq"),
            (conv_w, "whole"),
            (conv_bias.astype(f32)[None], "whole"),
            (gate_m, "whole"),
            (gate_bias.astype(f32), "whole"),
            (rate, "whole"),
        ],
        [(wide, f32, "seq")] * 6 + [(edge, f32, "seq")],
        [pltpu.VMEM((piece + pad_rows, lanes), f32), pltpu.VMEM((2, piece, lanes), f32)],
        gate_flops,
    )
    entry = carried(ends, 1, n)
    product = (
        ((local + cum * entry[:, :1]) * jax.nn.gelu(gate_in.astype(f32)))
        .astype(bf16)
        .reshape(rows, lanes)
    )
    w_out = jnp.concatenate(
        [
            jnp.concatenate([p[lanes : lanes + half_lanes] for p in pieces], axis=1)
            for pieces in (first, second)
        ],
        axis=0,
    )
    cuts = 1
    block = rows // (2 * cuts)

    def rows_of(a, h, q):
        begin = (h * cuts + q) * block
        return a[begin : begin + block]

    recurrent = tp_sum(lambda h, q: dot(rows_of(product, h, q), w_out), cuts)

    middle, normed2 = by_rows(norm_kernel, [x, recurrent.reshape(full)], [gain2], [f32, bf16], 0)
    normed2 = normed2.reshape(rows, width)
    w_mlp = jnp.concatenate(
        [jnp.concatenate(mlp0, axis=0), jnp.concatenate(mlp1, axis=0)], axis=1
    )
    both = dot(normed2, w_mlp).astype(bf16).astype(f32)
    both0, both1 = both[:, :units], both[:, units:]
    act, slope = gelu_parts(both0)
    hidden = (act * both1).astype(bf16)
    grad_down = scatter(
        lambda k: down(hidden[:, :half_units], sl(grad_low, k)),
        lambda k: down(hidden[:, half_units:], sl(grad_low, k)),
        right,
        left,
        n,
        chunk,
    )
    w_down = jnp.concatenate(
        [jnp.concatenate(down0, axis=1), jnp.concatenate(down1, axis=1)], axis=0
    )
    grad_hidden = across(grad_low, w_down)
    grad_both = jnp.concatenate(
        [(grad_hidden * both1 * slope).astype(bf16), (grad_hidden * act).astype(bf16)], axis=1
    )
    grad_normed2 = tp_sum(lambda h, q: across(rows_of(grad_both, h, q), w_mlp), cuts)
    grad_mlp = scatter(
        lambda k: down(sl(normed2, k), grad_both[:, :units]),
        lambda k: down(sl(normed2, k), grad_both[:, units:]),
        right,
        left,
        n,
        chunk,
    )
    mlp_out = tp_sum(lambda h, q: dot(rows_of(hidden, h, q), w_down), cuts)

    grad_middle, grad_rec, sum_gain2 = by_rows(
        middle_back_kernel,
        [middle, grad_normed2.reshape(full), cot],
        [gain2],
        [f32, bf16],
        1,
    )
    grad_rec = grad_rec.reshape(rows, width)

    grad_product = across(grad_rec, w_out).reshape(wide)
    tail, local_grad, first = per_sequence(
        reverse_kernel,
        seqs,
        [(grad_product, "seq"), (gate_in, "seq"), (decay, "seq")],
        [(wide, f32, "seq")] * 2 + [(edge, f32, "seq")],
        [pltpu.VMEM((piece, lanes), f32)],
        rows * lanes * 50,
    )
    incoming = carried(first, -1, n)
    grad_gates, grad_mixed, grad_gate_in, sums = per_sequence(
        gates_back_kernel,
        seqs,
        [
            (grad_product, "seq"),
            (gate_in, "seq"),
            (tail, "seq"),
            (local_grad, "seq"),
            (incoming, "seq"),
            (cum, "seq"),
            (local, "seq"),
            (entry, "seq"),
            (recur, "seq"),
            (admit, "seq"),
            (decay, "seq"),
            (mixed, "seq"),
            (gate_m, "whole"),
            (rate, "whole"),
        ],
        [
            ((2,) + wide, bf16, "pair"),
            (wide, bf16, "seq"),
            (wide, bf16, "seq"),
            ((pad_rows, lanes), f32, "whole"),
        ],
        [pltpu.VMEM((piece + pad_rows, lanes), f32), pltpu.VMEM((piece, lanes), f32)],
        gate_flops,
    )
    after = lax.ppermute(
        grad_mixed[:, : taps - 1], "seq", [(i + 1, i) for i in range(n - 1)]
    ).astype(f32)
    after = jnp.pad(after, ((0, 0), (0, pad_rows - taps + 1), (0, 0)))
    grad_inner, conv_sums = per_sequence(
        conv_back_kernel,
        seqs,
        [
            (grad_mixed, "seq"),
            (after, "seq"),
            (inner, "seq"),
            (before, "seq"),
            (conv_w, "whole"),
        ],
        [(wide, bf16, "seq"), ((pad_rows, lanes), f32, "whole")],
        [pltpu.VMEM((piece + pad_rows, lanes), f32)] * 2,
        rows * lanes * 16,
    )
    back0 = grad_inner.reshape(rows, lanes)
    back1 = grad_gate_in.reshape(rows, lanes)
    back = jnp.concatenate([back0, back1], axis=1)
    w_both = jnp.concatenate(
        [jnp.concatenate(in0, axis=1), jnp.concatenate(in1, axis=1)], axis=0
    )
    grad_normed1 = tp_sum(lambda h, q: dot(rows_of(back, h, q), w_both), cuts)
    low_mixed = mixed.astype(bf16).reshape(rows, lanes)
    grad_matrix = []
    for k in range(2):
        dense = down(low_mixed, grad_gates[k].reshape(rows, lanes)).astype(bf16)
        for h in range(heads):
            at = slice(h * head_width, (h + 1) * head_width)
            grad_matrix.append(dense[at, at])
    small = jnp.concatenate([sums[:4], conv_sums[:taps]], axis=0).astype(bf16)
    packed = jnp.concatenate(grad_matrix + [small.reshape(-1, head_width)], axis=0)
    packed = lax.psum(packed, "seq")
    grads = scatter(
        lambda k: jnp.concatenate(
            [down(back0, normed1[k]), down(product[:, :half_lanes], sl(grad_rec, k))], axis=0
        ),
        lambda k: jnp.concatenate(
            [down(back1, normed1[k]), down(product[:, half_lanes:], sl(grad_rec, k))], axis=0
        ),
        right,
        left,
        n,
        chunk,
    )

    if tiled:
        output = by_rows(
            output_kernel, [middle, mlp_out.reshape(full)], [], [bf16], 0, move, back=True
        )[0]
        grad_tokens, sum_gain1 = by_rows(
            start_back_kernel,
            [x, grad_normed1.reshape(full), grad_middle],
            [gain1],
            [f32],
            1,
            move,
            back=True,
        )
    else:
        output = own_order((middle + mlp_out.reshape(full).astype(f32)).astype(bf16), move, True)
        grad_start, terms = norm_back(
            x.astype(f32), grad_normed1.reshape(full).astype(f32), gain1
        )
        grad_tokens = own_order(grad_middle + grad_start, move, True)
        sum_gain1 = jnp.sum(terms, axis=(0, 1))[None]
    mine = lax.axis_index("seq")
    slots = (me - jnp.asarray(place, jnp.int32)) % n
    grad_gains = jnp.stack([jnp.sum(sum_gain1, axis=0), jnp.sum(sum_gain2, axis=0)])
    grad_gains = 0.5 * (grad_gains + core_swap(grad_gains))
    grad_gains = seq_sum(grad_gains.reshape(2, n, part)[:, slots], n)
    grad_gains = lax.dynamic_index_in_dim(grad_gains, mine, 1, keepdims=False)

    packed, grad_gains = lax.optimization_barrier((packed, grad_gains))
    packed = packed.astype(f32)
    matrix_rows = 2 * heads * head_width
    grad_matrix = packed[:matrix_rows].reshape(gate_matrix.shape)
    small = packed[matrix_rows:].reshape(4 + taps, lanes)
    return (
        output,
        grad_tokens,
        grad_gains[0],
        jnp.transpose(jnp.stack([g[:lanes] for g in grads]), (2, 0, 1)),
        small[4:],
        small[3],
        grad_matrix,
        small[1:3],
        small[0],
        jnp.concatenate([g[lanes:] for g in grads], axis=0),
        grad_gains[1],
        jnp.stack(grad_mlp, axis=1),
        jnp.concatenate(grad_down, axis=0),
    )


def solution(mesh):
    in_specs = (
        P(None, "seq", None),
        P("seq"),
        P("seq", None, "tp"),
        P(None, "tp"),
        P("tp"),
        P(None, "tp", None, None),
        P(None, "tp"),
        P("tp"),
        P("tp", "seq"),
        P("seq"),
        P("seq", None, "tp"),
        P("tp", "seq"),
        P(None, "seq", None),
    )
    out_specs = (
        P(None, "seq", None),
        P(None, "seq", None),
        P("seq"),
        P("seq", None, "tp"),
        P(None, "tp"),
        P("tp"),
        P(None, "tp", None, None),
        P(None, "tp"),
        P("tp"),
        P("tp", "seq"),
        P("seq"),
        P("seq", None, "tp"),
        P("tp", "seq"),
    )
    return jax.shard_map(shards, mesh=mesh, in_specs=in_specs, out_specs=out_specs, check_vma=False)
```

```python
import functools
import math

import jax
import jax.numpy as jnp
from jax import lax
from jax.experimental import pallas as pl
from jax.experimental.pallas import tpu as pltpu
from jax.sharding import PartitionSpec as P

f32 = jnp.float32
bf16 = jnp.bfloat16
eps = 1e-06
gelu_scale = math.sqrt(2.0 / math.pi)
step_rows = 16
pad_rows = 8
vmem_bytes = 48 * 2**20
ring_most = 8
lane_depth = 2
norm_rows = 128


def ring_order(n):
    return [*range(0, n, 2), *range(n - 1 - n % 2, 0, -2)]


def after(values, *earlier):
    return lax.optimization_barrier((values, *earlier))[0]


class Ring:
    def __init__(self, order, depth):
        n = len(order)
        self.n = n
        self.depth = depth
        self.pairs = {w: [(order[i], order[(i + w) % n]) for i in range(n)] for w in (1, -1)}
        self.queue = {1: [], -1: []}
        self.flying = {1: [], -1: []}
        self.landed = {1: [], -1: []}
        self.sent = {1: 0, -1: 0}
        self.last = {1: None, -1: None}

    def add(self, weights, delays=None):
        half = self.n // 2
        delays = delays or [0] * len(weights)
        left = {id(flow): flow.count for w in weights for flow in w.flows.values()}
        for turn in range(half + max(delays)):
            for late in (True, False):
                for weight, delay in zip(weights, delays):
                    if (delay > 0) != late or turn < delay:
                        continue
                    for way, flow in weight.flows.items():
                        if left[id(flow)]:
                            left[id(flow)] -= 1
                            self.queue[way].append(flow)

    def issue(self, most=None):
        for way in (1, -1):
            queue, flying, landed = self.queue[way], self.flying[way], self.landed[way]
            while queue and len(flying) < (most or self.depth) and not queue[0].busy:
                flow = queue.pop(0)
                message = flow.message()
                gate = self.sent[way] - self.depth
                if gate >= 0:
                    message = after(message, landed[gate])
                flow.busy = True
                self.sent[way] += 1
                self.last[way] = message
                flying.append((flow, lax.ppermute(message, "seq", self.pairs[way])))

    def hold(self, values):
        last = [message for message in self.last.values() if message is not None]
        return after(values, *last) if last else values

    def land(self, values=None, count=1):
        for turn in range(count):
            taken = [(w, *self.flying[w].pop(0)) for w in (1, -1) if self.flying[w]]
            arrived = [message for _, _, message in taken]
            if values is not None and taken and turn == count - 1:
                values, *arrived = lax.optimization_barrier((values, *arrived))
            for (way, flow, _), message in zip(taken, arrived):
                flow.arrive(message)
                flow.busy = False
                self.landed[way].append(message)
            self.issue()
        return values

    def drain(self):
        while self.queue[1] or self.queue[-1] or self.flying[1] or self.flying[-1]:
            self.land()


class Pieces:
    def __init__(self, own, count):
        self.value, self.count, self.busy, self.got = own, count, False, []

    def message(self):
        return self.value

    def arrive(self, message):
        self.value = message
        self.got.append(message)


class Totals:
    def __init__(self, part, slots):
        self.part, self.slots, self.count, self.busy = part, slots, len(slots), False
        self.got, self.at = None, 0

    def message(self):
        total = self.part(self.slots[self.at])
        if self.got is not None:
            total = total + self.got.astype(f32)
        self.at += 1
        return total.astype(bf16)

    def arrive(self, message):
        self.got = message


class Gather:
    def __init__(self, piece, far, n, chunk):
        half = n // 2
        self.piece, self.n, self.chunk, self.flows = piece, n, chunk, {}
        if n <= ring_most:
            self.flows = {w: Pieces(piece, half if w == far else half - 1) for w in (1, -1)}

    def slots(self):
        if not self.flows:
            pieces = lax.all_gather(self.piece, "seq")[self.chunk]
            return [pieces[k] for k in range(self.n)]
        return [self.piece, *self.flows[1].got, *self.flows[-1].got[::-1]]


class Scatter:
    def __init__(self, part, far, n, chunk):
        half = n // 2
        self.part, self.n, self.chunk, self.flows = part, n, chunk, {}
        if n <= ring_most:
            self.flows = {
                1: Totals(part, list(range(half if far == 1 else half + 1, n))),
                -1: Totals(part, list(range(half if far == -1 else half - 1, 0, -1))),
            }

    def total(self):
        if not self.flows:
            parts = jnp.stack([self.part(k).astype(bf16) for k in range(self.n)])
            parts = parts[jnp.argsort(self.chunk)]
            return lax.psum_scatter(parts, "seq", scatter_dimension=0).astype(f32)
        total = self.part(0)
        for flow in self.flows.values():
            if flow.got is not None:
                total = total + flow.got.astype(f32)
        return total


def core_swap(values):
    size = lax.axis_size("tp")
    return lax.ppermute(values, "tp", [(i, i ^ 1) for i in range(size)])


def chip_swap(values):
    size = lax.axis_size("tp")
    return lax.ppermute(values, "tp", [(i, i ^ 2) for i in range(size)])


def tp_sum(part, others=lambda v: v, chips=lambda v: v, totals=lambda v: v):
    got = core_swap(others(part(1).astype(bf16)))
    chip = chips((part(0) + got.astype(f32)).astype(bf16))
    far = chip_swap(chip)
    total = totals((chip.astype(f32) + far.astype(f32)).astype(bf16))
    return jnp.concatenate([total, core_swap(total)], axis=0), total


def gelu_parts(x):
    t = jnp.tanh(gelu_scale * (x + 0.044715 * x * x * x))
    value = 0.5 * x * (1.0 + t)
    slope = 0.5 * (1.0 + t) + 0.5 * x * (1.0 - t * t) * gelu_scale * (1.0 + 3 * 0.044715 * x * x)
    return value, slope


def drive_square(log_decay, decay):
    y = -2.0 * log_decay
    series = 1.0 - y * (1.0 / 9.0)
    for k in range(8, 1, -1):
        series = 1.0 - y * (1.0 / k) * series
    return jnp.where(y < 0.5, y * series, 1.0 - decay * decay)


def scan_block(a, b, rows, reverse):
    count = a.shape[0]
    by = 1
    while by < count:
        turn = count - by if reverse else by
        pa = pltpu.roll(a, turn, 0)
        pb = pltpu.roll(b, turn, 0)
        inside = rows < count - by if reverse else rows >= by
        b = jnp.where(inside, a * pb + b, b)
        a = jnp.where(inside, a * pa, a)
        by *= 2
    return a, b


def forward_kernel(
    inner, before, conv_w, conv_b, gate_m, gate_b, rate,
    mixed, recur, admit, decay, cum, local, ends, ext, gates,
):
    length, lanes = inner.shape
    ext[:pad_rows] = before[...]
    ext[pad_rows:] = inner[...].astype(f32)
    taps = conv_w.shape[0]
    total = jnp.broadcast_to(conv_b[...], (length, lanes))
    for lag in range(taps):
        total = total + conv_w[lag : lag + 1] * ext[pad_rows - lag : pad_rows - lag + length]
    mixed[...] = total
    low = total.astype(bf16)
    for k in range(2):
        gates[k] = jnp.dot(low, gate_m[k], preferred_element_type=f32) + gate_b[k : k + 1]
    rows = lax.broadcasted_iota(jnp.int32, (step_rows, lanes), 0)

    def step(i, carry):
        at = pl.ds(pl.multiple_of(i * step_rows, step_rows), step_rows)
        r = jax.nn.sigmoid(gates[0, at])
        g = jax.nn.sigmoid(gates[1, at])
        log_decay = -8.0 * r * rate[...]
        d = jnp.exp(log_decay)
        drive = jnp.sqrt(drive_square(log_decay, d)) * g * mixed[at]
        recur[at] = r
        admit[at] = g
        decay[at] = d
        a, b = scan_block(d, drive, rows, False)
        b = b + a * carry[1]
        a = a * carry[0]
        cum[at] = a
        local[at] = b
        return a[step_rows - 1 :], b[step_rows - 1 :]

    a, b = lax.fori_loop(
        0, length // step_rows, step, (jnp.ones((1, lanes), f32), jnp.zeros((1, lanes), f32))
    )
    ends[0:1] = a
    ends[1:2] = b
    ends[2:] = jnp.zeros((pad_rows - 2, lanes), f32)


def reverse_kernel(grad_product, gate_in, decay, tail, grad, first, nexts):
    length, lanes = gate_in.shape
    nexts[...] = pltpu.roll(decay[...], length - 1, 0)
    nexts[length - 1 :] = jnp.ones((1, lanes), f32)
    rows = lax.broadcasted_iota(jnp.int32, (step_rows, lanes), 0)
    steps = length // step_rows

    def step(i, carry):
        at = pl.ds(pl.multiple_of((steps - 1 - i) * step_rows, step_rows), step_rows)
        x = gate_in[at].astype(f32)
        direct = grad_product[at] * gelu_parts(x)[0]
        a, b = scan_block(nexts[at], direct, rows, True)
        b = b + a * carry[1]
        a = a * carry[0]
        tail[at] = a
        grad[at] = b
        return a[:1], b[:1]

    a, b = lax.fori_loop(0, steps, step, (jnp.ones((1, lanes), f32), jnp.zeros((1, lanes), f32)))
    first[0:1] = decay[0:1] * a
    first[1:2] = decay[0:1] * b
    first[2:] = jnp.zeros((pad_rows - 2, lanes), f32)


def gates_back_kernel(
    grad_product, gate_in, tail, grad, incoming, cum, local, entry, recur, admit, decay, mixed, gate_m, rate,
    grad_gates, grad_mixed, grad_gate_in, sums, previous, grad_mix,
):
    length, lanes = gate_in.shape
    enter = entry[0:1]
    later = incoming[0:1]
    previous[0:pad_rows] = jnp.broadcast_to(enter, (pad_rows, lanes))
    previous[pad_rows:] = local[...] + cum[...] * enter

    def step(i, carry):
        row = pl.multiple_of(i * step_rows, step_rows)
        at = pl.ds(row, step_rows)
        x = gate_in[at].astype(f32)
        slope = gelu_parts(x)[1]
        states = previous[pl.ds(row + pad_rows, step_rows)]
        head = previous[pl.ds(row, pad_rows)]
        rows = lax.broadcasted_iota(jnp.int32, (step_rows, lanes), 0)
        before = jnp.where(rows == 0, head[pad_rows - 1 :], pltpu.roll(states, 1, 0))
        grad_gate_in[at] = (slope * (grad_product[at] * states)).astype(bf16)
        total = grad[at] + tail[at] * later
        r, g, d, mix = recur[at], admit[at], decay[at], mixed[at]
        root = jnp.sqrt(drive_square(-8.0 * r * rate[...], d))
        grad_mix[at] = total * root * g
        both = total * mix
        gate1 = both * root * g * (1.0 - g)
        grad_log = total * before * d - both * g * d * d / root
        gate0 = -8.0 * rate[...] * grad_log * r * (1.0 - r)
        low0 = gate0.astype(bf16)
        low1 = gate1.astype(bf16)
        grad_gates[0, at] = low0
        grad_gates[1, at] = low1
        return (
            carry[0] - 8.0 * (grad_log * r),
            carry[1] + low0.astype(f32),
            carry[2] + low1.astype(f32),
        )

    zero = jnp.zeros((step_rows, lanes), f32)
    totals = lax.fori_loop(0, length // step_rows, step, (zero, zero, zero))
    back = grad_mix[...]
    for k in range(2):
        back = back + lax.dot_general(
            grad_gates[k], gate_m[k], (((1,), (1,)), ((), ())), preferred_element_type=f32
        )
    low = back.astype(bf16)
    grad_mixed[...] = low

    @pl.when(pl.program_id(0) == 0)
    def _():
        sums[...] = jnp.zeros_like(sums)

    for k in range(3):
        sums[k : k + 1] += jnp.sum(totals[k], axis=0, keepdims=True)
    sums[3:4] += jnp.sum(low.astype(f32), axis=0, keepdims=True)


def conv_back_kernel(grad_mixed, behind, inner, before, conv_w, grad_inner, sums, grad_ext, ext):
    length, lanes = inner.shape
    taps = conv_w.shape[0]
    ext[:pad_rows] = before[...]
    ext[pad_rows:] = inner[...].astype(f32)
    grad_ext[length:] = behind[...]
    grad = grad_mixed[...].astype(f32)
    grad_ext[:length] = grad

    @pl.when(pl.program_id(0) == 0)
    def _():
        sums[...] = jnp.zeros_like(sums)

    total = jnp.zeros((length, lanes), f32)
    for lag in range(taps):
        total = total + conv_w[lag : lag + 1] * grad_ext[lag : lag + length]
        term = grad * ext[pad_rows - lag : pad_rows - lag + length]
        sums[lag : lag + 1] += jnp.sum(term, axis=0, keepdims=True)
    grad_inner[...] = total.astype(bf16)


def per_sequence(kernel, seqs, inputs, outputs, scratch, flops):
    def spec(shape, kind):
        if kind == "whole":
            return pl.BlockSpec(shape, lambda s: (0,) * len(shape))
        if kind == "pair":
            return pl.BlockSpec((shape[0], None) + shape[2:], lambda s: (0, s, 0, 0))
        return pl.BlockSpec((None,) + shape[1:], lambda s: (s,) + (0,) * (len(shape) - 1))

    moved = sum(a.size * a.dtype.itemsize for a, _ in inputs)
    moved += sum(math.prod(shape) * jnp.dtype(t).itemsize for shape, t, _ in outputs)
    return pl.pallas_call(
        kernel,
        grid=(seqs,),
        in_specs=[spec(a.shape, kind) for a, kind in inputs],
        out_specs=[spec(shape, kind) for shape, _, kind in outputs],
        out_shape=[jax.ShapeDtypeStruct(shape, t) for shape, t, _ in outputs],
        scratch_shapes=scratch,
        compiler_params=pltpu.CompilerParams(vmem_limit_bytes=vmem_bytes),
        cost_estimate=pl.CostEstimate(flops=flops, bytes_accessed=moved, transcendentals=0),
    )(*[a for a, _ in inputs])


def moved_bytes(*arrays):
    return sum(math.prod(a.shape) * jnp.dtype(a.dtype).itemsize for a in arrays)


def by_rows(kernel, arrays, whole, outputs, sums, order=None, back=False, moved=()):
    seqs, length, width = arrays[0].shape
    block = min(norm_rows, length)
    near = pl.BlockSpec((None, block, width), lambda s, r, *_: (s, r, 0))
    far = pl.BlockSpec((None, block, width), lambda s, r, sequence, chunk: (sequence[s], r, 0))
    moves = order is not None
    total = pl.BlockSpec((pad_rows, width), lambda s, r, *_: (0, 0))
    out_shape = [jax.ShapeDtypeStruct((seqs, length, width), t) for t in outputs]
    out_shape += [jax.ShapeDtypeStruct((pad_rows, width), f32)] * sums
    return pl.pallas_call(
        kernel,
        grid_spec=pltpu.PrefetchScalarGridSpec(
            num_scalar_prefetch=2 if moves else 0,
            grid=(seqs, length // block),
            in_specs=[
                far if moves and (not back or i in moved) else near for i in range(len(arrays))
            ]
            + [pl.BlockSpec(w.shape, lambda s, r, *_: (0, 0)) for w in whole],
            out_specs=[far if moves and back else near] * len(outputs) + [total] * sums,
        ),
        out_shape=out_shape,
        compiler_params=pltpu.CompilerParams(vmem_limit_bytes=vmem_bytes),
        cost_estimate=pl.CostEstimate(
            flops=8 * seqs * length * width,
            bytes_accessed=moved_bytes(*arrays, *out_shape),
            transcendentals=0,
        ),
    )(*(order if moves else ()), *arrays, *whole)


def enter_kernel(sequence, chunk, *refs):
    count = len(refs) // 2
    part = refs[0].shape[1] // chunk.shape[0]
    for k in range(chunk.shape[0]):
        at = pl.ds(pl.multiple_of(chunk[k] * part, part), part)
        for i in range(count):
            refs[count + i][:, k * part : (k + 1) * part] = refs[i][:, at]


def norm_kernel(x, added, gain, middle, normed):
    total = x[...].astype(f32) + added[...].astype(f32)
    middle[...] = total
    inverse = lax.rsqrt(jnp.mean(total * total, axis=-1, keepdims=True) + eps)
    normed[...] = (total * inverse * gain[...]).astype(bf16)


def norm_back(values, grad, gain):
    inverse = lax.rsqrt(jnp.mean(values * values, axis=-1, keepdims=True) + eps)
    scaled = values * inverse
    weighted = grad * gain
    inner = jnp.mean(weighted * scaled, axis=-1, keepdims=True)
    return inverse * (weighted - scaled * inner), grad * scaled


def add_rows(total, values):
    @pl.when((pl.program_id(0) == 0) & (pl.program_id(1) == 0))
    def _():
        total[...] = jnp.zeros_like(total)

    rows, width = values.shape
    total[...] += jnp.sum(values.reshape(rows // pad_rows, pad_rows, width), axis=0)


def middle_back_kernel(middle, grad_normed, cot, gain, grad_middle, grad_low, total):
    grad, terms = norm_back(middle[...], grad_normed[...].astype(f32), gain[...])
    grad = grad + cot[...].astype(f32)
    grad_middle[...] = grad
    grad_low[...] = grad.astype(bf16)
    add_rows(total, terms)


def put_chunks(chunk, target, values):
    part = values.shape[1] // chunk.shape[0]
    for k in range(chunk.shape[0]):
        at = pl.ds(pl.multiple_of(chunk[k] * part, part), part)
        target[:, at] = values[:, k * part : (k + 1) * part]


def start_back_kernel(sequence, chunk, x, grad_normed, grad_middle, gain, grad_tokens):
    grad = norm_back(x[...].astype(f32), grad_normed[...].astype(f32), gain[...])[0]
    put_chunks(chunk, grad_tokens, grad + grad_middle[...])


def output_kernel(sequence, chunk, middle, added, output):
    put_chunks(chunk, output, (middle[...] + added[...].astype(f32)).astype(bf16))


def own_order(array, order, back=False):
    sequence, chunk = order
    if back:
        sequence, chunk = jnp.argsort(sequence), jnp.argsort(chunk)
    seqs, length, width = array.shape
    chunks = chunk.shape[0]
    split = array[sequence].reshape(seqs, length, chunks, width // chunks)
    return split[:, :, chunk].reshape(array.shape)


def carried(ends, way, n, between=lambda v: v):
    def shifted(values, by):
        pairs = [(i, i + way * by) for i in range(n) if 0 <= i + way * by < n]
        return lax.ppermute(values, "seq", pairs)

    ends = ends[:, :2]
    by = 1
    while 2 * by < n:
        earlier = shifted(ends, by)
        ends = ends[:, :1] * earlier + jnp.concatenate(
            [jnp.zeros_like(ends[:, 1:]), ends[:, 1:]], axis=1
        )
        by *= 2
        if by == 2:
            ends = between(ends)
    near, far = shifted(ends, 1), shifted(ends, 1 + by)
    state = near[:, :1] * far[:, 1:] + near[:, 1:]
    return jnp.pad(state, ((0, 0), (0, pad_rows - 1), (0, 0)))


def seq_sum(values, n):
    by = 1
    while by < n:
        values = values + lax.ppermute(values, "seq", [(i, i ^ by) for i in range(n)])
        by *= 2
    return values


def dense_heads(matrix):
    kinds, heads, width, _ = matrix.shape
    rows = [
        jnp.pad(matrix[:, h], ((0, 0), (0, 0), (h * width, (heads - 1 - h) * width)))
        for h in range(heads)
    ]
    return jnp.concatenate(rows, axis=1)


def across(a, b):
    return lax.dot_general(a, b, (((1,), (1,)), ((), ())), preferred_element_type=f32)


def down(a, b):
    return lax.dot_general(a, b, (((0,), (0,)), ((), ())), preferred_element_type=f32)


def dot(a, b):
    return jnp.dot(a, b, preferred_element_type=f32)


def shards(
    tokens,
    norm1_gain,
    in_weight,
    conv_weight,
    conv_bias,
    gate_matrix,
    gate_bias,
    decay_rate,
    out_weight,
    norm2_gain,
    mlp_weight,
    down_weight,
    cotangent,
):
    seqs, piece, width = tokens.shape
    rows = seqs * piece
    lanes = in_weight.shape[2]
    units = mlp_weight.shape[2]
    heads, head_width = gate_matrix.shape[1:3]
    taps = conv_weight.shape[0]
    n = lax.axis_size("seq")
    part = width // n
    order = ring_order(n)
    place = [order.index(i) for i in range(n)]
    me = jnp.asarray(place, jnp.int32)[lax.axis_index("seq")]
    chunk = jnp.asarray(order, jnp.int32)[(me - jnp.arange(n, dtype=jnp.int32)) % n]
    odd = lax.axis_index("tp") % 2
    sequence = (jnp.arange(seqs, dtype=jnp.int32) + odd * (seqs // 2)) % seqs
    move = (sequence, chunk)
    ring = Ring(order, lane_depth)
    tiled = part % 128 == 0

    def sl(a, k):
        return a[:, k * part : (k + 1) * part]

    w_in = jnp.transpose(in_weight, (1, 2, 0))
    half_lanes = lanes // 2
    own_gain = jnp.pad(jnp.stack([norm1_gain, norm2_gain]), ((0, 14), (0, 0)))
    first = Gather(jnp.concatenate([w_in[0], out_weight[:half_lanes]], axis=0), 1, n, chunk)
    second = Gather(
        jnp.concatenate([w_in[1], out_weight[half_lanes:], own_gain], axis=0), -1, n, chunk
    )
    mlp = [Gather(mlp_weight[:, 0], 1, n, chunk), Gather(mlp_weight[:, 1], -1, n, chunk)]
    downs = Gather(down_weight, 1, n, chunk)
    ring.add([first, second])
    ring.add([*mlp, downs], [0, 0, 2])
    ring.issue()

    tokens, cotangent = ring.land((tokens, cotangent))
    move = (sequence, chunk)
    if tiled:
        x, cot = by_rows(enter_kernel, [tokens, cotangent], [], [bf16, bf16], 0, move)
    else:
        x, cot = own_order(tokens, move), own_order(cotangent, move)
    full = x.shape
    x, cot = ring.land((x, cot))
    grad_low = cot.reshape(rows, width)
    start = x.reshape(rows, width).astype(f32)
    inverse1 = lax.rsqrt(jnp.mean(start * start, axis=-1, keepdims=True) + eps)
    for _ in range(n - 3):
        ring.land()
    first, second = first.slots(), second.slots()
    in0 = [p[:lanes] for p in first]
    in1 = [p[:lanes] for p in second]
    gains = [p[lanes + half_lanes : lanes + half_lanes + 2] for p in second]
    gain1, gain2 = (
        jnp.concatenate([g[i : i + 1] for g in gains], axis=1).astype(f32) for i in range(2)
    )
    normed1 = [
        (sl(start, k) * inverse1 * gains[k][:1].astype(f32)).astype(bf16) for k in range(n)
    ]
    inner = sum(across(normed1[k], in0[k]) for k in range(n)).astype(bf16)
    gate_in = sum(across(normed1[k], in1[k]) for k in range(n)).astype(bf16)
    inner = ring.land(inner)
    inner = inner.reshape(seqs, piece, lanes)
    gate_in = gate_in.reshape(seqs, piece, lanes)
    before = lax.ppermute(
        inner[:, piece - taps + 1 :], "seq", [(i, i + 1) for i in range(n - 1)]
    ).astype(f32)
    before = jnp.pad(before, ((0, 0), (pad_rows - taps + 1, 0), (0, 0)))
    conv_w = conv_weight.astype(f32)
    rate = decay_rate.astype(f32)[None]
    gate_m = dense_heads(gate_matrix)
    wide = (seqs, piece, lanes)
    edge = (seqs, pad_rows, lanes)
    gate_flops = 4 * rows * lanes * lanes
    mixed, recur, admit, decay, cum, local, ends = per_sequence(
        forward_kernel,
        seqs,
        [
            (inner, "seq"),
            (before, "seq"),
            (conv_w, "whole"),
            (conv_bias.astype(f32)[None], "whole"),
            (gate_m, "whole"),
            (gate_bias.astype(f32), "whole"),
            (rate, "whole"),
        ],
        [(wide, f32, "seq")] * 6 + [(edge, f32, "seq")],
        [pltpu.VMEM((piece + pad_rows, lanes), f32), pltpu.VMEM((2, piece, lanes), f32)],
        gate_flops,
    )
    ends = ring.land(ends)
    entry = ring.land(carried(ends, 1, n, ring.land))
    product = (
        ((local + cum * entry[:, :1]) * jax.nn.gelu(gate_in.astype(f32)))
        .astype(bf16)
        .reshape(rows, lanes)
    )
    w_out = jnp.concatenate(
        [
            jnp.concatenate([p[lanes : lanes + half_lanes] for p in pieces], axis=1)
            for pieces in (first, second)
        ],
        axis=0,
    )
    block = rows // 2

    def half_of(a, h):
        return a[h * block : (h + 1) * block]

    def wait_land(values, count):
        for _ in range(count):
            ring.land()
        return ring.land(values)

    recurrent, _ = tp_sum(
        lambda h: dot(half_of(product, h), w_out),
        chips=ring.land,
        totals=lambda v: wait_land(v, 3),
    )

    middle, normed2 = by_rows(norm_kernel, [x, recurrent.reshape(full)], [gain2], [f32, bf16], 0)
    normed2 = ring.land(normed2.reshape(rows, width))
    w_mlp = jnp.concatenate(
        [jnp.concatenate(w.slots(), axis=0) for w in mlp], axis=1
    )
    both = dot(normed2, w_mlp).astype(bf16)
    both0, both1 = both[:, :units].astype(f32), both[:, units:].astype(f32)
    hidden = (gelu_parts(both0)[0] * both1).astype(bf16)
    hidden, both = ring.land((hidden, both))
    ring.drain()
    w_down = jnp.concatenate(downs.slots(), axis=1)
    grad_down = Scatter(lambda k: down(hidden, sl(grad_low, k)), 1, n, chunk)
    grad_both = []
    grad_mlp = [
        Scatter(lambda k: down(sl(normed2, k), grad_both[0][:, :units]), -1, n, chunk),
        Scatter(lambda k: down(sl(normed2, k), grad_both[0][:, units:]), 1, n, chunk),
    ]
    ring.add([grad_down, *grad_mlp])
    ring.issue(1)
    both, w_down = ring.hold((both, w_down))
    both0, both1 = both[:, :units].astype(f32), both[:, units:].astype(f32)
    act, slope = gelu_parts(both0)
    grad_hidden = across(grad_low, w_down)
    grad_both.append(
        jnp.concatenate(
            [(grad_hidden * both1 * slope).astype(bf16), (grad_hidden * act).astype(bf16)],
            axis=1,
        )
    )
    grad_both[0] = ring.land(grad_both[0])
    grad_normed2, total2 = tp_sum(
        lambda h: across(half_of(grad_both[0], h), w_mlp),
        others=ring.land,
        chips=ring.land,
        totals=lambda v: wait_land(v, 2),
    )
    turned = jnp.concatenate([half_of(hidden, 1), half_of(hidden, 0)], axis=0)
    turned = jnp.where(odd == 1, turned, hidden)
    mlp_out = lax.psum(dot(after(turned, total2), w_down).astype(bf16), "tp")

    grad_middle, grad_rec, sum_gain2 = by_rows(
        middle_back_kernel,
        [middle, grad_normed2.reshape(full), cot],
        [gain2],
        [f32, bf16],
        1,
    )
    grad_rec = grad_rec.reshape(rows, width)

    grad_rec = ring.land(grad_rec)
    grad_product = across(grad_rec, w_out).reshape(wide)
    tail, local_grad, first = per_sequence(
        reverse_kernel,
        seqs,
        [(grad_product, "seq"), (gate_in, "seq"), (decay, "seq")],
        [(wide, f32, "seq")] * 2 + [(edge, f32, "seq")],
        [pltpu.VMEM((piece, lanes), f32)],
        rows * lanes * 50,
    )
    incoming = carried(ring.land(first), -1, n, ring.land)
    grad_gates, grad_mixed, grad_gate_in, sums = per_sequence(
        gates_back_kernel,
        seqs,
        [
            (grad_product, "seq"),
            (gate_in, "seq"),
            (tail, "seq"),
            (local_grad, "seq"),
            (incoming, "seq"),
            (cum, "seq"),
            (local, "seq"),
            (entry, "seq"),
            (recur, "seq"),
            (admit, "seq"),
            (decay, "seq"),
            (mixed, "seq"),
            (gate_m, "whole"),
            (rate, "whole"),
        ],
        [
            ((2,) + wide, bf16, "pair"),
            (wide, bf16, "seq"),
            (wide, bf16, "seq"),
            ((pad_rows, lanes), f32, "whole"),
        ],
        [pltpu.VMEM((piece + pad_rows, lanes), f32), pltpu.VMEM((piece, lanes), f32)],
        gate_flops,
    )
    grad_mixed = ring.land(grad_mixed)
    behind = lax.ppermute(
        grad_mixed[:, : taps - 1], "seq", [(i + 1, i) for i in range(n - 1)]
    ).astype(f32)
    behind = jnp.pad(behind, ((0, 0), (0, pad_rows - taps + 1), (0, 0)))
    behind = ring.land(behind)
    grad_inner, conv_sums = per_sequence(
        conv_back_kernel,
        seqs,
        [
            (grad_mixed, "seq"),
            (behind, "seq"),
            (inner, "seq"),
            (before, "seq"),
            (conv_w, "whole"),
        ],
        [(wide, bf16, "seq"), ((pad_rows, lanes), f32, "whole")],
        [pltpu.VMEM((piece + pad_rows, lanes), f32)] * 2,
        rows * lanes * 16,
    )
    back0 = grad_inner.reshape(rows, lanes)
    back1 = grad_gate_in.reshape(rows, lanes)
    back = jnp.concatenate([back0, back1], axis=1)
    w_both = jnp.concatenate(
        [jnp.concatenate(in0, axis=1), jnp.concatenate(in1, axis=1)], axis=0
    )
    ring.drain()
    grads = [
        Scatter(
            lambda k: jnp.concatenate(
                [down(back0, normed1[k]), down(product[:, :half_lanes], sl(grad_rec, k))], axis=0
            ),
            1,
            n,
            chunk,
        ),
        Scatter(
            lambda k: jnp.concatenate(
                [down(back1, normed1[k]), down(product[:, half_lanes:], sl(grad_rec, k))], axis=0
            ),
            -1,
            n,
            chunk,
        ),
    ]
    ring.add(grads)
    ring.issue()
    late = []

    def hold_output(chip):
        late.append(after(mlp_out, chip))
        return chip

    grad_normed1, total1 = tp_sum(
        lambda h: dot(half_of(back, h), w_both),
        chips=hold_output,
        totals=lambda v: wait_land(v, 2),
    )
    mlp_out = late[0]
    ring.drain()
    grads = [g.total() for g in grads]
    low_mixed = mixed.astype(bf16).reshape(rows, lanes)
    grad_matrix = []
    for k in range(2):
        dense = down(low_mixed, grad_gates[k].reshape(rows, lanes)).astype(bf16)
        for h in range(heads):
            at = slice(h * head_width, (h + 1) * head_width)
            grad_matrix.append(dense[at, at])
    small = jnp.concatenate([sums[:4], conv_sums[:taps]], axis=0).astype(bf16)
    packed = jnp.concatenate(grad_matrix + [small.reshape(-1, head_width)], axis=0)
    packed = lax.psum(packed, "seq")
    if tiled:
        output = by_rows(
            output_kernel,
            [middle, mlp_out.reshape(full)],
            [],
            [bf16],
            0,
            move,
            back=True,
            moved=(1,),
        )[0]
        grad_normed1, output = after((grad_normed1, output), output)
        grad_tokens = by_rows(
            start_back_kernel,
            [x, grad_normed1.reshape(full), grad_middle],
            [gain1],
            [f32],
            0,
            move,
            back=True,
        )[0]
    else:
        mlp_out = mlp_out.reshape(full)[sequence].astype(f32)
        output = own_order((middle + mlp_out).astype(bf16), move, True)
        grad_start = norm_back(x.astype(f32), grad_normed1.reshape(full).astype(f32), gain1)[0]
        grad_tokens = own_order(grad_middle + grad_start, move, True)
    mine = lax.axis_index("seq")
    slots = (me - jnp.asarray(place, jnp.int32)) % n
    sum_gain1 = jnp.sum(total1.astype(f32) * (start[:block] * inverse1[:block]), axis=0)
    grad_gains = jnp.stack([sum_gain1, 0.5 * jnp.sum(sum_gain2, axis=0)])
    grad_gains = grad_gains + core_swap(grad_gains)
    grad_gains = seq_sum(grad_gains.reshape(2, n, part)[:, slots], n)
    grad_gains = lax.dynamic_index_in_dim(grad_gains, mine, 1, keepdims=False)

    packed, grad_gains = lax.optimization_barrier((packed, grad_gains))
    packed = packed.astype(f32)
    matrix_rows = 2 * heads * head_width
    grad_matrix = packed[:matrix_rows].reshape(gate_matrix.shape)
    small = packed[matrix_rows:].reshape(4 + taps, lanes)
    return (
        output,
        grad_tokens,
        grad_gains[0],
        jnp.transpose(jnp.stack([g[:lanes] for g in grads]), (2, 0, 1)),
        small[4:],
        small[3],
        grad_matrix,
        small[1:3],
        small[0],
        jnp.concatenate([g[lanes:] for g in grads], axis=0),
        grad_gains[1],
        jnp.stack([g.total() for g in grad_mlp], axis=1),
        grad_down.total(),
    )


def solution(mesh):
    in_specs = (
        P(None, "seq", None),
        P("seq"),
        P("seq", None, "tp"),
        P(None, "tp"),
        P("tp"),
        P(None, "tp", None, None),
        P(None, "tp"),
        P("tp"),
        P("tp", "seq"),
        P("seq"),
        P("seq", None, "tp"),
        P("tp", "seq"),
        P(None, "seq", None),
    )
    out_specs = (
        P(None, "seq", None),
        P(None, "seq", None),
        P("seq"),
        P("seq", None, "tp"),
        P(None, "tp"),
        P("tp"),
        P(None, "tp", None, None),
        P(None, "tp"),
        P("tp"),
        P("tp", "seq"),
        P("seq"),
        P("seq", None, "tp"),
        P("tp", "seq"),
    )
    return jax.shard_map(shards, mesh=mesh, in_specs=in_specs, out_specs=out_specs, check_vma=False)
```

```python
import functools
import math

import jax
import jax.numpy as jnp
from jax import lax
from jax.experimental import pallas as pl
from jax.experimental.pallas import tpu as pltpu
from jax.sharding import PartitionSpec as P

f32 = jnp.float32
bf16 = jnp.bfloat16
eps = 1e-06
gelu_scale = math.sqrt(2.0 / math.pi)
step_rows = 16
pad_rows = 8
vmem_bytes = 48 * 2**20
ring_most = 8
lane_depth = 2
norm_rows = 128


def ring_order(n):
    return [*range(0, n, 2), *range(n - 1 - n % 2, 0, -2)]


def after(values, *earlier):
    return lax.optimization_barrier((values, *earlier))[0]


class Ring:
    def __init__(self, order, depth):
        n = len(order)
        self.n = n
        self.depth = depth
        self.pairs = {w: [(order[i], order[(i + w) % n]) for i in range(n)] for w in (1, -1)}
        self.queue = {1: [], -1: []}
        self.flying = {1: [], -1: []}
        self.landed = {1: [], -1: []}
        self.sent = {1: 0, -1: 0}
        self.last = {1: None, -1: None}
        self.token = None

    def add(self, weights, delays=None):
        half = self.n // 2
        delays = delays or [0] * len(weights)
        left = {id(flow): flow.count for w in weights for flow in w.flows.values()}
        for turn in range(half + max(delays)):
            for late in (True, False):
                for weight, delay in zip(weights, delays):
                    if (delay > 0) != late or turn < delay:
                        continue
                    for way, flow in weight.flows.items():
                        if left[id(flow)]:
                            left[id(flow)] -= 1
                            self.queue[way].append(flow)

    def issue(self, most=None):
        for way in (1, -1):
            queue, flying, landed = self.queue[way], self.flying[way], self.landed[way]
            while queue and len(flying) < (most or self.depth) and not queue[0].busy:
                flow = queue.pop(0)
                message = flow.message()
                gate = self.sent[way] - self.depth
                if gate >= 0:
                    message = after(message, landed[gate])
                if self.token is not None:
                    message = after(message, self.token)
                flow.busy = True
                self.sent[way] += 1
                self.last[way] = message
                flying.append((flow, lax.ppermute(message, "seq", self.pairs[way])))

    def hold(self, values):
        last = [message for message in self.last.values() if message is not None]
        return after(values, *last) if last else values

    def resume(self, token):
        self.token = token
        self.issue()
        return token

    def quiet(self, values):
        waiting = {w: self.queue[w] for w in (1, -1)}
        self.queue = {1: [], -1: []}
        for _ in range(self.depth):
            values = self.land(values)
        self.queue = waiting
        return values

    def land(self, values=None, count=1):
        for turn in range(count):
            taken = [(w, *self.flying[w].pop(0)) for w in (1, -1) if self.flying[w]]
            arrived = [message for _, _, message in taken]
            if values is not None and taken and turn == count - 1:
                values, *arrived = lax.optimization_barrier((values, *arrived))
            for (way, flow, _), message in zip(taken, arrived):
                flow.arrive(message)
                flow.busy = False
                self.landed[way].append(message)
            self.issue()
        return values

    def drain(self):
        while self.queue[1] or self.queue[-1] or self.flying[1] or self.flying[-1]:
            self.land()


class Pieces:
    def __init__(self, own, count):
        self.value, self.count, self.busy, self.got = own, count, False, []

    def message(self):
        return self.value

    def arrive(self, message):
        self.value = message
        self.got.append(message)


class Totals:
    def __init__(self, part, slots):
        self.part, self.slots, self.count, self.busy = part, slots, len(slots), False
        self.got, self.at = None, 0

    def message(self):
        total = self.part(self.slots[self.at])
        if self.got is not None:
            total = total + self.got.astype(f32)
        self.at += 1
        return total.astype(bf16)

    def arrive(self, message):
        self.got = message


class Gather:
    def __init__(self, piece, far, n, chunk):
        half = n // 2
        self.piece, self.n, self.chunk, self.flows = piece, n, chunk, {}
        if n <= ring_most:
            self.flows = {w: Pieces(piece, half if w == far else half - 1) for w in (1, -1)}

    def slots(self):
        if not self.flows:
            pieces = lax.all_gather(self.piece, "seq")[self.chunk]
            return [pieces[k] for k in range(self.n)]
        return [self.piece, *self.flows[1].got, *self.flows[-1].got[::-1]]


class Scatter:
    def __init__(self, part, far, n, chunk):
        half = n // 2
        self.part, self.n, self.chunk, self.flows = part, n, chunk, {}
        if n <= ring_most:
            self.flows = {
                1: Totals(part, list(range(half if far == 1 else half + 1, n))),
                -1: Totals(part, list(range(half if far == -1 else half - 1, 0, -1))),
            }

    def total(self):
        if not self.flows:
            parts = jnp.stack([self.part(k).astype(bf16) for k in range(self.n)])
            parts = parts[jnp.argsort(self.chunk)]
            return lax.psum_scatter(parts, "seq", scatter_dimension=0).astype(f32)
        total = self.part(0)
        for flow in self.flows.values():
            if flow.got is not None:
                total = total + flow.got.astype(f32)
        return total


def core_swap(values):
    size = lax.axis_size("tp")
    return lax.ppermute(values, "tp", [(i, i ^ 1) for i in range(size)])


def chip_swap(values):
    size = lax.axis_size("tp")
    return lax.ppermute(values, "tp", [(i, i ^ 2) for i in range(size)])


def tp_sum(part, others=lambda v: v, chips=lambda v: v, totals=lambda v: v):
    got = core_swap(others(part(1).astype(bf16)))
    chip = chips((part(0) + got.astype(f32)).astype(bf16))
    far = chip_swap(chip)
    total = totals((chip.astype(f32) + far.astype(f32)).astype(bf16))
    return total, core_swap(total)


def gelu_parts(x):
    t = jnp.tanh(gelu_scale * (x + 0.044715 * x * x * x))
    value = 0.5 * x * (1.0 + t)
    slope = 0.5 * (1.0 + t) + 0.5 * x * (1.0 - t * t) * gelu_scale * (1.0 + 3 * 0.044715 * x * x)
    return value, slope


def drive_square(log_decay, decay):
    y = -2.0 * log_decay
    series = 1.0 - y * (1.0 / 9.0)
    for k in range(8, 1, -1):
        series = 1.0 - y * (1.0 / k) * series
    return jnp.where(y < 0.5, y * series, 1.0 - decay * decay)


def scan_block(a, b, rows, reverse):
    count = a.shape[0]
    by = 1
    while by < count:
        turn = count - by if reverse else by
        pa = pltpu.roll(a, turn, 0)
        pb = pltpu.roll(b, turn, 0)
        inside = rows < count - by if reverse else rows >= by
        b = jnp.where(inside, a * pb + b, b)
        a = jnp.where(inside, a * pa, a)
        by *= 2
    return a, b


def forward_kernel(
    inner, before, conv_w, conv_b, gate_m, gate_b, rate,
    mixed, recur, admit, decay, root, cum, local, ends, ext, gates,
):
    length, lanes = inner.shape
    ext[:pad_rows] = before[...]
    ext[pad_rows:] = inner[...].astype(f32)
    taps = conv_w.shape[0]
    total = jnp.broadcast_to(conv_b[...], (length, lanes))
    for lag in range(taps):
        total = total + conv_w[lag : lag + 1] * ext[pad_rows - lag : pad_rows - lag + length]
    mixed[...] = total
    low = total.astype(bf16)
    for k in range(2):
        gates[k] = jnp.dot(low, gate_m[k], preferred_element_type=f32) + gate_b[k : k + 1]
    rows = lax.broadcasted_iota(jnp.int32, (step_rows, lanes), 0)

    def step(i, carry):
        at = pl.ds(pl.multiple_of(i * step_rows, step_rows), step_rows)
        r = jax.nn.sigmoid(gates[0, at])
        g = jax.nn.sigmoid(gates[1, at])
        log_decay = -8.0 * r * rate[...]
        d = jnp.exp(log_decay)
        m = jnp.sqrt(drive_square(log_decay, d))
        drive = m * g * mixed[at]
        root[at] = m
        recur[at] = r
        admit[at] = g
        decay[at] = d
        a, b = scan_block(d, drive, rows, False)
        b = b + a * carry[1]
        a = a * carry[0]
        cum[at] = a
        local[at] = b
        return a[step_rows - 1 :], b[step_rows - 1 :]

    a, b = lax.fori_loop(
        0, length // step_rows, step, (jnp.ones((1, lanes), f32), jnp.zeros((1, lanes), f32))
    )
    ends[0:1] = a
    ends[1:2] = b
    ends[2:] = jnp.zeros((pad_rows - 2, lanes), f32)


def reverse_kernel(grad_product, act, decay, tail, grad, first, nexts):
    length, lanes = act.shape
    nexts[...] = pltpu.roll(decay[...], length - 1, 0)
    nexts[length - 1 :] = jnp.ones((1, lanes), f32)
    rows = lax.broadcasted_iota(jnp.int32, (step_rows, lanes), 0)
    steps = length // step_rows

    def step(i, carry):
        at = pl.ds(pl.multiple_of((steps - 1 - i) * step_rows, step_rows), step_rows)
        direct = grad_product[at] * act[at]
        a, b = scan_block(nexts[at], direct, rows, True)
        b = b + a * carry[1]
        a = a * carry[0]
        tail[at] = a
        grad[at] = b
        return a[:1], b[:1]

    a, b = lax.fori_loop(0, steps, step, (jnp.ones((1, lanes), f32), jnp.zeros((1, lanes), f32)))
    first[0:1] = decay[0:1] * a
    first[1:2] = decay[0:1] * b
    first[2:] = jnp.zeros((pad_rows - 2, lanes), f32)


def gates_back_kernel(
    grad_product, slope, tail, grad, incoming, states, entry, recur, admit, decay, root, mixed, inner, before,
    gate_m, rate, conv_w, grad_gates, grad_inner, grad_gate_in, head, last, sums, grad_mix, grad_ext, ext,
):
    length, lanes = inner.shape
    enter = entry[0:1]
    later = incoming[0:1]
    taps = conv_w.shape[0]

    def step(i, carry):
        at = pl.ds(pl.multiple_of(i * step_rows, step_rows), step_rows)
        state = states[at]
        rows = lax.broadcasted_iota(jnp.int32, (step_rows, lanes), 0)
        earlier = jnp.where(rows == 0, carry[3], pltpu.roll(state, 1, 0))
        grad_gate_in[at] = (slope[at] * (grad_product[at] * state)).astype(bf16)
        total = grad[at] + tail[at] * later
        r, g, d, m, mix = recur[at], admit[at], decay[at], root[at], mixed[at]
        grad_mix[at] = total * m * g
        both = total * mix
        gate1 = both * m * g * (1.0 - g)
        grad_log = total * earlier * d - both * g * d * d / m
        gate0 = -8.0 * rate[...] * grad_log * r * (1.0 - r)
        low0 = gate0.astype(bf16)
        low1 = gate1.astype(bf16)
        grad_gates[0, at] = low0
        grad_gates[1, at] = low1
        return (
            carry[0] - 8.0 * (grad_log * r),
            carry[1] + low0.astype(f32),
            carry[2] + low1.astype(f32),
            state[step_rows - 1 :],
        )

    zero = jnp.zeros((step_rows, lanes), f32)
    totals = lax.fori_loop(0, length // step_rows, step, (zero, zero, zero, enter))
    back = grad_mix[...]
    for k in range(2):
        back = back + lax.dot_general(
            grad_gates[k], gate_m[k], (((1,), (1,)), ((), ())), preferred_element_type=f32
        )
    back = back.astype(bf16).astype(f32)
    head[...] = back[:pad_rows]
    grad_ext[:length] = back
    grad_ext[length:] = jnp.zeros((pad_rows, lanes), f32)
    ext[:pad_rows] = before[...]
    ext[pad_rows:] = inner[...].astype(f32)

    @pl.when(pl.program_id(0) == 0)
    def _():
        sums[...] = jnp.zeros_like(sums)

    for k in range(3):
        sums[k : k + 1] += jnp.sum(totals[k], axis=0, keepdims=True)
    sums[3:4] += jnp.sum(back, axis=0, keepdims=True)
    total = jnp.zeros((length, lanes), f32)
    for lag in range(taps):
        total = total + conv_w[lag : lag + 1] * grad_ext[lag : lag + length]
        term = back * ext[pad_rows - lag : pad_rows - lag + length]
        sums[4 + lag : 5 + lag] += jnp.sum(term, axis=0, keepdims=True)
    grad_inner[...] = total.astype(bf16)
    last[...] = total[length - pad_rows :]


def hidden_back_kernel(cot, w_down, act, slope, grad_both):
    units = w_down.shape[0]
    cut = math.gcd(units, 512)
    for j in range(0, units, cut):
        grad = lax.dot_general(
            cot[...], w_down[j : j + cut], (((1,), (1,)), ((), ())), preferred_element_type=f32
        )
        grad_both[:, j : j + cut] = (grad * slope[:, j : j + cut].astype(f32)).astype(bf16)
        grad_both[:, units + j : units + j + cut] = (
            grad * act[:, j : j + cut].astype(f32)
        ).astype(bf16)


def per_sequence(kernel, seqs, inputs, outputs, scratch, flops):
    def spec(shape, kind):
        if kind == "whole":
            return pl.BlockSpec(shape, lambda s: (0,) * len(shape))
        if kind == "pair":
            return pl.BlockSpec((shape[0], None) + shape[2:], lambda s: (0, s, 0, 0))
        return pl.BlockSpec((None,) + shape[1:], lambda s: (s,) + (0,) * (len(shape) - 1))

    moved = sum(a.size * a.dtype.itemsize for a, _ in inputs)
    moved += sum(math.prod(shape) * jnp.dtype(t).itemsize for shape, t, _ in outputs)
    return pl.pallas_call(
        kernel,
        grid=(seqs,),
        in_specs=[spec(a.shape, kind) for a, kind in inputs],
        out_specs=[spec(shape, kind) for shape, _, kind in outputs],
        out_shape=[jax.ShapeDtypeStruct(shape, t) for shape, t, _ in outputs],
        scratch_shapes=scratch,
        compiler_params=pltpu.CompilerParams(vmem_limit_bytes=vmem_bytes),
        cost_estimate=pl.CostEstimate(flops=flops, bytes_accessed=moved, transcendentals=0),
    )(*[a for a, _ in inputs])


def moved_bytes(*arrays):
    return sum(math.prod(a.shape) * jnp.dtype(a.dtype).itemsize for a in arrays)


def by_rows(
    kernel, arrays, whole, outputs, sums, order=None, back=False, moved=(), half=None, earlier=()
):
    seqs, length, width = arrays[0].shape
    block = min(norm_rows, length)
    count = seqs if half is None else seqs // 2
    skip = count * (half or 0)
    moves = order is not None
    tile = (None, block, width)
    near = pl.BlockSpec(tile, lambda s, r, *_: (s + skip, r, 0))
    own = pl.BlockSpec(tile, lambda s, r, *_: (s, r, 0))
    far = pl.BlockSpec(tile, lambda s, r, sequence, chunk: (sequence[s + skip], r, 0))
    total = pl.BlockSpec((pad_rows, width), lambda s, r, *_: (0, 0))
    out_shape = [jax.ShapeDtypeStruct((seqs, length, width), t) for t in outputs]
    out_shape += [jax.ShapeDtypeStruct((pad_rows, width), f32)] * sums
    scalars = 2 if moves else 0
    given = scalars + len(arrays) + len(whole)

    def body(*refs):
        kernel(*refs[:given], *refs[given + len(earlier) :])

    return pl.pallas_call(
        body,
        grid_spec=pltpu.PrefetchScalarGridSpec(
            num_scalar_prefetch=scalars,
            grid=(count, length // block),
            in_specs=[
                own
                if a.shape[0] != seqs
                else far
                if moves and (not back or i in moved)
                else near
                for i, a in enumerate(arrays)
            ]
            + [pl.BlockSpec(w.shape, lambda s, r, *_: (0, 0)) for w in whole]
            + [pl.BlockSpec(memory_space=pl.ANY)] * len(earlier),
            out_specs=[far if moves and back else near] * len(outputs) + [total] * sums,
        ),
        out_shape=out_shape,
        input_output_aliases={given + i: i for i in range(len(earlier))},
        compiler_params=pltpu.CompilerParams(vmem_limit_bytes=vmem_bytes),
        cost_estimate=pl.CostEstimate(
            flops=8 * count * length * width,
            bytes_accessed=moved_bytes(*arrays, *out_shape) * count // seqs,
            transcendentals=0,
        ),
    )(*(order if moves else ()), *arrays, *whole, *earlier)


def in_halves(kernel, arrays, summed, whole, outputs, sums, order=None, back=False):
    ready = by_rows(
        kernel, [arrays[0], summed[0], *arrays[1:]], whole, outputs, sums, order, back, (), 0
    )
    count = len(outputs)
    done = by_rows(
        kernel,
        [arrays[0], summed[1], *arrays[1:]],
        whole,
        outputs,
        sums,
        order,
        back,
        (),
        1,
        tuple(ready[:count]),
    )
    return [*done[:count], *(a + b for a, b in zip(ready[count:], done[count:]))]


def enter_kernel(sequence, chunk, *refs):
    count = len(refs) // 2
    part = refs[0].shape[1] // chunk.shape[0]
    for k in range(chunk.shape[0]):
        at = pl.ds(pl.multiple_of(chunk[k] * part, part), part)
        for i in range(count):
            refs[count + i][:, k * part : (k + 1) * part] = refs[i][:, at]


def norm_kernel(x, added, gain, middle, normed):
    total = x[...].astype(f32) + added[...].astype(f32)
    middle[...] = total
    inverse = lax.rsqrt(jnp.mean(total * total, axis=-1, keepdims=True) + eps)
    normed[...] = (total * inverse * gain[...]).astype(bf16)


def norm_back(values, grad, gain):
    inverse = lax.rsqrt(jnp.mean(values * values, axis=-1, keepdims=True) + eps)
    scaled = values * inverse
    weighted = grad * gain
    inner = jnp.mean(weighted * scaled, axis=-1, keepdims=True)
    return inverse * (weighted - scaled * inner), grad * scaled


def add_rows(total, values):
    @pl.when((pl.program_id(0) == 0) & (pl.program_id(1) == 0))
    def _():
        total[...] = jnp.zeros_like(total)

    rows, width = values.shape
    total[...] += jnp.sum(values.reshape(rows // pad_rows, pad_rows, width), axis=0)


def middle_back_kernel(middle, grad_normed, cot, gain, grad_middle, grad_low, total):
    grad, terms = norm_back(middle[...], grad_normed[...].astype(f32), gain[...])
    grad = grad + cot[...].astype(f32)
    grad_middle[...] = grad
    grad_low[...] = grad.astype(bf16)
    add_rows(total, terms)


def put_chunks(chunk, target, values):
    part = values.shape[1] // chunk.shape[0]
    for k in range(chunk.shape[0]):
        at = pl.ds(pl.multiple_of(chunk[k] * part, part), part)
        target[:, at] = values[:, k * part : (k + 1) * part]


def start_back_kernel(sequence, chunk, x, grad_normed, grad_middle, gain, grad_tokens):
    grad = norm_back(x[...].astype(f32), grad_normed[...].astype(f32), gain[...])[0]
    put_chunks(chunk, grad_tokens, grad + grad_middle[...])


def output_kernel(sequence, chunk, middle, added, output):
    put_chunks(chunk, output, (middle[...] + added[...].astype(f32)).astype(bf16))


def own_order(array, order, back=False):
    sequence, chunk = order
    if back:
        sequence, chunk = jnp.argsort(sequence), jnp.argsort(chunk)
    seqs, length, width = array.shape
    chunks = chunk.shape[0]
    split = array[sequence].reshape(seqs, length, chunks, width // chunks)
    return split[:, :, chunk].reshape(array.shape)


def carried(ends, way, n, between=lambda v: v):
    def shifted(values, by):
        pairs = [(i, i + way * by) for i in range(n) if 0 <= i + way * by < n]
        return lax.ppermute(values, "seq", pairs)

    ends = ends[:, :2]
    by = 1
    while 2 * by < n:
        earlier = shifted(ends, by)
        ends = ends[:, :1] * earlier + jnp.concatenate(
            [jnp.zeros_like(ends[:, 1:]), ends[:, 1:]], axis=1
        )
        by *= 2
        if by == 2:
            ends = between(ends)
    near, far = shifted(ends, 1), shifted(ends, 1 + by)
    state = near[:, :1] * far[:, 1:] + near[:, 1:]
    return jnp.pad(state, ((0, 0), (0, pad_rows - 1), (0, 0)))


def seq_sum(values, n):
    by = 1
    while by < n:
        values = values + lax.ppermute(values, "seq", [(i, i ^ by) for i in range(n)])
        by *= 2
    return values


def dense_heads(matrix):
    kinds, heads, width, _ = matrix.shape
    rows = [
        jnp.pad(matrix[:, h], ((0, 0), (0, 0), (h * width, (heads - 1 - h) * width)))
        for h in range(heads)
    ]
    return jnp.concatenate(rows, axis=1)


def across(a, b):
    return lax.dot_general(a, b, (((1,), (1,)), ((), ())), preferred_element_type=f32)


def down(a, b):
    return lax.dot_general(a, b, (((0,), (0,)), ((), ())), preferred_element_type=f32)


def dot(a, b):
    return jnp.dot(a, b, preferred_element_type=f32)


def shards(
    tokens,
    norm1_gain,
    in_weight,
    conv_weight,
    conv_bias,
    gate_matrix,
    gate_bias,
    decay_rate,
    out_weight,
    norm2_gain,
    mlp_weight,
    down_weight,
    cotangent,
):
    seqs, piece, width = tokens.shape
    rows = seqs * piece
    lanes = in_weight.shape[2]
    units = mlp_weight.shape[2]
    heads, head_width = gate_matrix.shape[1:3]
    taps = conv_weight.shape[0]
    n = lax.axis_size("seq")
    part = width // n
    order = ring_order(n)
    place = [order.index(i) for i in range(n)]
    me = jnp.asarray(place, jnp.int32)[lax.axis_index("seq")]
    chunk = jnp.asarray(order, jnp.int32)[(me - jnp.arange(n, dtype=jnp.int32)) % n]
    odd = lax.axis_index("tp") % 2
    sequence = (jnp.arange(seqs, dtype=jnp.int32) + odd * (seqs // 2)) % seqs
    move = (sequence, chunk)
    ring = Ring(order, lane_depth)
    tiled = part % 128 == 0

    def sl(a, k):
        return a[:, k * part : (k + 1) * part]

    move = (sequence, chunk)
    w_in = jnp.transpose(in_weight, (1, 2, 0))
    half_lanes = lanes // 2
    own_gain = jnp.pad(jnp.stack([norm1_gain, norm2_gain]), ((0, 14), (0, 0)))
    first = Gather(jnp.concatenate([w_in[0], out_weight[:half_lanes]], axis=0), 1, n, chunk)
    second = Gather(
        jnp.concatenate([w_in[1], out_weight[half_lanes:], own_gain], axis=0), -1, n, chunk
    )
    mlp = [Gather(mlp_weight[:, 0], 1, n, chunk), Gather(mlp_weight[:, 1], -1, n, chunk)]
    downs = Gather(down_weight, 1, n, chunk)
    ring.add([first, second])
    ring.add([*mlp, downs], [0, 0, 2])
    ring.issue()

    tokens, cotangent = ring.land((tokens, cotangent))
    if tiled:
        x, cot = by_rows(enter_kernel, [tokens, cotangent], [], [bf16, bf16], 0, move)
    else:
        x, cot = own_order(tokens, move), own_order(cotangent, move)
    full = x.shape
    part_full = (seqs // 2, piece, width)
    x, cot = ring.land((x, cot))
    grad_low = cot.reshape(rows, width)
    start = x.reshape(rows, width).astype(f32)
    inverse1 = lax.rsqrt(jnp.mean(start * start, axis=-1, keepdims=True) + eps)
    for _ in range(n - 3):
        ring.land()
    first, second = first.slots(), second.slots()
    in0 = [p[:lanes] for p in first]
    in1 = [p[:lanes] for p in second]
    gains = [p[lanes + half_lanes : lanes + half_lanes + 2] for p in second]
    gain1, gain2 = (
        jnp.concatenate([g[i : i + 1] for g in gains], axis=1).astype(f32) for i in range(2)
    )
    normed1 = [
        (sl(start, k) * inverse1 * gains[k][:1].astype(f32)).astype(bf16) for k in range(n)
    ]
    inner = sum(across(normed1[k], in0[k]) for k in range(n)).astype(bf16)
    gate_in = sum(across(normed1[k], in1[k]) for k in range(n)).astype(bf16)
    inner = ring.land(inner)
    inner = inner.reshape(seqs, piece, lanes)
    gate_in = gate_in.reshape(seqs, piece, lanes)
    before = lax.ppermute(
        inner[:, piece - taps + 1 :], "seq", [(i, i + 1) for i in range(n - 1)]
    ).astype(f32)
    before = ring.land(jnp.pad(before, ((0, 0), (pad_rows - taps + 1, 0), (0, 0))))
    conv_w = conv_weight.astype(f32)
    rate = decay_rate.astype(f32)[None]
    gate_m = dense_heads(gate_matrix)
    wide = (seqs, piece, lanes)
    edge = (seqs, pad_rows, lanes)
    gate_flops = 4 * rows * lanes * lanes
    mixed, recur, admit, decay, root, cum, local, ends = per_sequence(
        forward_kernel,
        seqs,
        [
            (inner, "seq"),
            (before, "seq"),
            (conv_w, "whole"),
            (conv_bias.astype(f32)[None], "whole"),
            (gate_m, "whole"),
            (gate_bias.astype(f32), "whole"),
            (rate, "whole"),
        ],
        [(wide, f32, "seq")] * 7 + [(edge, f32, "seq")],
        [pltpu.VMEM((piece + pad_rows, lanes), f32), pltpu.VMEM((2, piece, lanes), f32)],
        gate_flops,
    )
    entry = ring.land(carried(ring.land(ends), 1, n, ring.land))
    states = local + cum * entry[:, :1]
    product = (states * gelu_parts(gate_in.astype(f32))[0]).astype(bf16).reshape(rows, lanes)
    w_out = jnp.concatenate(
        [
            jnp.concatenate([p[lanes : lanes + half_lanes] for p in pieces], axis=1)
            for pieces in (first, second)
        ],
        axis=0,
    )
    block = rows // 2

    def half_of(a, h):
        return a[h * block : (h + 1) * block]

    def lands(values, count):
        for _ in range(count):
            ring.land()
        return ring.resume(values)

    chips = []

    def keep(chip):
        chips.append(ring.land(chip))
        return chips[0]

    recurrent = tp_sum(
        lambda h: dot(half_of(product, h), w_out),
        chips=keep,
        totals=lambda v: lands(v, 3),
    )
    gate_act, gate_slope = gelu_parts(after(gate_in, chips[0]).astype(f32))

    middle, normed2 = in_halves(
        norm_kernel, [x], [r.reshape(part_full) for r in recurrent], [gain2], [f32, bf16], 0
    )
    normed2 = ring.land(normed2.reshape(rows, width))
    w_mlp = jnp.concatenate([jnp.concatenate(w.slots(), axis=0) for w in mlp], axis=1)
    both = dot(normed2, w_mlp).astype(bf16)
    both0, both1 = both[:, :units].astype(f32), both[:, units:].astype(f32)
    act, slope = gelu_parts(both0)
    hidden = (act * both1).astype(bf16)
    hidden, act, slope = ring.land((hidden, act.astype(bf16), (slope * both1).astype(bf16)))
    ring.drain()
    w_down = jnp.concatenate(downs.slots(), axis=1)
    ring.token = None
    grad_both = []
    grad_down = Scatter(lambda k: down(hidden, sl(grad_low, k)), 1, n, chunk)
    grad_mlp = [
        Scatter(lambda k: down(sl(normed2, k), grad_both[0][:, :units]), -1, n, chunk),
        Scatter(lambda k: down(sl(normed2, k), grad_both[0][:, units:]), 1, n, chunk),
    ]
    ring.add([grad_down, *grad_mlp])
    ring.issue(1)
    act, slope, w_down = ring.hold((act, slope, w_down))
    grad_both.append(
        pl.pallas_call(
            hidden_back_kernel,
            grid=(seqs,),
            in_specs=[
                pl.BlockSpec((piece, width), lambda s: (s, 0)),
                pl.BlockSpec((units, width), lambda s: (0, 0)),
                pl.BlockSpec((piece, units), lambda s: (s, 0)),
                pl.BlockSpec((piece, units), lambda s: (s, 0)),
            ],
            out_specs=pl.BlockSpec((piece, 2 * units), lambda s: (s, 0)),
            out_shape=jax.ShapeDtypeStruct((rows, 2 * units), bf16),
            compiler_params=pltpu.CompilerParams(vmem_limit_bytes=vmem_bytes),
            cost_estimate=pl.CostEstimate(
                flops=2 * rows * width * units,
                bytes_accessed=moved_bytes(grad_low, w_down, act, slope, both),
                transcendentals=0,
            ),
        )(grad_low, w_down, act, slope)
    )
    ring.issue()
    grad_normed2 = tp_sum(
        lambda h: across(half_of(grad_both[0], h), w_mlp),
        others=ring.land,
        chips=ring.land,
        totals=lambda v: lands(v, 3),
    )
    turned = jnp.concatenate([half_of(hidden, 1), half_of(hidden, 0)], axis=0)
    turned = jnp.where(odd == 1, turned, hidden)
    mlp_out = lax.psum(dot(after(turned, grad_normed2[0]), w_down).astype(bf16), "tp")

    grad_middle, grad_rec, sum_gain2 = in_halves(
        middle_back_kernel,
        [middle, cot],
        [g.reshape(part_full) for g in grad_normed2],
        [gain2],
        [f32, bf16],
        1,
    )
    grad_rec = ring.land(grad_rec.reshape(rows, width))

    grad_product = across(grad_rec, w_out).reshape(wide)
    tail, local_grad, early = per_sequence(
        reverse_kernel,
        seqs,
        [(grad_product, "seq"), (gate_act, "seq"), (decay, "seq")],
        [(wide, f32, "seq")] * 2 + [(edge, f32, "seq")],
        [pltpu.VMEM((piece, lanes), f32)],
        rows * lanes * 50,
    )
    incoming = ring.land(carried(ring.land(early), -1, n, ring.land))
    grad_gates, grad_inner, grad_gate_in, head, last, sums = per_sequence(
        gates_back_kernel,
        seqs,
        [
            (grad_product, "seq"),
            (gate_slope, "seq"),
            (tail, "seq"),
            (local_grad, "seq"),
            (incoming, "seq"),
            (states, "seq"),
            (entry, "seq"),
            (recur, "seq"),
            (admit, "seq"),
            (decay, "seq"),
            (root, "seq"),
            (mixed, "seq"),
            (inner, "seq"),
            (before, "seq"),
            (gate_m, "whole"),
            (rate, "whole"),
            (conv_w, "whole"),
        ],
        [
            ((2,) + wide, bf16, "pair"),
            (wide, bf16, "seq"),
            (wide, bf16, "seq"),
            (edge, f32, "seq"),
            (edge, f32, "seq"),
            ((pad_rows, lanes), f32, "whole"),
        ],
        [pltpu.VMEM((piece, lanes), f32)] + [pltpu.VMEM((piece + pad_rows, lanes), f32)] * 2,
        gate_flops,
    )
    head = ring.land(head)
    behind = lax.ppermute(
        head[:, : taps - 1].astype(bf16), "seq", [(i + 1, i) for i in range(n - 1)]
    ).astype(f32)
    beyond = jnp.concatenate([jnp.zeros_like(last), behind], axis=1)
    beyond = jnp.pad(beyond, ((0, 0), (0, 1), (0, 0)))
    for lag in range(1, taps):
        last = last + conv_w[lag] * beyond[:, lag : lag + pad_rows]
    grad_inner = lax.dynamic_update_slice(
        grad_inner, last.astype(bf16), (0, piece - pad_rows, 0)
    )
    back0 = grad_inner.reshape(rows, lanes)
    back1 = grad_gate_in.reshape(rows, lanes)
    back = ring.land(jnp.concatenate([back0, back1], axis=1))
    w_both = jnp.concatenate([jnp.concatenate(in0, axis=1), jnp.concatenate(in1, axis=1)], axis=0)
    grads = [
        Scatter(lambda k: down(back0, normed1[k]), 1, n, chunk),
        Scatter(lambda k: down(back1, normed1[k]), -1, n, chunk),
        Scatter(lambda k: down(product, sl(grad_rec, k)), -1, n, chunk),
    ]
    ring.add(grads)
    ring.issue()
    late = []

    def hold_output(chip):
        late.append(after(mlp_out, chip))
        return ring.land(chip)

    grad_normed1 = tp_sum(
        lambda h: dot(half_of(back, h), w_both),
        chips=hold_output,
        totals=lambda v: lands(v, 4),
    )
    mlp_out = late[0]
    ring.drain()
    grads = [g.total() for g in grads]
    low_mixed = mixed.astype(bf16).reshape(rows, lanes)
    grad_matrix = []
    for k in range(2):
        dense = down(low_mixed, grad_gates[k].reshape(rows, lanes)).astype(bf16)
        for h in range(heads):
            at = slice(h * head_width, (h + 1) * head_width)
            grad_matrix.append(dense[at, at])
    packed = jnp.concatenate(
        grad_matrix + [sums.astype(bf16).reshape(-1, head_width)], axis=0
    )
    packed = lax.psum(packed, "seq")

    if tiled:
        output = by_rows(
            output_kernel,
            [middle, mlp_out.reshape(full)],
            [],
            [bf16],
            0,
            move,
            back=True,
            moved=(1,),
        )[0]
        grad_tokens = in_halves(
            start_back_kernel,
            [x, grad_middle],
            [g.reshape(part_full) for g in grad_normed1],
            [gain1],
            [f32],
            0,
            move,
            back=True,
        )[0]
    else:
        mlp_out = mlp_out.reshape(full)[sequence].astype(f32)
        output = own_order((middle + mlp_out).astype(bf16), move, True)
        grad_normed1_all = jnp.concatenate(grad_normed1, axis=0).reshape(full).astype(f32)
        grad_start = norm_back(x.astype(f32), grad_normed1_all, gain1)[0]
        grad_tokens = own_order(grad_middle + grad_start, move, True)
    mine = lax.axis_index("seq")
    slots = (me - jnp.asarray(place, jnp.int32)) % n
    scaled1 = start[:block] * inverse1[:block]
    sum_gain1 = jnp.sum(grad_normed1[0].astype(f32) * scaled1, axis=0)
    grad_gains = jnp.stack([sum_gain1, 0.5 * jnp.sum(sum_gain2, axis=0)])
    grad_gains = grad_gains + core_swap(grad_gains)
    grad_gains = seq_sum(grad_gains.reshape(2, n, part)[:, slots], n)
    grad_gains = lax.dynamic_index_in_dim(grad_gains, mine, 1, keepdims=False)

    packed, grad_gains = lax.optimization_barrier((packed, grad_gains))
    packed = packed.astype(f32)
    matrix_rows = 2 * heads * head_width
    grad_matrix = packed[:matrix_rows].reshape(gate_matrix.shape)
    small = packed[matrix_rows:].reshape(4 + taps, lanes)
    return (
        output,
        grad_tokens,
        grad_gains[0],
        jnp.transpose(jnp.stack(grads[:2]), (2, 0, 1)),
        small[4:],
        small[3],
        grad_matrix,
        small[1:3],
        small[0],
        grads[2],
        grad_gains[1],
        jnp.stack([g.total() for g in grad_mlp], axis=1),
        grad_down.total(),
    )


def solution(mesh):
    in_specs = (
        P(None, "seq", None),
        P("seq"),
        P("seq", None, "tp"),
        P(None, "tp"),
        P("tp"),
        P(None, "tp", None, None),
        P(None, "tp"),
        P("tp"),
        P("tp", "seq"),
        P("seq"),
        P("seq", None, "tp"),
        P("tp", "seq"),
        P(None, "seq", None),
    )
    out_specs = (
        P(None, "seq", None),
        P(None, "seq", None),
        P("seq"),
        P("seq", None, "tp"),
        P(None, "tp"),
        P("tp"),
        P(None, "tp", None, None),
        P(None, "tp"),
        P("tp"),
        P("tp", "seq"),
        P("seq"),
        P("seq", None, "tp"),
        P("tp", "seq"),
    )
    return jax.shard_map(shards, mesh=mesh, in_specs=in_specs, out_specs=out_specs, check_vma=False)
```

```python
import functools
import math

import jax
import jax.numpy as jnp
from jax import lax
from jax.experimental import pallas as pl
from jax.experimental.pallas import tpu as pltpu
from jax.sharding import PartitionSpec as P

f32 = jnp.float32
bf16 = jnp.bfloat16
eps = 1e-06
gelu_scale = math.sqrt(2.0 / math.pi)
step_rows = 16
pad_rows = 8
vmem_bytes = 48 * 2**20
ring_most = 8
lane_depth = 2
norm_rows = 128


def ring_order(n):
    return [*range(0, n, 2), *range(n - 1 - n % 2, 0, -2)]


def after(values, *earlier):
    return lax.optimization_barrier((values, *earlier))[0]


class Ring:
    def __init__(self, order, depth):
        n = len(order)
        self.n = n
        self.depth = depth
        self.pairs = {w: [(order[i], order[(i + w) % n]) for i in range(n)] for w in (1, -1)}
        self.queue = {1: [], -1: []}
        self.flying = {1: [], -1: []}
        self.landed = {1: [], -1: []}
        self.sent = {1: 0, -1: 0}
        self.last = {1: None, -1: None}
        self.token = None

    def add(self, weights, delays=None):
        half = self.n // 2
        delays = delays or [0] * len(weights)
        left = {id(flow): flow.count for w in weights for flow in w.flows.values()}
        for turn in range(half + max(delays)):
            for late in (True, False):
                for weight, delay in zip(weights, delays):
                    if (delay > 0) != late or turn < delay:
                        continue
                    for way, flow in weight.flows.items():
                        if left[id(flow)]:
                            left[id(flow)] -= 1
                            self.queue[way].append(flow)

    def issue(self, most=None):
        for way in (1, -1):
            queue, flying, landed = self.queue[way], self.flying[way], self.landed[way]
            while queue and len(flying) < (most or self.depth) and not queue[0].busy:
                flow = queue.pop(0)
                message = flow.message()
                gate = self.sent[way] - self.depth
                if gate >= 0:
                    message = after(message, landed[gate])
                if self.token is not None:
                    message = after(message, self.token)
                flow.busy = True
                self.sent[way] += 1
                self.last[way] = message
                flying.append((flow, lax.ppermute(message, "seq", self.pairs[way])))

    def hold(self, values):
        last = [message for message in self.last.values() if message is not None]
        return after(values, *last) if last else values

    def resume(self, token):
        self.token = token
        self.issue()
        return token

    def quiet(self, values):
        waiting = {w: self.queue[w] for w in (1, -1)}
        self.queue = {1: [], -1: []}
        for _ in range(self.depth):
            values = self.land(values)
        self.queue = waiting
        return values

    def land(self, values=None, count=1):
        for turn in range(count):
            taken = [(w, *self.flying[w].pop(0)) for w in (1, -1) if self.flying[w]]
            arrived = [message for _, _, message in taken]
            if values is not None and taken and turn == count - 1:
                values, *arrived = lax.optimization_barrier((values, *arrived))
            for (way, flow, _), message in zip(taken, arrived):
                flow.arrive(message)
                flow.busy = False
                self.landed[way].append(message)
            self.issue()
        return values

    def drain(self):
        while self.queue[1] or self.queue[-1] or self.flying[1] or self.flying[-1]:
            self.land()


class Pieces:
    def __init__(self, own, count):
        self.value, self.count, self.busy, self.got = own, count, False, []

    def message(self):
        return self.value

    def arrive(self, message):
        self.value = message
        self.got.append(message)


class Totals:
    def __init__(self, part, slots):
        self.part, self.slots, self.count, self.busy = part, slots, len(slots), False
        self.got, self.at = None, 0

    def message(self):
        total = self.part(self.slots[self.at])
        if self.got is not None:
            total = total + self.got.astype(f32)
        self.at += 1
        return total.astype(bf16)

    def arrive(self, message):
        self.got = message


class Gather:
    def __init__(self, piece, far, n, chunk):
        half = n // 2
        self.piece, self.n, self.chunk, self.flows = piece, n, chunk, {}
        if n <= ring_most:
            self.flows = {w: Pieces(piece, half if w == far else half - 1) for w in (1, -1)}

    def slots(self):
        if not self.flows:
            pieces = lax.all_gather(self.piece, "seq")[self.chunk]
            return [pieces[k] for k in range(self.n)]
        return [self.piece, *self.flows[1].got, *self.flows[-1].got[::-1]]


class Scatter:
    def __init__(self, part, far, n, chunk):
        half = n // 2
        self.part, self.n, self.chunk, self.flows = part, n, chunk, {}
        if n <= ring_most:
            self.flows = {
                1: Totals(part, list(range(half if far == 1 else half + 1, n))),
                -1: Totals(part, list(range(half if far == -1 else half - 1, 0, -1))),
            }

    def total(self):
        if not self.flows:
            parts = jnp.stack([self.part(k).astype(bf16) for k in range(self.n)])
            parts = parts[jnp.argsort(self.chunk)]
            return lax.psum_scatter(parts, "seq", scatter_dimension=0).astype(f32)
        total = self.part(0)
        for flow in self.flows.values():
            if flow.got is not None:
                total = total + flow.got.astype(f32)
        return total


def core_swap(values):
    size = lax.axis_size("tp")
    return lax.ppermute(values, "tp", [(i, i ^ 1) for i in range(size)])


def chip_swap(values):
    size = lax.axis_size("tp")
    return lax.ppermute(values, "tp", [(i, i ^ 2) for i in range(size)])


def tp_sum(part, others=lambda v: v, chips=lambda v: v, totals=lambda v: v):
    got = core_swap(others(part(1).astype(bf16)))
    own = lax.optimization_barrier(part(0).astype(bf16))
    chip = chips((own.astype(f32) + got.astype(f32)).astype(bf16))
    far = chip_swap(chip)
    total = totals((chip.astype(f32) + far.astype(f32)).astype(bf16))
    return total, core_swap(total)


def gelu_parts(x):
    t = jnp.tanh(gelu_scale * (x + 0.044715 * x * x * x))
    value = 0.5 * x * (1.0 + t)
    slope = 0.5 * (1.0 + t) + 0.5 * x * (1.0 - t * t) * gelu_scale * (1.0 + 3 * 0.044715 * x * x)
    return value, slope


def drive_square(log_decay, decay):
    y = -2.0 * log_decay
    series = 1.0 - y * (1.0 / 9.0)
    for k in range(8, 1, -1):
        series = 1.0 - y * (1.0 / k) * series
    return jnp.where(y < 0.5, y * series, 1.0 - decay * decay)


def scan_block(a, b, rows, reverse):
    count = a.shape[0]
    by = 1
    while by < count:
        turn = count - by if reverse else by
        pa = pltpu.roll(a, turn, 0)
        pb = pltpu.roll(b, turn, 0)
        inside = rows < count - by if reverse else rows >= by
        b = jnp.where(inside, a * pb + b, b)
        a = jnp.where(inside, a * pa, a)
        by *= 2
    return a, b


def forward_kernel(
    inner, before, conv_w, conv_b, gate_m, gate_b, rate,
    mixed, recur, admit, decay, root, cum, local, ends, ext, gates,
):
    length, lanes = inner.shape
    ext[:pad_rows] = before[...]
    ext[pad_rows:] = inner[...].astype(f32)
    taps = conv_w.shape[0]
    total = jnp.broadcast_to(conv_b[...], (length, lanes))
    for lag in range(taps):
        total = total + conv_w[lag : lag + 1] * ext[pad_rows - lag : pad_rows - lag + length]
    mixed[...] = total
    low = total.astype(bf16)
    for k in range(2):
        gates[k] = jnp.dot(low, gate_m[k], preferred_element_type=f32) + gate_b[k : k + 1]
    rows = lax.broadcasted_iota(jnp.int32, (step_rows, lanes), 0)

    def step(i, carry):
        at = pl.ds(pl.multiple_of(i * step_rows, step_rows), step_rows)
        r = jax.nn.sigmoid(gates[0, at])
        g = jax.nn.sigmoid(gates[1, at])
        log_decay = -8.0 * r * rate[...]
        d = jnp.exp(log_decay)
        m = jnp.sqrt(drive_square(log_decay, d))
        drive = m * g * mixed[at]
        root[at] = m
        recur[at] = r
        admit[at] = g
        decay[at] = d
        a, b = scan_block(d, drive, rows, False)
        b = b + a * carry[1]
        a = a * carry[0]
        cum[at] = a
        local[at] = b
        return a[step_rows - 1 :], b[step_rows - 1 :]

    a, b = lax.fori_loop(
        0, length // step_rows, step, (jnp.ones((1, lanes), f32), jnp.zeros((1, lanes), f32))
    )
    ends[0:1] = a
    ends[1:2] = b
    ends[2:] = jnp.zeros((pad_rows - 2, lanes), f32)


def reverse_kernel(grad_product, act, decay, tail, grad, first, nexts):
    length, lanes = act.shape
    nexts[...] = pltpu.roll(decay[...], length - 1, 0)
    nexts[length - 1 :] = jnp.ones((1, lanes), f32)
    rows = lax.broadcasted_iota(jnp.int32, (step_rows, lanes), 0)
    steps = length // step_rows

    def step(i, carry):
        at = pl.ds(pl.multiple_of((steps - 1 - i) * step_rows, step_rows), step_rows)
        direct = grad_product[at] * act[at]
        a, b = scan_block(nexts[at], direct, rows, True)
        b = b + a * carry[1]
        a = a * carry[0]
        tail[at] = a
        grad[at] = b
        return a[:1], b[:1]

    a, b = lax.fori_loop(0, steps, step, (jnp.ones((1, lanes), f32), jnp.zeros((1, lanes), f32)))
    first[0:1] = decay[0:1] * a
    first[1:2] = decay[0:1] * b
    first[2:] = jnp.zeros((pad_rows - 2, lanes), f32)


def gates_back_kernel(
    grad_product, slope, tail, grad, incoming, states, entry, recur, admit, decay, root, mixed, inner, before,
    gate_m, rate, conv_w, grad_gates, grad_inner, grad_gate_in, head, last, sums, grad_mix, grad_ext, ext,
):
    length, lanes = inner.shape
    enter = entry[0:1]
    later = incoming[0:1]
    taps = conv_w.shape[0]

    def step(i, carry):
        at = pl.ds(pl.multiple_of(i * step_rows, step_rows), step_rows)
        state = states[at]
        rows = lax.broadcasted_iota(jnp.int32, (step_rows, lanes), 0)
        earlier = jnp.where(rows == 0, carry[3], pltpu.roll(state, 1, 0))
        grad_gate_in[at] = (slope[at] * (grad_product[at] * state)).astype(bf16)
        total = grad[at] + tail[at] * later
        r, g, d, m, mix = recur[at], admit[at], decay[at], root[at], mixed[at]
        grad_mix[at] = total * m * g
        both = total * mix
        gate1 = both * m * g * (1.0 - g)
        grad_log = total * earlier * d - both * g * d * d / m
        gate0 = -8.0 * rate[...] * grad_log * r * (1.0 - r)
        low0 = gate0.astype(bf16)
        low1 = gate1.astype(bf16)
        grad_gates[0, at] = low0
        grad_gates[1, at] = low1
        return (
            carry[0] - 8.0 * (grad_log * r),
            carry[1] + low0.astype(f32),
            carry[2] + low1.astype(f32),
            state[step_rows - 1 :],
        )

    zero = jnp.zeros((step_rows, lanes), f32)
    totals = lax.fori_loop(0, length // step_rows, step, (zero, zero, zero, enter))
    back = grad_mix[...]
    for k in range(2):
        back = back + lax.dot_general(
            grad_gates[k], gate_m[k], (((1,), (1,)), ((), ())), preferred_element_type=f32
        )
    back = back.astype(bf16).astype(f32)
    head[...] = back[:pad_rows]
    grad_ext[:length] = back
    grad_ext[length:] = jnp.zeros((pad_rows, lanes), f32)
    ext[:pad_rows] = before[...]
    ext[pad_rows:] = inner[...].astype(f32)

    @pl.when(pl.program_id(0) == 0)
    def _():
        sums[...] = jnp.zeros_like(sums)

    for k in range(3):
        sums[k : k + 1] += jnp.sum(totals[k], axis=0, keepdims=True)
    sums[3:4] += jnp.sum(back, axis=0, keepdims=True)
    total = jnp.zeros((length, lanes), f32)
    for lag in range(taps):
        total = total + conv_w[lag : lag + 1] * grad_ext[lag : lag + length]
        term = back * ext[pad_rows - lag : pad_rows - lag + length]
        sums[4 + lag : 5 + lag] += jnp.sum(term, axis=0, keepdims=True)
    grad_inner[...] = total.astype(bf16)
    last[...] = total[length - pad_rows :]


def hidden_back_kernel(cot, w_down, act, slope, grad_both):
    units = w_down.shape[0]
    cut = math.gcd(units, 512)
    for j in range(0, units, cut):
        grad = lax.dot_general(
            cot[...], w_down[j : j + cut], (((1,), (1,)), ((), ())), preferred_element_type=f32
        )
        grad_both[:, j : j + cut] = (grad * slope[:, j : j + cut].astype(f32)).astype(bf16)
        grad_both[:, units + j : units + j + cut] = (
            grad * act[:, j : j + cut].astype(f32)
        ).astype(bf16)


def per_sequence(kernel, seqs, inputs, outputs, scratch, flops):
    def spec(shape, kind):
        if kind == "whole":
            return pl.BlockSpec(shape, lambda s: (0,) * len(shape))
        if kind == "pair":
            return pl.BlockSpec((shape[0], None) + shape[2:], lambda s: (0, s, 0, 0))
        return pl.BlockSpec((None,) + shape[1:], lambda s: (s,) + (0,) * (len(shape) - 1))

    moved = sum(a.size * a.dtype.itemsize for a, _ in inputs)
    moved += sum(math.prod(shape) * jnp.dtype(t).itemsize for shape, t, _ in outputs)
    return pl.pallas_call(
        kernel,
        grid=(seqs,),
        in_specs=[spec(a.shape, kind) for a, kind in inputs],
        out_specs=[spec(shape, kind) for shape, _, kind in outputs],
        out_shape=[jax.ShapeDtypeStruct(shape, t) for shape, t, _ in outputs],
        scratch_shapes=scratch,
        compiler_params=pltpu.CompilerParams(vmem_limit_bytes=vmem_bytes),
        cost_estimate=pl.CostEstimate(flops=flops, bytes_accessed=moved, transcendentals=0),
    )(*[a for a, _ in inputs])


def moved_bytes(*arrays):
    return sum(math.prod(a.shape) * jnp.dtype(a.dtype).itemsize for a in arrays)


def by_rows(
    kernel, arrays, whole, outputs, sums, order=None, back=False, moved=(), half=None, earlier=()
):
    seqs, length, width = arrays[0].shape
    block = min(norm_rows, length)
    count = seqs if half is None else seqs // 2
    skip = count * (half or 0)
    moves = order is not None
    tile = (None, block, width)
    near = pl.BlockSpec(tile, lambda s, r, *_: (s + skip, r, 0))
    own = pl.BlockSpec(tile, lambda s, r, *_: (s, r, 0))
    far = pl.BlockSpec(tile, lambda s, r, sequence, chunk: (sequence[s + skip], r, 0))
    total = pl.BlockSpec((pad_rows, width), lambda s, r, *_: (0, 0))
    out_shape = [jax.ShapeDtypeStruct((seqs, length, width), t) for t in outputs]
    out_shape += [jax.ShapeDtypeStruct((pad_rows, width), f32)] * sums
    scalars = 2 if moves else 0
    given = scalars + len(arrays) + len(whole)

    def body(*refs):
        kernel(*refs[:given], *refs[given + len(earlier) :])

    return pl.pallas_call(
        body,
        grid_spec=pltpu.PrefetchScalarGridSpec(
            num_scalar_prefetch=scalars,
            grid=(count, length // block),
            in_specs=[
                own
                if a.shape[0] != seqs
                else far
                if moves and (not back or i in moved)
                else near
                for i, a in enumerate(arrays)
            ]
            + [pl.BlockSpec(w.shape, lambda s, r, *_: (0, 0)) for w in whole]
            + [pl.BlockSpec(memory_space=pl.ANY)] * len(earlier),
            out_specs=[far if moves and back else near] * len(outputs) + [total] * sums,
        ),
        out_shape=out_shape,
        input_output_aliases={given + i: i for i in range(len(earlier))},
        compiler_params=pltpu.CompilerParams(vmem_limit_bytes=vmem_bytes),
        cost_estimate=pl.CostEstimate(
            flops=8 * count * length * width,
            bytes_accessed=moved_bytes(*arrays, *out_shape) * count // seqs,
            transcendentals=0,
        ),
    )(*(order if moves else ()), *arrays, *whole, *earlier)


def in_halves(kernel, arrays, summed, whole, outputs, sums, order=None, back=False):
    ready = by_rows(
        kernel, [arrays[0], summed[0], *arrays[1:]], whole, outputs, sums, order, back, (), 0
    )
    count = len(outputs)
    done = by_rows(
        kernel,
        [arrays[0], summed[1], *arrays[1:]],
        whole,
        outputs,
        sums,
        order,
        back,
        (),
        1,
        tuple(ready[:count]),
    )
    return [*done[:count], *(a + b for a, b in zip(ready[count:], done[count:]))]


def enter_kernel(sequence, chunk, tokens, cotangent, x, cot, turned):
    part = x.shape[1] // chunk.shape[0]
    turned[...] = cotangent[...]
    for k in range(chunk.shape[0]):
        at = pl.ds(pl.multiple_of(chunk[k] * part, part), part)
        x[:, k * part : (k + 1) * part] = tokens[:, at]
        cot[:, k * part : (k + 1) * part] = cotangent[:, at]


def norm_kernel(x, added, gain, middle, normed):
    total = x[...].astype(f32) + added[...].astype(f32)
    middle[...] = total
    inverse = lax.rsqrt(jnp.mean(total * total, axis=-1, keepdims=True) + eps)
    normed[...] = (total * inverse * gain[...]).astype(bf16)


def norm_back(values, grad, gain):
    inverse = lax.rsqrt(jnp.mean(values * values, axis=-1, keepdims=True) + eps)
    scaled = values * inverse
    weighted = grad * gain
    inner = jnp.mean(weighted * scaled, axis=-1, keepdims=True)
    return inverse * (weighted - scaled * inner), grad * scaled


def add_rows(total, values):
    @pl.when((pl.program_id(0) == 0) & (pl.program_id(1) == 0))
    def _():
        total[...] = jnp.zeros_like(total)

    rows, width = values.shape
    total[...] += jnp.sum(values.reshape(rows // pad_rows, pad_rows, width), axis=0)


def middle_back_kernel(middle, grad_normed, cot, gain, grad_middle, grad_low, total):
    grad, terms = norm_back(middle[...], grad_normed[...].astype(f32), gain[...])
    grad = grad + cot[...].astype(f32)
    grad_middle[...] = grad
    grad_low[...] = grad.astype(bf16)
    add_rows(total, terms)


def put_chunks(chunk, target, values):
    part = values.shape[1] // chunk.shape[0]
    for k in range(chunk.shape[0]):
        at = pl.ds(pl.multiple_of(chunk[k] * part, part), part)
        target[:, at] = values[:, k * part : (k + 1) * part]


def start_back_kernel(sequence, chunk, x, grad_normed, grad_middle, gain, grad_tokens):
    grad = norm_back(x[...].astype(f32), grad_normed[...].astype(f32), gain[...])[0]
    put_chunks(chunk, grad_tokens, grad + grad_middle[...])


def output_kernel(sequence, chunk, middle, added, output):
    part = middle.shape[1] // chunk.shape[0]
    for k in range(chunk.shape[0]):
        at = pl.ds(pl.multiple_of(chunk[k] * part, part), part)
        total = middle[:, k * part : (k + 1) * part] + added[:, at].astype(f32)
        output[:, at] = total.astype(bf16)


def own_order(array, order, back=False):
    sequence, chunk = order
    if back:
        sequence, chunk = jnp.argsort(sequence), jnp.argsort(chunk)
    seqs, length, width = array.shape
    chunks = chunk.shape[0]
    split = array[sequence].reshape(seqs, length, chunks, width // chunks)
    return split[:, :, chunk].reshape(array.shape)


def carried(ends, way, n, between=lambda v: v):
    def shifted(values, by):
        pairs = [(i, i + way * by) for i in range(n) if 0 <= i + way * by < n]
        return lax.ppermute(values, "seq", pairs)

    ends = ends[:, :2]
    by = 1
    while 2 * by < n:
        earlier = shifted(ends, by)
        ends = ends[:, :1] * earlier + jnp.concatenate(
            [jnp.zeros_like(ends[:, 1:]), ends[:, 1:]], axis=1
        )
        by *= 2
        if by == 2:
            ends = between(ends)
    near, far = shifted(ends, 1), shifted(ends, 1 + by)
    state = near[:, :1] * far[:, 1:] + near[:, 1:]
    return jnp.pad(state, ((0, 0), (0, pad_rows - 1), (0, 0)))


def seq_sum(values, n):
    by = 1
    while by < n:
        values = values + lax.ppermute(values, "seq", [(i, i ^ by) for i in range(n)])
        by *= 2
    return values


def dense_heads(matrix):
    kinds, heads, width, _ = matrix.shape
    rows = [
        jnp.pad(matrix[:, h], ((0, 0), (0, 0), (h * width, (heads - 1 - h) * width)))
        for h in range(heads)
    ]
    return jnp.concatenate(rows, axis=1)


def across(a, b):
    return lax.dot_general(a, b, (((1,), (1,)), ((), ())), preferred_element_type=f32)


def down(a, b):
    return lax.dot_general(a, b, (((0,), (0,)), ((), ())), preferred_element_type=f32)


def dot(a, b):
    return jnp.dot(a, b, preferred_element_type=f32)


def shards(
    tokens,
    norm1_gain,
    in_weight,
    conv_weight,
    conv_bias,
    gate_matrix,
    gate_bias,
    decay_rate,
    out_weight,
    norm2_gain,
    mlp_weight,
    down_weight,
    cotangent,
):
    seqs, piece, width = tokens.shape
    rows = seqs * piece
    lanes = in_weight.shape[2]
    units = mlp_weight.shape[2]
    heads, head_width = gate_matrix.shape[1:3]
    taps = conv_weight.shape[0]
    n = lax.axis_size("seq")
    part = width // n
    order = ring_order(n)
    place = [order.index(i) for i in range(n)]
    me = jnp.asarray(place, jnp.int32)[lax.axis_index("seq")]
    chunk = jnp.asarray(order, jnp.int32)[(me - jnp.arange(n, dtype=jnp.int32)) % n]
    odd = lax.axis_index("tp") % 2
    sequence = (jnp.arange(seqs, dtype=jnp.int32) + odd * (seqs // 2)) % seqs
    move = (sequence, chunk)
    ring = Ring(order, lane_depth)
    tiled = part % 128 == 0

    def sl(a, k):
        return a[:, k * part : (k + 1) * part]

    move = (sequence, chunk)
    w_in = jnp.transpose(in_weight, (1, 2, 0))
    half_lanes = lanes // 2
    own_gain = jnp.pad(jnp.stack([norm1_gain, norm2_gain]), ((0, 14), (0, 0)))
    first = Gather(jnp.concatenate([w_in[0], out_weight[:half_lanes]], axis=0), 1, n, chunk)
    second = Gather(
        jnp.concatenate([w_in[1], out_weight[half_lanes:], own_gain], axis=0), -1, n, chunk
    )
    mlp = [Gather(mlp_weight[:, 0], 1, n, chunk), Gather(mlp_weight[:, 1], -1, n, chunk)]
    ring.add([first, second])
    ring.add(mlp)
    ring.issue()

    tokens, cotangent = ring.land((tokens, cotangent))
    if tiled:
        x, cot, cot_turned = by_rows(enter_kernel, [tokens, cotangent], [], [bf16] * 3, 0, move)
    else:
        x, cot = own_order(tokens, move), own_order(cotangent, move)
        cot_turned = cotangent[sequence]
    full = x.shape
    part_full = (seqs // 2, piece, width)
    x, cot, cot_turned, down_weight, tail_rows = ring.land(
        (x, cot, cot_turned, down_weight, tokens[:, piece - taps + 1 :])
    )
    behind_rows = lax.ppermute(tail_rows, "seq", [(i, i + 1) for i in range(n - 1)])
    w_down = lax.all_gather(down_weight, "seq", axis=1, tiled=True)
    cot_turned = cot_turned.reshape(rows, width)
    start = x.reshape(rows, width).astype(f32)
    inverse1 = lax.rsqrt(jnp.mean(start * start, axis=-1, keepdims=True) + eps)
    for turn in range(n - 3):
        if turn == 3:
            behind_rows = ring.land(behind_rows)
        else:
            ring.land()
    first, second = first.slots(), second.slots()
    in0 = [p[:lanes] for p in first]
    in1 = [p[:lanes] for p in second]
    gains = [p[lanes + half_lanes : lanes + half_lanes + 2] for p in second]
    gain1, gain2 = (
        jnp.concatenate([g[i : i + 1] for g in gains], axis=1).astype(f32) for i in range(2)
    )
    normed1 = [
        (sl(start, k) * inverse1 * gains[k][:1].astype(f32)).astype(bf16) for k in range(n)
    ]
    inner = sum(across(normed1[k], in0[k]) for k in range(n)).astype(bf16)
    gate_in = sum(across(normed1[k], in1[k]) for k in range(n)).astype(bf16)
    count = seqs * (taps - 1)
    start_before = behind_rows[sequence].reshape(count, n, part)[:, chunk].reshape(count, width)
    start_before = jnp.pad(start_before.astype(f32), ((0, -count % 16), (0, 0)))
    inverse_before = lax.rsqrt(
        jnp.mean(start_before * start_before, axis=-1, keepdims=True) + eps
    )
    normed_before = [
        (sl(start_before, k) * inverse_before * gains[k][:1].astype(f32)).astype(bf16)
        for k in range(n)
    ]
    before = sum(across(normed_before[k], in0[k]) for k in range(n)).astype(bf16)
    before = before[:count].astype(f32).reshape(seqs, taps - 1, lanes)
    before = jnp.pad(before, ((0, 0), (pad_rows - taps + 1, 0), (0, 0)))
    inner = inner.reshape(seqs, piece, lanes)
    gate_in = gate_in.reshape(seqs, piece, lanes)
    inner = ring.land(inner)
    conv_w = conv_weight.astype(f32)
    rate = decay_rate.astype(f32)[None]
    gate_m = dense_heads(gate_matrix)
    wide = (seqs, piece, lanes)
    edge = (seqs, pad_rows, lanes)
    gate_flops = 4 * rows * lanes * lanes
    mixed, recur, admit, decay, root, cum, local, ends = per_sequence(
        forward_kernel,
        seqs,
        [
            (inner, "seq"),
            (before, "seq"),
            (conv_w, "whole"),
            (conv_bias.astype(f32)[None], "whole"),
            (gate_m, "whole"),
            (gate_bias.astype(f32), "whole"),
            (rate, "whole"),
        ],
        [(wide, f32, "seq")] * 7 + [(edge, f32, "seq")],
        [pltpu.VMEM((piece + pad_rows, lanes), f32), pltpu.VMEM((2, piece, lanes), f32)],
        gate_flops,
    )
    entry = ring.land(carried(ring.land(ends), 1, n))
    states = local + cum * entry[:, :1]
    product = (states * gelu_parts(gate_in.astype(f32))[0]).astype(bf16).reshape(rows, lanes)
    w_out = jnp.concatenate(
        [
            jnp.concatenate([p[lanes : lanes + half_lanes] for p in pieces], axis=1)
            for pieces in (first, second)
        ],
        axis=0,
    )
    block = rows // 2

    def half_of(a, h):
        return a[h * block : (h + 1) * block]

    def lands(values, count):
        for _ in range(count - 1):
            ring.land()
        return ring.land(values)

    chips = []

    def keep(chip):
        chips.append(chip)
        return chip

    recurrent = tp_sum(
        lambda h: dot(half_of(product, h), w_out),
        chips=keep,
        totals=lambda v: lands(v, 4),
    )
    gate_act, gate_slope = gelu_parts(after(gate_in, chips[0]).astype(f32))

    middle, normed2 = in_halves(
        norm_kernel, [x], [r.reshape(part_full) for r in recurrent], [gain2], [f32, bf16], 0
    )
    normed2 = normed2.reshape(rows, width)
    w_mlp = jnp.concatenate([jnp.concatenate(w.slots(), axis=0) for w in mlp], axis=1)
    both = dot(normed2, w_mlp).astype(bf16)
    both0, both1 = both[:, :units].astype(f32), both[:, units:].astype(f32)
    act, slope = gelu_parts(both0)
    hidden = (act * both1).astype(bf16)
    act, slope = act.astype(bf16), (slope * both1).astype(bf16)
    ring.drain()
    ring.token = None
    grad_down = down(hidden, cot_turned).astype(bf16)
    act, slope = after((act, slope), grad_down)
    grad_down = lax.psum_scatter(grad_down, "seq", scatter_dimension=1, tiled=True).astype(f32)
    grad_both = []
    grad_mlp = [
        Scatter(lambda k: down(sl(normed2, k), grad_both[0][:, :units]), 1, n, chunk),
        Scatter(lambda k: down(sl(normed2, k), grad_both[0][:, units:]), -1, n, chunk),
    ]
    ring.add(grad_mlp)
    grad_both.append(
        pl.pallas_call(
            hidden_back_kernel,
            grid=(seqs,),
            in_specs=[
                pl.BlockSpec((piece, width), lambda s: (s, 0)),
                pl.BlockSpec((units, width), lambda s: (0, 0)),
                pl.BlockSpec((piece, units), lambda s: (s, 0)),
                pl.BlockSpec((piece, units), lambda s: (s, 0)),
            ],
            out_specs=pl.BlockSpec((piece, 2 * units), lambda s: (s, 0)),
            out_shape=jax.ShapeDtypeStruct((rows, 2 * units), bf16),
            compiler_params=pltpu.CompilerParams(vmem_limit_bytes=vmem_bytes),
            cost_estimate=pl.CostEstimate(
                flops=2 * rows * width * units,
                bytes_accessed=moved_bytes(cot_turned, w_down, act, slope, both),
                transcendentals=0,
            ),
        )(cot_turned, w_down, act, slope)
    )
    ring.issue()
    grad_normed2 = tp_sum(
        lambda h: across(half_of(grad_both[0], h), w_mlp),
        totals=lambda v: lands(v, 2),
    )
    turned = jnp.concatenate([half_of(hidden, 1), half_of(hidden, 0)], axis=0)
    turned = jnp.where(odd == 1, turned, hidden)

    grad_middle, grad_rec, sum_gain2 = in_halves(
        middle_back_kernel,
        [middle, cot],
        [g.reshape(part_full) for g in grad_normed2],
        [gain2],
        [f32, bf16],
        1,
    )
    grad_out = Scatter(lambda k: down(product, sl(grad_rec, k)), -1, n, chunk)
    ring.add([grad_out])
    grad_rec = ring.land(grad_rec.reshape(rows, width))
    mlp_out = lax.psum(dot(after(turned, grad_middle), w_down).astype(bf16), "tp")

    grad_product = across(grad_rec, w_out).reshape(wide)
    tail, local_grad, early = per_sequence(
        reverse_kernel,
        seqs,
        [(grad_product, "seq"), (gate_act, "seq"), (decay, "seq")],
        [(wide, f32, "seq")] * 2 + [(edge, f32, "seq")],
        [pltpu.VMEM((piece, lanes), f32)],
        rows * lanes * 50,
    )
    incoming = ring.land(after(carried(early, -1, n), grad_down), 2)
    grad_gates, grad_inner, grad_gate_in, head, last, sums = per_sequence(
        gates_back_kernel,
        seqs,
        [
            (grad_product, "seq"),
            (gate_slope, "seq"),
            (tail, "seq"),
            (local_grad, "seq"),
            (incoming, "seq"),
            (states, "seq"),
            (entry, "seq"),
            (recur, "seq"),
            (admit, "seq"),
            (decay, "seq"),
            (root, "seq"),
            (mixed, "seq"),
            (inner, "seq"),
            (before, "seq"),
            (gate_m, "whole"),
            (rate, "whole"),
            (conv_w, "whole"),
        ],
        [
            ((2,) + wide, bf16, "pair"),
            (wide, bf16, "seq"),
            (wide, bf16, "seq"),
            (edge, f32, "seq"),
            (edge, f32, "seq"),
            ((pad_rows, lanes), f32, "whole"),
        ],
        [pltpu.VMEM((piece, lanes), f32)] + [pltpu.VMEM((piece + pad_rows, lanes), f32)] * 2,
        gate_flops,
    )
    head = ring.land(head)
    behind = lax.ppermute(
        head[:, : taps - 1].astype(bf16), "seq", [(i + 1, i) for i in range(n - 1)]
    ).astype(f32)
    beyond = jnp.concatenate([jnp.zeros_like(last), behind], axis=1)
    beyond = jnp.pad(beyond, ((0, 0), (0, 1), (0, 0)))
    for lag in range(1, taps):
        last = last + conv_w[lag] * beyond[:, lag : lag + pad_rows]
    grad_inner = lax.dynamic_update_slice(
        grad_inner, last.astype(bf16), (0, piece - pad_rows, 0)
    )
    back0 = grad_inner.reshape(rows, lanes)
    back1 = grad_gate_in.reshape(rows, lanes)
    back = ring.land(jnp.concatenate([back0, back1], axis=1))
    w_both = jnp.concatenate([jnp.concatenate(in0, axis=1), jnp.concatenate(in1, axis=1)], axis=0)
    grads = [
        Scatter(lambda k: down(back0, normed1[k]), 1, n, chunk),
        Scatter(lambda k: down(back1, normed1[k]), -1, n, chunk),
    ]
    ring.add(grads)
    ring.issue()
    late = []

    def hold_output(chip):
        late.append(after(mlp_out, chip))
        return ring.land(chip)

    grad_normed1 = tp_sum(
        lambda h: dot(half_of(back, h), w_both),
        chips=hold_output,
        totals=lambda v: lands(v, 4),
    )
    mlp_out = late[0]
    ready = None
    if tiled:
        summed1 = [g.reshape(part_full) for g in grad_normed1]
        ready = by_rows(
            start_back_kernel,
            [x, summed1[0], grad_middle],
            [gain1],
            [f32],
            0,
            move,
            back=True,
            half=0,
        )
        ring.resume(ready[0])
        total1 = after(grad_normed1[0], ready[0])
    else:
        total1 = grad_normed1[0]
    ring.drain()
    grads = [g.total() for g in grads]
    low_mixed = mixed.astype(bf16).reshape(rows, lanes)
    grad_matrix = []
    for k in range(2):
        dense = down(low_mixed, grad_gates[k].reshape(rows, lanes)).astype(bf16)
        for h in range(heads):
            at = slice(h * head_width, (h + 1) * head_width)
            grad_matrix.append(dense[at, at])
    packed = jnp.concatenate(
        grad_matrix + [sums.astype(bf16).reshape(-1, head_width)], axis=0
    )
    packed = lax.psum(packed, "seq")

    if tiled:
        output = by_rows(
            output_kernel,
            [middle, mlp_out.reshape(full)],
            [],
            [bf16],
            0,
            move,
            back=True,
            moved=(1,),
        )[0]
        grad_tokens = by_rows(
            start_back_kernel,
            [x, summed1[1], grad_middle],
            [gain1],
            [f32],
            0,
            move,
            back=True,
            half=1,
            earlier=ready,
        )[0]
    else:
        mlp_out = mlp_out.reshape(full).astype(f32)
        output = (own_order(middle, move, True) + mlp_out).astype(bf16)
        grad_normed1_all = jnp.concatenate(grad_normed1, axis=0).reshape(full).astype(f32)
        grad_start = norm_back(x.astype(f32), grad_normed1_all, gain1)[0]
        grad_tokens = own_order(grad_middle + grad_start, move, True)
    mine = lax.axis_index("seq")
    slots = (me - jnp.asarray(place, jnp.int32)) % n
    scaled1 = start[:block] * inverse1[:block]
    sum_gain1 = jnp.sum(total1.astype(f32) * scaled1, axis=0)
    grad_gains = jnp.stack([sum_gain1, 0.5 * jnp.sum(sum_gain2, axis=0)])
    grad_gains = grad_gains + core_swap(grad_gains)
    grad_gains = seq_sum(grad_gains.reshape(2, n, part)[:, slots], n)
    grad_gains = lax.dynamic_index_in_dim(grad_gains, mine, 1, keepdims=False)

    packed, grad_gains = lax.optimization_barrier((packed, grad_gains))
    packed = packed.astype(f32)
    matrix_rows = 2 * heads * head_width
    grad_matrix = packed[:matrix_rows].reshape(gate_matrix.shape)
    small = packed[matrix_rows:].reshape(4 + taps, lanes)
    return (
        output,
        grad_tokens,
        grad_gains[0],
        jnp.transpose(jnp.stack(grads[:2]), (2, 0, 1)),
        small[4:],
        small[3],
        grad_matrix,
        small[1:3],
        small[0],
        grad_out.total(),
        grad_gains[1],
        jnp.stack([g.total() for g in grad_mlp], axis=1),
        grad_down,
    )


def solution(mesh):
    in_specs = (
        P(None, "seq", None),
        P("seq"),
        P("seq", None, "tp"),
        P(None, "tp"),
        P("tp"),
        P(None, "tp", None, None),
        P(None, "tp"),
        P("tp"),
        P("tp", "seq"),
        P("seq"),
        P("seq", None, "tp"),
        P("tp", "seq"),
        P(None, "seq", None),
    )
    out_specs = (
        P(None, "seq", None),
        P(None, "seq", None),
        P("seq"),
        P("seq", None, "tp"),
        P(None, "tp"),
        P("tp"),
        P(None, "tp", None, None),
        P(None, "tp"),
        P("tp"),
        P("tp", "seq"),
        P("seq"),
        P("seq", None, "tp"),
        P("tp", "seq"),
    )
    return jax.shard_map(shards, mesh=mesh, in_specs=in_specs, out_specs=out_specs, check_vma=False)
```

```python
import functools
import math

import jax
import jax.numpy as jnp
from jax import lax
from jax.experimental import pallas as pl
from jax.experimental.pallas import tpu as pltpu
from jax.sharding import PartitionSpec as P

f32 = jnp.float32
bf16 = jnp.bfloat16
eps = 1e-06
gelu_scale = math.sqrt(2.0 / math.pi)
step_rows = 16
pad_rows = 8
vmem_bytes = 48 * 2**20
ring_most = 8
lane_depth = 2
landings = (3, 1, 1, 1, 1, 1, 0, 4, 1, 1, 1, 1, 0, 0, 2, 1, 1, 0, 1, 1, 1, 0, 0, 4)
norm_rows = 128


def ring_order(n):
    return [*range(0, n, 2), *range(n - 1 - n % 2, 0, -2)]


def after(values, *earlier):
    return lax.optimization_barrier((values, *earlier))[0]


class Ring:
    def __init__(self, order, depth):
        n = len(order)
        self.n = n
        self.depth = depth
        self.pairs = {w: [(order[i], order[(i + w) % n]) for i in range(n)] for w in (1, -1)}
        self.queue = {1: [], -1: []}
        self.flying = {1: [], -1: []}
        self.landed = {1: [], -1: []}
        self.sent = {1: 0, -1: 0}
        self.last = {1: None, -1: None}
        self.token = None

    def add(self, weights, delays=None):
        half = self.n // 2
        delays = delays or [0] * len(weights)
        left = {id(flow): flow.count for w in weights for flow in w.flows.values()}
        for turn in range(half + max(delays)):
            for late in (True, False):
                for weight, delay in zip(weights, delays):
                    if (delay > 0) != late or turn < delay:
                        continue
                    for way, flow in weight.flows.items():
                        if left[id(flow)]:
                            left[id(flow)] -= 1
                            self.queue[way].append(flow)

    def issue(self, most=None):
        for way in (1, -1):
            queue, flying, landed = self.queue[way], self.flying[way], self.landed[way]
            while queue and len(flying) < (most or self.depth) and not queue[0].busy:
                flow = queue.pop(0)
                message = flow.message()
                gate = self.sent[way] - self.depth
                if gate >= 0:
                    message = after(message, landed[gate])
                if self.token is not None:
                    message = after(message, self.token)
                flow.busy = True
                self.sent[way] += 1
                self.last[way] = message
                flying.append((flow, lax.ppermute(message, "seq", self.pairs[way])))

    def hold(self, values):
        last = [message for message in self.last.values() if message is not None]
        return after(values, *last) if last else values

    def resume(self, token):
        self.token = token
        self.issue()
        return token

    def quiet(self, values):
        waiting = {w: self.queue[w] for w in (1, -1)}
        self.queue = {1: [], -1: []}
        for _ in range(self.depth):
            values = self.land(values)
        self.queue = waiting
        return values

    def land(self, values=None, count=1):
        for turn in range(count):
            taken = [(w, *self.flying[w].pop(0)) for w in (1, -1) if self.flying[w]]
            arrived = [message for _, _, message in taken]
            if values is not None and taken and turn == count - 1:
                values, *arrived = lax.optimization_barrier((values, *arrived))
            for (way, flow, _), message in zip(taken, arrived):
                flow.arrive(message)
                flow.busy = False
                self.landed[way].append(message)
            self.issue()
        return values

    def need(self, weights):
        flows = [flow for w in weights for flow in w.flows.values()]
        while any(len(flow.got) < flow.count for flow in flows):
            self.land()

    def drain(self):
        while self.queue[1] or self.queue[-1] or self.flying[1] or self.flying[-1]:
            self.land()


class Pieces:
    def __init__(self, own, count):
        self.value, self.count, self.busy, self.got = own, count, False, []

    def message(self):
        return self.value

    def arrive(self, message):
        self.value = message
        self.got.append(message)


class Totals:
    def __init__(self, part, slots):
        self.part, self.slots, self.count, self.busy = part, slots, len(slots), False
        self.got, self.at = None, 0

    def message(self):
        total = self.part(self.slots[self.at])
        if self.got is not None:
            total = total + self.got.astype(f32)
        self.at += 1
        return total.astype(bf16)

    def arrive(self, message):
        self.got = message


class Gather:
    def __init__(self, piece, far, n, chunk):
        half = n // 2
        self.piece, self.n, self.chunk, self.flows = piece, n, chunk, {}
        if n <= ring_most:
            self.flows = {w: Pieces(piece, half if w == far else half - 1) for w in (1, -1)}

    def slots(self):
        if not self.flows:
            pieces = lax.all_gather(self.piece, "seq")[self.chunk]
            return [pieces[k] for k in range(self.n)]
        return [self.piece, *self.flows[1].got, *self.flows[-1].got[::-1]]


class Scatter:
    def __init__(self, part, far, n, chunk):
        half = n // 2
        self.part, self.n, self.chunk, self.flows = part, n, chunk, {}
        if n <= ring_most:
            self.flows = {
                1: Totals(part, list(range(half if far == 1 else half + 1, n))),
                -1: Totals(part, list(range(half if far == -1 else half - 1, 0, -1))),
            }

    def total(self):
        if not self.flows:
            parts = jnp.stack([self.part(k).astype(bf16) for k in range(self.n)])
            parts = parts[jnp.argsort(self.chunk)]
            return lax.psum_scatter(parts, "seq", scatter_dimension=0).astype(f32)
        total = self.part(0)
        for flow in self.flows.values():
            if flow.got is not None:
                total = total + flow.got.astype(f32)
        return total


def core_swap(values):
    size = lax.axis_size("tp")
    return lax.ppermute(values, "tp", [(i, i ^ 1) for i in range(size)])


def chip_swap(values):
    size = lax.axis_size("tp")
    return lax.ppermute(values, "tp", [(i, i ^ 2) for i in range(size)])


def tp_sum(part, others=lambda v: v, owns=lambda v: v, chips=lambda v: v, totals=lambda v: v):
    got = core_swap(others(part(1).astype(bf16)))
    own = owns(lax.optimization_barrier(part(0).astype(bf16)))
    chip = chips((own.astype(f32) + got.astype(f32)).astype(bf16))
    far = chip_swap(chip)
    total = totals((chip.astype(f32) + far.astype(f32)).astype(bf16))
    return total, core_swap(total)


def gelu_parts(x):
    t = jnp.tanh(gelu_scale * (x + 0.044715 * x * x * x))
    value = 0.5 * x * (1.0 + t)
    slope = 0.5 * (1.0 + t) + 0.5 * x * (1.0 - t * t) * gelu_scale * (1.0 + 3 * 0.044715 * x * x)
    return value, slope


def drive_square(log_decay, decay):
    y = -2.0 * log_decay
    series = 1.0 - y * (1.0 / 9.0)
    for k in range(8, 1, -1):
        series = 1.0 - y * (1.0 / k) * series
    return jnp.where(y < 0.5, y * series, 1.0 - decay * decay)


def scan_block(a, b, rows, reverse):
    count = a.shape[0]
    by = 1
    while by < count:
        turn = count - by if reverse else by
        pa = pltpu.roll(a, turn, 0)
        pb = pltpu.roll(b, turn, 0)
        inside = rows < count - by if reverse else rows >= by
        b = jnp.where(inside, a * pb + b, b)
        a = jnp.where(inside, a * pa, a)
        by *= 2
    return a, b


def forward_kernel(
    inner, before, conv_w, conv_b, gate_m, gate_b, rate,
    mixed, recur, admit, decay, root, cum, local, ends, ext, gates,
):
    length, lanes = inner.shape
    ext[:pad_rows] = before[...]
    ext[pad_rows:] = inner[...].astype(f32)
    taps = conv_w.shape[0]
    total = jnp.broadcast_to(conv_b[...], (length, lanes))
    for lag in range(taps):
        total = total + conv_w[lag : lag + 1] * ext[pad_rows - lag : pad_rows - lag + length]
    mixed[...] = total
    low = total.astype(bf16)
    for k in range(2):
        gates[k] = jnp.dot(low, gate_m[k], preferred_element_type=f32) + gate_b[k : k + 1]
    rows = lax.broadcasted_iota(jnp.int32, (step_rows, lanes), 0)

    def step(i, carry):
        at = pl.ds(pl.multiple_of(i * step_rows, step_rows), step_rows)
        r = jax.nn.sigmoid(gates[0, at])
        g = jax.nn.sigmoid(gates[1, at])
        log_decay = -8.0 * r * rate[...]
        d = jnp.exp(log_decay)
        m = jnp.sqrt(drive_square(log_decay, d))
        drive = m * g * mixed[at]
        root[at] = m
        recur[at] = r
        admit[at] = g
        decay[at] = d
        a, b = scan_block(d, drive, rows, False)
        b = b + a * carry[1]
        a = a * carry[0]
        cum[at] = a
        local[at] = b
        return a[step_rows - 1 :], b[step_rows - 1 :]

    a, b = lax.fori_loop(
        0, length // step_rows, step, (jnp.ones((1, lanes), f32), jnp.zeros((1, lanes), f32))
    )
    ends[0:1] = a
    ends[1:2] = b
    ends[2:] = jnp.zeros((pad_rows - 2, lanes), f32)


def reverse_kernel(grad_product, act, decay, tail, grad, first, nexts):
    length, lanes = act.shape
    nexts[...] = pltpu.roll(decay[...], length - 1, 0)
    nexts[length - 1 :] = jnp.ones((1, lanes), f32)
    rows = lax.broadcasted_iota(jnp.int32, (step_rows, lanes), 0)
    steps = length // step_rows

    def step(i, carry):
        at = pl.ds(pl.multiple_of((steps - 1 - i) * step_rows, step_rows), step_rows)
        direct = grad_product[at] * act[at]
        a, b = scan_block(nexts[at], direct, rows, True)
        b = b + a * carry[1]
        a = a * carry[0]
        tail[at] = a
        grad[at] = b
        return a[:1], b[:1]

    a, b = lax.fori_loop(0, steps, step, (jnp.ones((1, lanes), f32), jnp.zeros((1, lanes), f32)))
    first[0:1] = decay[0:1] * a
    first[1:2] = decay[0:1] * b
    first[2:] = jnp.zeros((pad_rows - 2, lanes), f32)


def gates_back_kernel(
    grad_product, slope, tail, grad, incoming, states, entry, recur, admit, decay, root, mixed, inner, before,
    gate_m, rate, conv_w, grad_gates, grad_inner, grad_gate_in, head, last, sums, grad_mix, grad_ext, ext,
):
    length, lanes = inner.shape
    enter = entry[0:1]
    later = incoming[0:1]
    taps = conv_w.shape[0]

    def step(i, carry):
        at = pl.ds(pl.multiple_of(i * step_rows, step_rows), step_rows)
        state = states[at]
        rows = lax.broadcasted_iota(jnp.int32, (step_rows, lanes), 0)
        earlier = jnp.where(rows == 0, carry[3], pltpu.roll(state, 1, 0))
        grad_gate_in[at] = (slope[at] * (grad_product[at] * state)).astype(bf16)
        total = grad[at] + tail[at] * later
        r, g, d, m, mix = recur[at], admit[at], decay[at], root[at], mixed[at]
        grad_mix[at] = total * m * g
        both = total * mix
        gate1 = both * m * g * (1.0 - g)
        grad_log = total * earlier * d - both * g * d * d / m
        gate0 = -8.0 * rate[...] * grad_log * r * (1.0 - r)
        low0 = gate0.astype(bf16)
        low1 = gate1.astype(bf16)
        grad_gates[0, at] = low0
        grad_gates[1, at] = low1
        return (
            carry[0] - 8.0 * (grad_log * r),
            carry[1] + low0.astype(f32),
            carry[2] + low1.astype(f32),
            state[step_rows - 1 :],
        )

    zero = jnp.zeros((step_rows, lanes), f32)
    totals = lax.fori_loop(0, length // step_rows, step, (zero, zero, zero, enter))
    back = grad_mix[...]
    for k in range(2):
        back = back + lax.dot_general(
            grad_gates[k], gate_m[k], (((1,), (1,)), ((), ())), preferred_element_type=f32
        )
    back = back.astype(bf16).astype(f32)
    head[...] = back[:pad_rows]
    grad_ext[:length] = back
    grad_ext[length:] = jnp.zeros((pad_rows, lanes), f32)
    ext[:pad_rows] = before[...]
    ext[pad_rows:] = inner[...].astype(f32)

    @pl.when(pl.program_id(0) == 0)
    def _():
        sums[...] = jnp.zeros_like(sums)

    for k in range(3):
        sums[k : k + 1] += jnp.sum(totals[k], axis=0, keepdims=True)
    sums[3:4] += jnp.sum(back, axis=0, keepdims=True)
    total = jnp.zeros((length, lanes), f32)
    for lag in range(taps):
        total = total + conv_w[lag : lag + 1] * grad_ext[lag : lag + length]
        term = back * ext[pad_rows - lag : pad_rows - lag + length]
        sums[4 + lag : 5 + lag] += jnp.sum(term, axis=0, keepdims=True)
    grad_inner[...] = total.astype(bf16)
    last[...] = total[length - pad_rows :]


def hidden_back_kernel(cot, w_down, act, slope, grad_both):
    units = w_down.shape[0]
    cut = math.gcd(units, 512)
    for j in range(0, units, cut):
        grad = lax.dot_general(
            cot[...], w_down[j : j + cut], (((1,), (1,)), ((), ())), preferred_element_type=f32
        )
        grad_both[:, j : j + cut] = (grad * slope[:, j : j + cut].astype(f32)).astype(bf16)
        grad_both[:, units + j : units + j + cut] = (
            grad * act[:, j : j + cut].astype(f32)
        ).astype(bf16)


def per_sequence(kernel, seqs, inputs, outputs, scratch, flops):
    def spec(shape, kind):
        if kind == "whole":
            return pl.BlockSpec(shape, lambda s: (0,) * len(shape))
        if kind == "pair":
            return pl.BlockSpec((shape[0], None) + shape[2:], lambda s: (0, s, 0, 0))
        return pl.BlockSpec((None,) + shape[1:], lambda s: (s,) + (0,) * (len(shape) - 1))

    moved = sum(a.size * a.dtype.itemsize for a, _ in inputs)
    moved += sum(math.prod(shape) * jnp.dtype(t).itemsize for shape, t, _ in outputs)
    return pl.pallas_call(
        kernel,
        grid=(seqs,),
        in_specs=[spec(a.shape, kind) for a, kind in inputs],
        out_specs=[spec(shape, kind) for shape, _, kind in outputs],
        out_shape=[jax.ShapeDtypeStruct(shape, t) for shape, t, _ in outputs],
        scratch_shapes=scratch,
        compiler_params=pltpu.CompilerParams(vmem_limit_bytes=vmem_bytes),
        cost_estimate=pl.CostEstimate(flops=flops, bytes_accessed=moved, transcendentals=0),
    )(*[a for a, _ in inputs])


def moved_bytes(*arrays):
    return sum(math.prod(a.shape) * jnp.dtype(a.dtype).itemsize for a in arrays)


def by_rows(
    kernel, arrays, whole, outputs, sums, order=None, back=False, moved=(), half=None, earlier=()
):
    seqs, length, width = arrays[0].shape
    block = min(norm_rows, length)
    count = seqs if half is None else seqs // 2
    skip = count * (half or 0)
    moves = order is not None
    tile = (None, block, width)
    near = pl.BlockSpec(tile, lambda s, r, *_: (s + skip, r, 0))
    own = pl.BlockSpec(tile, lambda s, r, *_: (s, r, 0))
    far = pl.BlockSpec(tile, lambda s, r, sequence, chunk: (sequence[s + skip], r, 0))
    total = pl.BlockSpec((pad_rows, width), lambda s, r, *_: (0, 0))
    out_shape = [jax.ShapeDtypeStruct((seqs, length, width), t) for t in outputs]
    out_shape += [jax.ShapeDtypeStruct((pad_rows, width), f32)] * sums
    scalars = 2 if moves else 0
    given = scalars + len(arrays) + len(whole)

    def body(*refs):
        kernel(*refs[:given], *refs[given + len(earlier) :])

    return pl.pallas_call(
        body,
        grid_spec=pltpu.PrefetchScalarGridSpec(
            num_scalar_prefetch=scalars,
            grid=(count, length // block),
            in_specs=[
                own
                if a.shape[0] != seqs
                else far
                if moves and (not back or i in moved)
                else near
                for i, a in enumerate(arrays)
            ]
            + [pl.BlockSpec(w.shape, lambda s, r, *_: (0, 0)) for w in whole]
            + [pl.BlockSpec(memory_space=pl.ANY)] * len(earlier),
            out_specs=[far if moves and back else near] * len(outputs) + [total] * sums,
        ),
        out_shape=out_shape,
        input_output_aliases={given + i: i for i in range(len(earlier))},
        compiler_params=pltpu.CompilerParams(vmem_limit_bytes=vmem_bytes),
        cost_estimate=pl.CostEstimate(
            flops=8 * count * length * width,
            bytes_accessed=moved_bytes(*arrays, *out_shape) * count // seqs,
            transcendentals=0,
        ),
    )(*(order if moves else ()), *arrays, *whole, *earlier)


def in_halves(kernel, arrays, summed, whole, outputs, sums, order=None, back=False):
    ready = by_rows(
        kernel, [arrays[0], summed[0], *arrays[1:]], whole, outputs, sums, order, back, (), 0
    )
    count = len(outputs)
    done = by_rows(
        kernel,
        [arrays[0], summed[1], *arrays[1:]],
        whole,
        outputs,
        sums,
        order,
        back,
        (),
        1,
        tuple(ready[:count]),
    )
    return [*done[:count], *(a + b for a, b in zip(ready[count:], done[count:]))]


def enter_kernel(sequence, chunk, tokens, cotangent, x, cot):
    part = x.shape[1] // chunk.shape[0]
    for k in range(chunk.shape[0]):
        at = pl.ds(pl.multiple_of(chunk[k] * part, part), part)
        x[:, k * part : (k + 1) * part] = tokens[:, at]
        cot[:, k * part : (k + 1) * part] = cotangent[:, at]


def norm_kernel(x, added, gain, middle, normed):
    total = x[...].astype(f32) + added[...].astype(f32)
    middle[...] = total
    inverse = lax.rsqrt(jnp.mean(total * total, axis=-1, keepdims=True) + eps)
    normed[...] = (total * inverse * gain[...]).astype(bf16)


def norm_back(values, grad, gain):
    inverse = lax.rsqrt(jnp.mean(values * values, axis=-1, keepdims=True) + eps)
    scaled = values * inverse
    weighted = grad * gain
    inner = jnp.mean(weighted * scaled, axis=-1, keepdims=True)
    return inverse * (weighted - scaled * inner), grad * scaled


def add_rows(total, values):
    @pl.when((pl.program_id(0) == 0) & (pl.program_id(1) == 0))
    def _():
        total[...] = jnp.zeros_like(total)

    rows, width = values.shape
    total[...] += jnp.sum(values.reshape(rows // pad_rows, pad_rows, width), axis=0)


def middle_back_kernel(middle, grad_normed, cot, gain, grad_middle, grad_low, total):
    grad, terms = norm_back(middle[...], grad_normed[...].astype(f32), gain[...])
    grad = grad + cot[...].astype(f32)
    grad_middle[...] = grad
    grad_low[...] = grad.astype(bf16)
    add_rows(total, terms)


def put_chunks(chunk, target, values):
    part = values.shape[1] // chunk.shape[0]
    for k in range(chunk.shape[0]):
        at = pl.ds(pl.multiple_of(chunk[k] * part, part), part)
        target[:, at] = values[:, k * part : (k + 1) * part]


def start_back_kernel(sequence, chunk, x, grad_normed, grad_middle, gain, grad_tokens):
    grad = norm_back(x[...].astype(f32), grad_normed[...].astype(f32), gain[...])[0]
    put_chunks(chunk, grad_tokens, grad + grad_middle[...])


def output_kernel(sequence, chunk, middle, added, output):
    part = middle.shape[1] // chunk.shape[0]
    for k in range(chunk.shape[0]):
        at = pl.ds(pl.multiple_of(chunk[k] * part, part), part)
        near = slice(k * part, (k + 1) * part)
        output[:, at] = (middle[:, near] + added[:, near].astype(f32)).astype(bf16)


def own_order(array, order, back=False):
    sequence, chunk = order
    if back:
        sequence, chunk = jnp.argsort(sequence), jnp.argsort(chunk)
    seqs, length, width = array.shape
    chunks = chunk.shape[0]
    split = array[sequence].reshape(seqs, length, chunks, width // chunks)
    return split[:, :, chunk].reshape(array.shape)


def carried(ends, way, n, between=lambda v: v):
    def shifted(values, by):
        pairs = [(i, i + way * by) for i in range(n) if 0 <= i + way * by < n]
        return lax.ppermute(values, "seq", pairs)

    ends = ends[:, :2]
    by = 1
    while 2 * by < n:
        earlier = shifted(ends, by)
        ends = ends[:, :1] * earlier + jnp.concatenate(
            [jnp.zeros_like(ends[:, 1:]), ends[:, 1:]], axis=1
        )
        by *= 2
        if by == 2:
            ends = between(ends)
    near, far = shifted(ends, 1), shifted(ends, 1 + by)
    state = near[:, :1] * far[:, 1:] + near[:, 1:]
    return jnp.pad(state, ((0, 0), (0, pad_rows - 1), (0, 0)))


def seq_sum(values, n):
    by = 1
    while by < n:
        values = values + lax.ppermute(values, "seq", [(i, i ^ by) for i in range(n)])
        by *= 2
    return values


def dense_heads(matrix):
    kinds, heads, width, _ = matrix.shape
    rows = [
        jnp.pad(matrix[:, h], ((0, 0), (0, 0), (h * width, (heads - 1 - h) * width)))
        for h in range(heads)
    ]
    return jnp.concatenate(rows, axis=1)


def across(a, b):
    return lax.dot_general(a, b, (((1,), (1,)), ((), ())), preferred_element_type=f32)


def down(a, b):
    return lax.dot_general(a, b, (((0,), (0,)), ((), ())), preferred_element_type=f32)


def dot(a, b):
    return jnp.dot(a, b, preferred_element_type=f32)


def shards(
    tokens,
    norm1_gain,
    in_weight,
    conv_weight,
    conv_bias,
    gate_matrix,
    gate_bias,
    decay_rate,
    out_weight,
    norm2_gain,
    mlp_weight,
    down_weight,
    cotangent,
):
    seqs, piece, width = tokens.shape
    rows = seqs * piece
    lanes = in_weight.shape[2]
    units = mlp_weight.shape[2]
    heads, head_width = gate_matrix.shape[1:3]
    taps = conv_weight.shape[0]
    n = lax.axis_size("seq")
    part = width // n
    order = ring_order(n)
    place = [order.index(i) for i in range(n)]
    me = jnp.asarray(place, jnp.int32)[lax.axis_index("seq")]
    chunk = jnp.asarray(order, jnp.int32)[(me - jnp.arange(n, dtype=jnp.int32)) % n]
    odd = lax.axis_index("tp") % 2
    sequence = (jnp.arange(seqs, dtype=jnp.int32) + odd * (seqs // 2)) % seqs
    move = (sequence, chunk)
    ring = Ring(order, lane_depth)
    tiled = part % 128 == 0

    def sl(a, k):
        return a[:, k * part : (k + 1) * part]

    move = (sequence, chunk)
    w_in = jnp.transpose(in_weight, (1, 2, 0))
    half_lanes = lanes // 2
    own_gain = jnp.pad(jnp.stack([norm1_gain, norm2_gain]), ((0, 14), (0, 0)))
    first = Gather(jnp.concatenate([w_in[0], out_weight[:half_lanes]], axis=0), 1, n, chunk)
    second = Gather(
        jnp.concatenate([w_in[1], out_weight[half_lanes:], own_gain], axis=0), -1, n, chunk
    )
    mlp = [Gather(mlp_weight[:, 0], 1, n, chunk), Gather(mlp_weight[:, 1], -1, n, chunk)]
    downs = Gather(down_weight, 1, n, chunk)
    ring.add([first, second])
    ring.add([*mlp, downs], [0, 0, 3])
    ring.issue()

    tokens, cotangent = ring.land((tokens, cotangent))
    if tiled:
        x, cot = by_rows(enter_kernel, [tokens, cotangent], [], [bf16] * 2, 0, move)
    else:
        x, cot = own_order(tokens, move), own_order(cotangent, move)
    full = x.shape
    part_full = (seqs // 2, piece, width)
    x, cot, tail_rows = ring.land((x, cot, tokens[:, piece - taps + 1 :]))
    behind_rows = lax.ppermute(tail_rows, "seq", [(i, i + 1) for i in range(n - 1)])
    grad_low = cot.reshape(rows, width)
    start = x.reshape(rows, width).astype(f32)
    inverse1 = lax.rsqrt(jnp.mean(start * start, axis=-1, keepdims=True) + eps)
    count = seqs * (taps - 1)

    def start_of(behind):
        values = behind[sequence].reshape(count, n, part)[:, chunk].reshape(count, width)
        values = jnp.pad(values.astype(f32), ((0, -count % 16), (0, 0)))
        return values, lax.rsqrt(jnp.mean(values * values, axis=-1, keepdims=True) + eps)

    normed1, pieces0, pieces1, gains = {}, {}, {}, {}
    totals = None

    def use(k, piece0, piece1):
        nonlocal totals
        pieces0[k], pieces1[k] = piece0, piece1
        gains[k] = piece1[lanes + half_lanes : lanes + half_lanes + 2]
        normed1[k] = (sl(start, k) * inverse1 * gains[k][:1].astype(f32)).astype(bf16)
        shares = across(normed1[k], piece0[:lanes]), across(normed1[k], piece1[:lanes])
        totals = shares if totals is None else tuple(t + s for t, s in zip(totals, shares))

    for turn in range(n - 3):
        if turn == landings[0]:
            behind_rows = ring.land(behind_rows)
        else:
            ring.land()
    for k, (piece0, piece1) in enumerate(zip(first.slots(), second.slots())):
        use(k, piece0, piece1)
    inner, gate_in = (t.astype(bf16) for t in totals)
    first, second = ([pieces[k] for k in range(n)] for pieces in (pieces0, pieces1))
    in0 = [p[:lanes] for p in first]
    in1 = [p[:lanes] for p in second]
    gain1, gain2 = (
        jnp.concatenate([gains[k][i : i + 1] for k in range(n)], axis=1).astype(f32)
        for i in range(2)
    )
    w_both = jnp.concatenate([jnp.concatenate(in0, axis=1), jnp.concatenate(in1, axis=1)], axis=0)
    start_before, inverse_before = start_of(behind_rows)
    normed_before = (start_before * inverse_before * gain1).astype(bf16)
    before = across(normed_before, w_both[:lanes]).astype(bf16)
    before = before[:count].astype(f32).reshape(seqs, taps - 1, lanes)
    before = jnp.pad(before, ((0, 0), (pad_rows - taps + 1, 0), (0, 0)))
    inner = inner.reshape(seqs, piece, lanes)
    gate_in = gate_in.reshape(seqs, piece, lanes)
    inner = ring.land(inner, landings[1])
    conv_w = conv_weight.astype(f32)
    rate = decay_rate.astype(f32)[None]
    gate_m = dense_heads(gate_matrix)
    wide = (seqs, piece, lanes)
    edge = (seqs, pad_rows, lanes)
    gate_flops = 4 * rows * lanes * lanes
    mixed, recur, admit, decay, root, cum, local, ends = per_sequence(
        forward_kernel,
        seqs,
        [
            (inner, "seq"),
            (before, "seq"),
            (conv_w, "whole"),
            (conv_bias.astype(f32)[None], "whole"),
            (gate_m, "whole"),
            (gate_bias.astype(f32), "whole"),
            (rate, "whole"),
        ],
        [(wide, f32, "seq")] * 7 + [(edge, f32, "seq")],
        [pltpu.VMEM((piece + pad_rows, lanes), f32), pltpu.VMEM((2, piece, lanes), f32)],
        gate_flops,
    )
    ends = ring.land(ends, landings[2])
    entry = carried(ends, 1, n, lambda v: ring.land(v, landings[3]))
    entry = ring.land(entry, landings[4])
    states = local + cum * entry[:, :1]
    product = (states * gelu_parts(gate_in.astype(f32))[0]).astype(bf16).reshape(rows, lanes)
    w_out = jnp.concatenate(
        [
            jnp.concatenate([p[lanes : lanes + half_lanes] for p in pieces], axis=1)
            for pieces in (first, second)
        ],
        axis=0,
    )
    block = rows // 2

    def half_of(a, h):
        return a[h * block : (h + 1) * block]

    def lands(values, count):
        for _ in range(count - 1):
            ring.land()
        return ring.land(values)

    chips = []

    def keep(chip):
        chips.append(ring.land(chip, landings[6]))
        return chips[0]

    recurrent = tp_sum(
        lambda h: dot(half_of(product, h), w_out),
        others=lambda v: ring.land(v, landings[5]),
        chips=keep,
        totals=lambda v: lands(v, landings[7]),
    )
    gate_act, gate_slope = gelu_parts(after(gate_in, chips[0]).astype(f32))

    middle, normed2 = in_halves(
        norm_kernel, [x], [r.reshape(part_full) for r in recurrent], [gain2], [f32, bf16], 0
    )
    normed2 = ring.land(normed2.reshape(rows, width), landings[8])
    ring.need(mlp)
    w_mlp = jnp.concatenate([jnp.concatenate(w.slots(), axis=0) for w in mlp], axis=1)
    both = dot(normed2, w_mlp).astype(bf16)
    both0, both1 = both[:, :units].astype(f32), both[:, units:].astype(f32)
    act, slope = gelu_parts(both0)
    hidden = (act * both1).astype(bf16)
    hidden, act, slope = ring.land(
        (hidden, act.astype(bf16), (slope * both1).astype(bf16)), landings[9]
    )
    ring.drain()
    w_down = jnp.concatenate(downs.slots(), axis=1)
    grad_both = []
    grad_down = Scatter(lambda k: down(hidden, sl(grad_low, k)), 1, n, chunk)
    grad_mlp = Scatter(lambda k: down(sl(normed2, k), grad_both[0]), -1, n, chunk)
    ring.add([grad_down, grad_mlp])
    ring.issue(landings[10])
    act, slope, w_down = ring.hold((act, slope, w_down))
    grad_both.append(
        pl.pallas_call(
            hidden_back_kernel,
            grid=(seqs,),
            in_specs=[
                pl.BlockSpec((piece, width), lambda s: (s, 0)),
                pl.BlockSpec((units, width), lambda s: (0, 0)),
                pl.BlockSpec((piece, units), lambda s: (s, 0)),
                pl.BlockSpec((piece, units), lambda s: (s, 0)),
            ],
            out_specs=pl.BlockSpec((piece, 2 * units), lambda s: (s, 0)),
            out_shape=jax.ShapeDtypeStruct((rows, 2 * units), bf16),
            compiler_params=pltpu.CompilerParams(vmem_limit_bytes=vmem_bytes),
            cost_estimate=pl.CostEstimate(
                flops=2 * rows * width * units,
                bytes_accessed=moved_bytes(grad_low, w_down, act, slope, both),
                transcendentals=0,
            ),
        )(grad_low, w_down, act, slope)
    )
    ring.issue()
    grad_normed2 = tp_sum(
        lambda h: across(half_of(grad_both[0], h), w_mlp),
        others=lambda v: ring.land(v, landings[11]),
        owns=lambda v: ring.land(v, landings[12]),
        chips=lambda v: ring.land(v, landings[13]),
        totals=lambda v: lands(v, landings[14]),
    )
    turned = jnp.concatenate([half_of(hidden, 1), half_of(hidden, 0)], axis=0)
    turned = jnp.where(odd == 1, turned, hidden)

    grad_middle, grad_rec, sum_gain2 = in_halves(
        middle_back_kernel,
        [middle, cot],
        [g.reshape(part_full) for g in grad_normed2],
        [gain2],
        [f32, bf16],
        1,
    )
    grad_out = Scatter(lambda k: down(product, sl(grad_rec, k)), 1, n, chunk)
    ring.add([grad_out])
    grad_rec = ring.land(grad_rec.reshape(rows, width), landings[15])
    mlp_out = lax.psum(dot(after(turned, grad_middle), w_down).astype(bf16), "tp")

    grad_product = across(grad_rec, w_out).reshape(wide)
    tail, local_grad, early = per_sequence(
        reverse_kernel,
        seqs,
        [(grad_product, "seq"), (gate_act, "seq"), (decay, "seq")],
        [(wide, f32, "seq")] * 2 + [(edge, f32, "seq")],
        [pltpu.VMEM((piece, lanes), f32)],
        rows * lanes * 50,
    )
    early = ring.land(early, landings[16])
    incoming = carried(early, -1, n, lambda v: ring.land(v, landings[17]))
    incoming = ring.land(incoming, landings[18])
    grad_gates, grad_inner, grad_gate_in, head, last, sums = per_sequence(
        gates_back_kernel,
        seqs,
        [
            (grad_product, "seq"),
            (gate_slope, "seq"),
            (tail, "seq"),
            (local_grad, "seq"),
            (incoming, "seq"),
            (states, "seq"),
            (entry, "seq"),
            (recur, "seq"),
            (admit, "seq"),
            (decay, "seq"),
            (root, "seq"),
            (mixed, "seq"),
            (inner, "seq"),
            (before, "seq"),
            (gate_m, "whole"),
            (rate, "whole"),
            (conv_w, "whole"),
        ],
        [
            ((2,) + wide, bf16, "pair"),
            (wide, bf16, "seq"),
            (wide, bf16, "seq"),
            (edge, f32, "seq"),
            (edge, f32, "seq"),
            ((pad_rows, lanes), f32, "whole"),
        ],
        [pltpu.VMEM((piece, lanes), f32)] + [pltpu.VMEM((piece + pad_rows, lanes), f32)] * 2,
        gate_flops,
    )
    head = ring.land(head, landings[19])
    behind = lax.ppermute(
        head[:, : taps - 1].astype(bf16), "seq", [(i + 1, i) for i in range(n - 1)]
    ).astype(f32)
    beyond = jnp.concatenate([jnp.zeros_like(last), behind], axis=1)
    beyond = jnp.pad(beyond, ((0, 0), (0, 1), (0, 0)))
    for lag in range(1, taps):
        last = last + conv_w[lag] * beyond[:, lag : lag + pad_rows]
    grad_inner = lax.dynamic_update_slice(
        grad_inner, last.astype(bf16), (0, piece - pad_rows, 0)
    )
    back0 = grad_inner.reshape(rows, lanes)
    back1 = grad_gate_in.reshape(rows, lanes)
    back = ring.land(jnp.concatenate([back0, back1], axis=1), landings[20])
    grads = [
        Scatter(lambda k: down(back0, normed1[k]), 1, n, chunk),
        Scatter(lambda k: down(back1, normed1[k]), -1, n, chunk),
    ]
    ring.add(grads)
    ring.issue()
    late = []

    def hold_output(chip):
        late.append(after(mlp_out, chip))
        return ring.land(chip, landings[22])

    grad_normed1 = tp_sum(
        lambda h: dot(half_of(back, h), w_both),
        others=lambda v: ring.land(v, landings[21]),
        chips=hold_output,
        totals=lambda v: lands(v, landings[23]),
    )
    mlp_out = late[0]
    ready = None
    if tiled:
        summed1 = [g.reshape(part_full) for g in grad_normed1]
        ready = by_rows(
            start_back_kernel,
            [x, summed1[0], grad_middle],
            [gain1],
            [f32],
            0,
            move,
            back=True,
            half=0,
        )
        grad_tokens = by_rows(
            start_back_kernel,
            [x, summed1[1], grad_middle],
            [gain1],
            [f32],
            0,
            move,
            back=True,
            half=1,
            earlier=ready,
        )[0]
        ring.resume(grad_tokens)
        total1 = after(grad_normed1[0], ready[0])
    else:
        total1 = grad_normed1[0]
    ring.drain()
    grads = [g.total() for g in grads]
    low_mixed = mixed.astype(bf16).reshape(rows, lanes)
    grad_matrix = []
    for k in range(2):
        dense = down(low_mixed, grad_gates[k].reshape(rows, lanes)).astype(bf16)
        for h in range(heads):
            at = slice(h * head_width, (h + 1) * head_width)
            grad_matrix.append(dense[at, at])
    packed = jnp.concatenate(
        grad_matrix + [sums.astype(bf16).reshape(-1, head_width)], axis=0
    )
    packed = lax.psum(packed, "seq")

    if tiled:
        output = by_rows(
            output_kernel,
            [middle, mlp_out.reshape(full)],
            [],
            [bf16],
            0,
            move,
            back=True,
            moved=(1,),
        )[0]
    else:
        mlp_out = mlp_out.reshape(full)[sequence].astype(f32)
        output = own_order((middle + mlp_out).astype(bf16), move, True)
        grad_normed1_all = jnp.concatenate(grad_normed1, axis=0).reshape(full).astype(f32)
        grad_start = norm_back(x.astype(f32), grad_normed1_all, gain1)[0]
        grad_tokens = own_order(grad_middle + grad_start, move, True)
    mine = lax.axis_index("seq")
    slots = (me - jnp.asarray(place, jnp.int32)) % n
    scaled1 = start[:block] * inverse1[:block]
    sum_gain1 = jnp.sum(total1.astype(f32) * scaled1, axis=0)
    grad_gains = jnp.stack([sum_gain1, 0.5 * jnp.sum(sum_gain2, axis=0)])
    grad_gains = grad_gains + core_swap(grad_gains)
    grad_gains = seq_sum(grad_gains.reshape(2, n, part)[:, slots], n)
    grad_gains = lax.dynamic_index_in_dim(grad_gains, mine, 1, keepdims=False)

    packed, grad_gains = lax.optimization_barrier((packed, grad_gains))
    packed = packed.astype(f32)
    matrix_rows = 2 * heads * head_width
    grad_matrix = packed[:matrix_rows].reshape(gate_matrix.shape)
    small = packed[matrix_rows:].reshape(4 + taps, lanes)
    return (
        output,
        grad_tokens,
        grad_gains[0],
        jnp.transpose(jnp.stack(grads[:2]), (2, 0, 1)),
        small[4:],
        small[3],
        grad_matrix,
        small[1:3],
        small[0],
        grad_out.total(),
        grad_gains[1],
        grad_mlp.total().reshape(part, 2, units),
        grad_down.total(),
    )


def solution(mesh):
    in_specs = (
        P(None, "seq", None),
        P("seq"),
        P("seq", None, "tp"),
        P(None, "tp"),
        P("tp"),
        P(None, "tp", None, None),
        P(None, "tp"),
        P("tp"),
        P("tp", "seq"),
        P("seq"),
        P("seq", None, "tp"),
        P("tp", "seq"),
        P(None, "seq", None),
    )
    out_specs = (
        P(None, "seq", None),
        P(None, "seq", None),
        P("seq"),
        P("seq", None, "tp"),
        P(None, "tp"),
        P("tp"),
        P(None, "tp", None, None),
        P(None, "tp"),
        P("tp"),
        P("tp", "seq"),
        P("seq"),
        P("seq", None, "tp"),
        P("tp", "seq"),
    )
    return jax.shard_map(shards, mesh=mesh, in_specs=in_specs, out_specs=out_specs, check_vma=False)
```

```python
import functools
import math

import jax
import jax.numpy as jnp
from jax import lax
from jax.experimental import pallas as pl
from jax.experimental.pallas import tpu as pltpu
from jax.sharding import PartitionSpec as P

f32 = jnp.float32
bf16 = jnp.bfloat16
eps = 1e-06
gelu_scale = math.sqrt(2.0 / math.pi)
step_rows = 16
pad_rows = 8
vmem_bytes = 48 * 2**20
ring_most = 8
lane_depth = 2
norm_rows = 128


def ring_order(n):
    return [*range(0, n, 2), *range(n - 1 - n % 2, 0, -2)]


def after(values, *earlier):
    return lax.optimization_barrier((values, *earlier))[0]


class Ring:
    def __init__(self, order, depth):
        n = len(order)
        self.n = n
        self.depth = depth
        self.pairs = {w: [(order[i], order[(i + w) % n]) for i in range(n)] for w in (1, -1)}
        self.queue = {1: [], -1: []}
        self.flying = {1: [], -1: []}
        self.landed = {1: [], -1: []}
        self.sent = {1: 0, -1: 0}
        self.last = {1: None, -1: None}
        self.token = None

    def add(self, weights, delays=None):
        half = self.n // 2
        delays = delays or [0] * len(weights)
        left = {id(flow): flow.count for w in weights for flow in w.flows.values()}
        for turn in range(half + max(delays)):
            for late in (True, False):
                for weight, delay in zip(weights, delays):
                    if (delay > 0) != late or turn < delay:
                        continue
                    for way, flow in weight.flows.items():
                        if left[id(flow)]:
                            left[id(flow)] -= 1
                            self.queue[way].append(flow)

    def issue(self, most=None):
        for way in (1, -1):
            queue, flying, landed = self.queue[way], self.flying[way], self.landed[way]
            while queue and len(flying) < (most or self.depth) and not queue[0].busy:
                flow = queue.pop(0)
                message = flow.message()
                gate = self.sent[way] - self.depth
                if gate >= 0:
                    message = after(message, landed[gate])
                if self.token is not None:
                    message = after(message, self.token)
                flow.busy = True
                self.sent[way] += 1
                self.last[way] = message
                flying.append((flow, lax.ppermute(message, "seq", self.pairs[way])))

    def hold(self, values):
        last = [message for message in self.last.values() if message is not None]
        return after(values, *last) if last else values

    def resume(self, token):
        self.token = token
        self.issue()
        return token

    def quiet(self, values):
        waiting = {w: self.queue[w] for w in (1, -1)}
        self.queue = {1: [], -1: []}
        for _ in range(self.depth):
            values = self.land(values)
        self.queue = waiting
        return values

    def land(self, values=None, count=1):
        for turn in range(count):
            taken = [(w, *self.flying[w].pop(0)) for w in (1, -1) if self.flying[w]]
            arrived = [message for _, _, message in taken]
            if values is not None and taken and turn == count - 1:
                values, *arrived = lax.optimization_barrier((values, *arrived))
            for (way, flow, _), message in zip(taken, arrived):
                flow.arrive(message)
                flow.busy = False
                self.landed[way].append(message)
            self.issue()
        return values

    def drain(self):
        while self.queue[1] or self.queue[-1] or self.flying[1] or self.flying[-1]:
            self.land()


class Pieces:
    def __init__(self, own, count):
        self.value, self.count, self.busy, self.got = own, count, False, []

    def message(self):
        return self.value

    def arrive(self, message):
        self.value = message
        self.got.append(message)


class Totals:
    def __init__(self, part, slots):
        self.part, self.slots, self.count, self.busy = part, slots, len(slots), False
        self.got, self.at = None, 0

    def message(self):
        total = self.part(self.slots[self.at])
        if self.got is not None:
            total = total + self.got.astype(f32)
        self.at += 1
        return total.astype(bf16)

    def arrive(self, message):
        self.got = message


class Gather:
    def __init__(self, piece, far, n, chunk):
        half = n // 2
        self.piece, self.n, self.chunk, self.flows = piece, n, chunk, {}
        if n <= ring_most:
            self.flows = {w: Pieces(piece, half if w == far else half - 1) for w in (1, -1)}

    def slots(self):
        if not self.flows:
            pieces = lax.all_gather(self.piece, "seq")[self.chunk]
            return [pieces[k] for k in range(self.n)]
        return [self.piece, *self.flows[1].got, *self.flows[-1].got[::-1]]


class Scatter:
    def __init__(self, part, far, n, chunk):
        half = n // 2
        self.part, self.n, self.chunk, self.flows = part, n, chunk, {}
        if n <= ring_most:
            self.flows = {
                1: Totals(part, list(range(half if far == 1 else half + 1, n))),
                -1: Totals(part, list(range(half if far == -1 else half - 1, 0, -1))),
            }

    def total(self):
        if not self.flows:
            parts = jnp.stack([self.part(k).astype(bf16) for k in range(self.n)])
            parts = parts[jnp.argsort(self.chunk)]
            return lax.psum_scatter(parts, "seq", scatter_dimension=0).astype(f32)
        total = self.part(0)
        for flow in self.flows.values():
            if flow.got is not None:
                total = total + flow.got.astype(f32)
        return total


def core_swap(values):
    size = lax.axis_size("tp")
    return lax.ppermute(values, "tp", [(i, i ^ 1) for i in range(size)])


def chip_swap(values):
    size = lax.axis_size("tp")
    return lax.ppermute(values, "tp", [(i, i ^ 2) for i in range(size)])


def tp_sum(part, others=lambda v: v, chips=lambda v: v, totals=lambda v: v):
    got = core_swap(others(part(1).astype(bf16)))
    own = lax.optimization_barrier(part(0).astype(bf16))
    chip = chips((own.astype(f32) + got.astype(f32)).astype(bf16))
    far = chip_swap(chip)
    total = totals((chip.astype(f32) + far.astype(f32)).astype(bf16))
    return total, core_swap(total)


def gelu_parts(x):
    t = jnp.tanh(gelu_scale * (x + 0.044715 * x * x * x))
    value = 0.5 * x * (1.0 + t)
    slope = 0.5 * (1.0 + t) + 0.5 * x * (1.0 - t * t) * gelu_scale * (1.0 + 3 * 0.044715 * x * x)
    return value, slope


def drive_square(log_decay, decay):
    y = -2.0 * log_decay
    series = 1.0 - y * (1.0 / 9.0)
    for k in range(8, 1, -1):
        series = 1.0 - y * (1.0 / k) * series
    return jnp.where(y < 0.5, y * series, 1.0 - decay * decay)


def scan_block(a, b, rows, reverse):
    count = a.shape[0]
    by = 1
    while by < count:
        turn = count - by if reverse else by
        pa = pltpu.roll(a, turn, 0)
        pb = pltpu.roll(b, turn, 0)
        inside = rows < count - by if reverse else rows >= by
        b = jnp.where(inside, a * pb + b, b)
        a = jnp.where(inside, a * pa, a)
        by *= 2
    return a, b


def forward_kernel(
    inner, before, conv_w, conv_b, gate_m, gate_b, rate,
    mixed, recur, admit, decay, root, cum, local, ends, ext, gates,
):
    length, lanes = inner.shape
    ext[:pad_rows] = before[...]
    ext[pad_rows:] = inner[...].astype(f32)
    taps = conv_w.shape[0]
    total = jnp.broadcast_to(conv_b[...], (length, lanes))
    for lag in range(taps):
        total = total + conv_w[lag : lag + 1] * ext[pad_rows - lag : pad_rows - lag + length]
    mixed[...] = total
    low = total.astype(bf16)
    for k in range(2):
        gates[k] = jnp.dot(low, gate_m[k], preferred_element_type=f32) + gate_b[k : k + 1]
    rows = lax.broadcasted_iota(jnp.int32, (step_rows, lanes), 0)

    def step(i, carry):
        at = pl.ds(pl.multiple_of(i * step_rows, step_rows), step_rows)
        r = jax.nn.sigmoid(gates[0, at])
        g = jax.nn.sigmoid(gates[1, at])
        log_decay = -8.0 * r * rate[...]
        d = jnp.exp(log_decay)
        m = jnp.sqrt(drive_square(log_decay, d))
        drive = m * g * mixed[at]
        root[at] = m
        recur[at] = r
        admit[at] = g
        decay[at] = d
        a, b = scan_block(d, drive, rows, False)
        b = b + a * carry[1]
        a = a * carry[0]
        cum[at] = a
        local[at] = b
        return a[step_rows - 1 :], b[step_rows - 1 :]

    a, b = lax.fori_loop(
        0, length // step_rows, step, (jnp.ones((1, lanes), f32), jnp.zeros((1, lanes), f32))
    )
    ends[0:1] = a
    ends[1:2] = b
    ends[2:] = jnp.zeros((pad_rows - 2, lanes), f32)


def reverse_kernel(grad_product, act, decay, tail, grad, first, nexts):
    length, lanes = act.shape
    nexts[...] = pltpu.roll(decay[...], length - 1, 0)
    nexts[length - 1 :] = jnp.ones((1, lanes), f32)
    rows = lax.broadcasted_iota(jnp.int32, (step_rows, lanes), 0)
    steps = length // step_rows

    def step(i, carry):
        at = pl.ds(pl.multiple_of((steps - 1 - i) * step_rows, step_rows), step_rows)
        direct = grad_product[at] * act[at]
        a, b = scan_block(nexts[at], direct, rows, True)
        b = b + a * carry[1]
        a = a * carry[0]
        tail[at] = a
        grad[at] = b
        return a[:1], b[:1]

    a, b = lax.fori_loop(0, steps, step, (jnp.ones((1, lanes), f32), jnp.zeros((1, lanes), f32)))
    first[0:1] = decay[0:1] * a
    first[1:2] = decay[0:1] * b
    first[2:] = jnp.zeros((pad_rows - 2, lanes), f32)


def gates_back_kernel(
    grad_product, slope, tail, grad, incoming, states, entry, recur, admit, decay, root, mixed, inner, before,
    gate_m, rate, conv_w, grad_gates, grad_inner, grad_gate_in, head, last, sums, grad_mix, grad_ext, ext,
):
    length, lanes = inner.shape
    enter = entry[0:1]
    later = incoming[0:1]
    taps = conv_w.shape[0]

    def step(i, carry):
        at = pl.ds(pl.multiple_of(i * step_rows, step_rows), step_rows)
        state = states[at]
        rows = lax.broadcasted_iota(jnp.int32, (step_rows, lanes), 0)
        earlier = jnp.where(rows == 0, carry[3], pltpu.roll(state, 1, 0))
        grad_gate_in[at] = (slope[at] * (grad_product[at] * state)).astype(bf16)
        total = grad[at] + tail[at] * later
        r, g, d, m, mix = recur[at], admit[at], decay[at], root[at], mixed[at]
        grad_mix[at] = total * m * g
        both = total * mix
        gate1 = both * m * g * (1.0 - g)
        grad_log = total * earlier * d - both * g * d * d / m
        gate0 = -8.0 * rate[...] * grad_log * r * (1.0 - r)
        low0 = gate0.astype(bf16)
        low1 = gate1.astype(bf16)
        grad_gates[0, at] = low0
        grad_gates[1, at] = low1
        return (
            carry[0] - 8.0 * (grad_log * r),
            carry[1] + low0.astype(f32),
            carry[2] + low1.astype(f32),
            state[step_rows - 1 :],
        )

    zero = jnp.zeros((step_rows, lanes), f32)
    totals = lax.fori_loop(0, length // step_rows, step, (zero, zero, zero, enter))
    back = grad_mix[...]
    for k in range(2):
        back = back + lax.dot_general(
            grad_gates[k], gate_m[k], (((1,), (1,)), ((), ())), preferred_element_type=f32
        )
    back = back.astype(bf16).astype(f32)
    head[...] = back[:pad_rows]
    grad_ext[:length] = back
    grad_ext[length:] = jnp.zeros((pad_rows, lanes), f32)
    ext[:pad_rows] = before[...]
    ext[pad_rows:] = inner[...].astype(f32)

    @pl.when(pl.program_id(0) == 0)
    def _():
        sums[...] = jnp.zeros_like(sums)

    for k in range(3):
        sums[k : k + 1] += jnp.sum(totals[k], axis=0, keepdims=True)
    sums[3:4] += jnp.sum(back, axis=0, keepdims=True)
    total = jnp.zeros((length, lanes), f32)
    for lag in range(taps):
        total = total + conv_w[lag : lag + 1] * grad_ext[lag : lag + length]
        term = back * ext[pad_rows - lag : pad_rows - lag + length]
        sums[4 + lag : 5 + lag] += jnp.sum(term, axis=0, keepdims=True)
    grad_inner[...] = total.astype(bf16)
    last[...] = total[length - pad_rows :]


def hidden_back_kernel(cot, w_down, act, slope, grad_both):
    units = w_down.shape[0]
    cut = math.gcd(units, 512)
    for j in range(0, units, cut):
        grad = lax.dot_general(
            cot[...], w_down[j : j + cut], (((1,), (1,)), ((), ())), preferred_element_type=f32
        )
        grad_both[:, j : j + cut] = (grad * slope[:, j : j + cut].astype(f32)).astype(bf16)
        grad_both[:, units + j : units + j + cut] = (
            grad * act[:, j : j + cut].astype(f32)
        ).astype(bf16)


def per_sequence(kernel, seqs, inputs, outputs, scratch, flops):
    def spec(shape, kind):
        if kind == "whole":
            return pl.BlockSpec(shape, lambda s: (0,) * len(shape))
        if kind == "pair":
            return pl.BlockSpec((shape[0], None) + shape[2:], lambda s: (0, s, 0, 0))
        return pl.BlockSpec((None,) + shape[1:], lambda s: (s,) + (0,) * (len(shape) - 1))

    moved = sum(a.size * a.dtype.itemsize for a, _ in inputs)
    moved += sum(math.prod(shape) * jnp.dtype(t).itemsize for shape, t, _ in outputs)
    return pl.pallas_call(
        kernel,
        grid=(seqs,),
        in_specs=[spec(a.shape, kind) for a, kind in inputs],
        out_specs=[spec(shape, kind) for shape, _, kind in outputs],
        out_shape=[jax.ShapeDtypeStruct(shape, t) for shape, t, _ in outputs],
        scratch_shapes=scratch,
        compiler_params=pltpu.CompilerParams(vmem_limit_bytes=vmem_bytes),
        cost_estimate=pl.CostEstimate(flops=flops, bytes_accessed=moved, transcendentals=0),
    )(*[a for a, _ in inputs])


def moved_bytes(*arrays):
    return sum(math.prod(a.shape) * jnp.dtype(a.dtype).itemsize for a in arrays)


def by_rows(
    kernel, arrays, whole, outputs, sums, order=None, back=False, moved=(), half=None, earlier=()
):
    seqs, length, width = arrays[0].shape
    block = min(norm_rows, length)
    count = seqs if half is None else seqs // 2
    skip = count * (half or 0)
    moves = order is not None
    tile = (None, block, width)
    near = pl.BlockSpec(tile, lambda s, r, *_: (s + skip, r, 0))
    own = pl.BlockSpec(tile, lambda s, r, *_: (s, r, 0))
    far = pl.BlockSpec(tile, lambda s, r, sequence, chunk: (sequence[s + skip], r, 0))
    total = pl.BlockSpec((pad_rows, width), lambda s, r, *_: (0, 0))
    out_shape = [jax.ShapeDtypeStruct((seqs, length, width), t) for t in outputs]
    out_shape += [jax.ShapeDtypeStruct((pad_rows, width), f32)] * sums
    scalars = 2 if moves else 0
    given = scalars + len(arrays) + len(whole)

    def body(*refs):
        kernel(*refs[:given], *refs[given + len(earlier) :])

    return pl.pallas_call(
        body,
        grid_spec=pltpu.PrefetchScalarGridSpec(
            num_scalar_prefetch=scalars,
            grid=(count, length // block),
            in_specs=[
                own
                if a.shape[0] != seqs
                else far
                if moves and (not back or i in moved)
                else near
                for i, a in enumerate(arrays)
            ]
            + [pl.BlockSpec(w.shape, lambda s, r, *_: (0, 0)) for w in whole]
            + [pl.BlockSpec(memory_space=pl.ANY)] * len(earlier),
            out_specs=[far if moves and back else near] * len(outputs) + [total] * sums,
        ),
        out_shape=out_shape,
        input_output_aliases={given + i: i for i in range(len(earlier))},
        compiler_params=pltpu.CompilerParams(vmem_limit_bytes=vmem_bytes),
        cost_estimate=pl.CostEstimate(
            flops=8 * count * length * width,
            bytes_accessed=moved_bytes(*arrays, *out_shape) * count // seqs,
            transcendentals=0,
        ),
    )(*(order if moves else ()), *arrays, *whole, *earlier)


def in_halves(kernel, arrays, summed, whole, outputs, sums, order=None, back=False):
    ready = by_rows(
        kernel, [arrays[0], summed[0], *arrays[1:]], whole, outputs, sums, order, back, (), 0
    )
    count = len(outputs)
    done = by_rows(
        kernel,
        [arrays[0], summed[1], *arrays[1:]],
        whole,
        outputs,
        sums,
        order,
        back,
        (),
        1,
        tuple(ready[:count]),
    )
    return [*done[:count], *(a + b for a, b in zip(ready[count:], done[count:]))]


def enter_kernel(sequence, chunk, *refs):
    count = len(refs) // 2
    part = refs[0].shape[1] // chunk.shape[0]
    for k in range(chunk.shape[0]):
        at = pl.ds(pl.multiple_of(chunk[k] * part, part), part)
        for i in range(count):
            refs[count + i][:, k * part : (k + 1) * part] = refs[i][:, at]


def norm_kernel(x, added, gain, middle, normed):
    total = x[...].astype(f32) + added[...].astype(f32)
    middle[...] = total
    inverse = lax.rsqrt(jnp.mean(total * total, axis=-1, keepdims=True) + eps)
    normed[...] = (total * inverse * gain[...]).astype(bf16)


def norm_back(values, grad, gain):
    inverse = lax.rsqrt(jnp.mean(values * values, axis=-1, keepdims=True) + eps)
    scaled = values * inverse
    weighted = grad * gain
    inner = jnp.mean(weighted * scaled, axis=-1, keepdims=True)
    return inverse * (weighted - scaled * inner), grad * scaled


def add_rows(total, values):
    @pl.when((pl.program_id(0) == 0) & (pl.program_id(1) == 0))
    def _():
        total[...] = jnp.zeros_like(total)

    rows, width = values.shape
    total[...] += jnp.sum(values.reshape(rows // pad_rows, pad_rows, width), axis=0)


def middle_back_kernel(middle, grad_normed, cot, gain, grad_middle, grad_low, total):
    grad, terms = norm_back(middle[...], grad_normed[...].astype(f32), gain[...])
    grad = grad + cot[...].astype(f32)
    grad_middle[...] = grad
    grad_low[...] = grad.astype(bf16)
    add_rows(total, terms)


def put_chunks(chunk, target, values):
    part = values.shape[1] // chunk.shape[0]
    for k in range(chunk.shape[0]):
        at = pl.ds(pl.multiple_of(chunk[k] * part, part), part)
        target[:, at] = values[:, k * part : (k + 1) * part]


def start_back_kernel(sequence, chunk, x, grad_normed, grad_middle, gain, grad_tokens):
    grad = norm_back(x[...].astype(f32), grad_normed[...].astype(f32), gain[...])[0]
    put_chunks(chunk, grad_tokens, grad + grad_middle[...])


def output_kernel(sequence, chunk, middle, added, output):
    put_chunks(chunk, output, (middle[...] + added[...].astype(f32)).astype(bf16))


def own_order(array, order, back=False):
    sequence, chunk = order
    if back:
        sequence, chunk = jnp.argsort(sequence), jnp.argsort(chunk)
    seqs, length, width = array.shape
    chunks = chunk.shape[0]
    split = array[sequence].reshape(seqs, length, chunks, width // chunks)
    return split[:, :, chunk].reshape(array.shape)


def carried(ends, way, n, between=lambda v: v):
    def shifted(values, by):
        pairs = [(i, i + way * by) for i in range(n) if 0 <= i + way * by < n]
        return lax.ppermute(values, "seq", pairs)

    ends = ends[:, :2]
    by = 1
    while 2 * by < n:
        earlier = shifted(ends, by)
        ends = ends[:, :1] * earlier + jnp.concatenate(
            [jnp.zeros_like(ends[:, 1:]), ends[:, 1:]], axis=1
        )
        by *= 2
        if by == 2:
            ends = between(ends)
    near, far = shifted(ends, 1), shifted(ends, 1 + by)
    state = near[:, :1] * far[:, 1:] + near[:, 1:]
    return jnp.pad(state, ((0, 0), (0, pad_rows - 1), (0, 0)))


def seq_sum(values, n):
    by = 1
    while by < n:
        values = values + lax.ppermute(values, "seq", [(i, i ^ by) for i in range(n)])
        by *= 2
    return values


def dense_heads(matrix):
    kinds, heads, width, _ = matrix.shape
    rows = [
        jnp.pad(matrix[:, h], ((0, 0), (0, 0), (h * width, (heads - 1 - h) * width)))
        for h in range(heads)
    ]
    return jnp.concatenate(rows, axis=1)


def across(a, b):
    return lax.dot_general(a, b, (((1,), (1,)), ((), ())), preferred_element_type=f32)


def down(a, b):
    return lax.dot_general(a, b, (((0,), (0,)), ((), ())), preferred_element_type=f32)


def dot(a, b):
    return jnp.dot(a, b, preferred_element_type=f32)


def shards(
    tokens,
    norm1_gain,
    in_weight,
    conv_weight,
    conv_bias,
    gate_matrix,
    gate_bias,
    decay_rate,
    out_weight,
    norm2_gain,
    mlp_weight,
    down_weight,
    cotangent,
):
    seqs, piece, width = tokens.shape
    rows = seqs * piece
    lanes = in_weight.shape[2]
    units = mlp_weight.shape[2]
    heads, head_width = gate_matrix.shape[1:3]
    taps = conv_weight.shape[0]
    n = lax.axis_size("seq")
    part = width // n
    order = ring_order(n)
    place = [order.index(i) for i in range(n)]
    me = jnp.asarray(place, jnp.int32)[lax.axis_index("seq")]
    chunk = jnp.asarray(order, jnp.int32)[(me - jnp.arange(n, dtype=jnp.int32)) % n]
    odd = lax.axis_index("tp") % 2
    sequence = (jnp.arange(seqs, dtype=jnp.int32) + odd * (seqs // 2)) % seqs
    move = (sequence, chunk)
    ring = Ring(order, lane_depth)
    tiled = part % 128 == 0

    def sl(a, k):
        return a[:, k * part : (k + 1) * part]

    move = (sequence, chunk)
    w_in = jnp.transpose(in_weight, (1, 2, 0))
    half_lanes = lanes // 2
    own_gain = jnp.pad(jnp.stack([norm1_gain, norm2_gain]), ((0, 14), (0, 0)))
    first = Gather(jnp.concatenate([w_in[0], out_weight[:half_lanes]], axis=0), 1, n, chunk)
    second = Gather(
        jnp.concatenate([w_in[1], out_weight[half_lanes:], own_gain], axis=0), -1, n, chunk
    )
    mlp = [Gather(mlp_weight[:, 0], 1, n, chunk), Gather(mlp_weight[:, 1], -1, n, chunk)]
    downs = Gather(down_weight, 1, n, chunk)
    ring.add([first, second])
    ring.add([*mlp, downs], [0, 0, 2])
    ring.issue()

    tokens, cotangent = ring.land((tokens, cotangent))
    if tiled:
        x, cot = by_rows(enter_kernel, [tokens, cotangent], [], [bf16, bf16], 0, move)
    else:
        x, cot = own_order(tokens, move), own_order(cotangent, move)
    full = x.shape
    part_full = (seqs // 2, piece, width)
    x, cot = ring.land((x, cot))
    grad_low = cot.reshape(rows, width)
    start = x.reshape(rows, width).astype(f32)
    inverse1 = lax.rsqrt(jnp.mean(start * start, axis=-1, keepdims=True) + eps)
    for _ in range(n - 3):
        ring.land()
    first, second = first.slots(), second.slots()
    in0 = [p[:lanes] for p in first]
    in1 = [p[:lanes] for p in second]
    gains = [p[lanes + half_lanes : lanes + half_lanes + 2] for p in second]
    gain1, gain2 = (
        jnp.concatenate([g[i : i + 1] for g in gains], axis=1).astype(f32) for i in range(2)
    )
    normed1 = [
        (sl(start, k) * inverse1 * gains[k][:1].astype(f32)).astype(bf16) for k in range(n)
    ]
    inner = sum(across(normed1[k], in0[k]) for k in range(n)).astype(bf16)
    gate_in = sum(across(normed1[k], in1[k]) for k in range(n)).astype(bf16)
    inner = ring.land(inner)
    inner = inner.reshape(seqs, piece, lanes)
    gate_in = gate_in.reshape(seqs, piece, lanes)
    before = lax.ppermute(
        inner[:, piece - taps + 1 :], "seq", [(i, i + 1) for i in range(n - 1)]
    ).astype(f32)
    before = ring.land(jnp.pad(before, ((0, 0), (pad_rows - taps + 1, 0), (0, 0))))
    conv_w = conv_weight.astype(f32)
    rate = decay_rate.astype(f32)[None]
    gate_m = dense_heads(gate_matrix)
    wide = (seqs, piece, lanes)
    edge = (seqs, pad_rows, lanes)
    gate_flops = 4 * rows * lanes * lanes
    mixed, recur, admit, decay, root, cum, local, ends = per_sequence(
        forward_kernel,
        seqs,
        [
            (inner, "seq"),
            (before, "seq"),
            (conv_w, "whole"),
            (conv_bias.astype(f32)[None], "whole"),
            (gate_m, "whole"),
            (gate_bias.astype(f32), "whole"),
            (rate, "whole"),
        ],
        [(wide, f32, "seq")] * 7 + [(edge, f32, "seq")],
        [pltpu.VMEM((piece + pad_rows, lanes), f32), pltpu.VMEM((2, piece, lanes), f32)],
        gate_flops,
    )
    entry = ring.land(carried(ring.land(ends), 1, n, ring.land))
    states = local + cum * entry[:, :1]
    product = (states * gelu_parts(gate_in.astype(f32))[0]).astype(bf16).reshape(rows, lanes)
    w_out = jnp.concatenate(
        [
            jnp.concatenate([p[lanes : lanes + half_lanes] for p in pieces], axis=1)
            for pieces in (first, second)
        ],
        axis=0,
    )
    block = rows // 2

    def half_of(a, h):
        return a[h * block : (h + 1) * block]

    def lands(values, count):
        for _ in range(count):
            ring.land()
        return ring.resume(values)

    chips = []

    def keep(chip):
        chips.append(ring.land(chip))
        return chips[0]

    recurrent = tp_sum(
        lambda h: dot(half_of(product, h), w_out),
        chips=keep,
        totals=lambda v: lands(v, 3),
    )
    gate_act, gate_slope = gelu_parts(after(gate_in, chips[0]).astype(f32))

    middle, normed2 = in_halves(
        norm_kernel, [x], [r.reshape(part_full) for r in recurrent], [gain2], [f32, bf16], 0
    )
    normed2 = ring.land(normed2.reshape(rows, width))
    w_mlp = jnp.concatenate([jnp.concatenate(w.slots(), axis=0) for w in mlp], axis=1)
    both = dot(normed2, w_mlp).astype(bf16)
    both0, both1 = both[:, :units].astype(f32), both[:, units:].astype(f32)
    act, slope = gelu_parts(both0)
    hidden = (act * both1).astype(bf16)
    hidden, act, slope = ring.land((hidden, act.astype(bf16), (slope * both1).astype(bf16)))
    ring.drain()
    w_down = jnp.concatenate(downs.slots(), axis=1)
    ring.token = None
    grad_both = []
    grad_down = Scatter(lambda k: down(hidden, sl(grad_low, k)), 1, n, chunk)
    grad_mlp = Scatter(lambda k: down(sl(normed2, k), grad_both[0]), -1, n, chunk)
    ring.add([grad_down, grad_mlp])
    ring.issue(1)
    act, slope, w_down = ring.hold((act, slope, w_down))
    grad_both.append(
        pl.pallas_call(
            hidden_back_kernel,
            grid=(seqs,),
            in_specs=[
                pl.BlockSpec((piece, width), lambda s: (s, 0)),
                pl.BlockSpec((units, width), lambda s: (0, 0)),
                pl.BlockSpec((piece, units), lambda s: (s, 0)),
                pl.BlockSpec((piece, units), lambda s: (s, 0)),
            ],
            out_specs=pl.BlockSpec((piece, 2 * units), lambda s: (s, 0)),
            out_shape=jax.ShapeDtypeStruct((rows, 2 * units), bf16),
            compiler_params=pltpu.CompilerParams(vmem_limit_bytes=vmem_bytes),
            cost_estimate=pl.CostEstimate(
                flops=2 * rows * width * units,
                bytes_accessed=moved_bytes(grad_low, w_down, act, slope, both),
                transcendentals=0,
            ),
        )(grad_low, w_down, act, slope)
    )
    ring.issue()
    grad_normed2 = tp_sum(
        lambda h: across(half_of(grad_both[0], h), w_mlp),
        others=ring.land,
        totals=lambda v: ring.land((ring.land(), v)[1]),
    )
    turned = jnp.concatenate([half_of(hidden, 1), half_of(hidden, 0)], axis=0)
    turned = jnp.where(odd == 1, turned, hidden)

    grad_middle, grad_rec, sum_gain2 = in_halves(
        middle_back_kernel,
        [middle, cot],
        [g.reshape(part_full) for g in grad_normed2],
        [gain2],
        [f32, bf16],
        1,
    )
    grad_out = Scatter(lambda k: down(product, sl(grad_rec, k)), 1, n, chunk)
    ring.add([grad_out])
    grad_rec = ring.land(grad_rec.reshape(rows, width))

    grad_product = across(grad_rec, w_out).reshape(wide)
    tail, local_grad, early = per_sequence(
        reverse_kernel,
        seqs,
        [(grad_product, "seq"), (gate_act, "seq"), (decay, "seq")],
        [(wide, f32, "seq")] * 2 + [(edge, f32, "seq")],
        [pltpu.VMEM((piece, lanes), f32)],
        rows * lanes * 50,
    )
    rounds = []

    def keep_round(ends):
        rounds.append(ends)
        return ends

    incoming = ring.land(carried(ring.land(early), -1, n, keep_round))
    mlp_out = lax.psum(dot(after(turned, *rounds), w_down).astype(bf16), "tp")
    grad_gates, grad_inner, grad_gate_in, head, last, sums = per_sequence(
        gates_back_kernel,
        seqs,
        [
            (grad_product, "seq"),
            (gate_slope, "seq"),
            (tail, "seq"),
            (local_grad, "seq"),
            (incoming, "seq"),
            (states, "seq"),
            (entry, "seq"),
            (recur, "seq"),
            (admit, "seq"),
            (decay, "seq"),
            (root, "seq"),
            (mixed, "seq"),
            (inner, "seq"),
            (before, "seq"),
            (gate_m, "whole"),
            (rate, "whole"),
            (conv_w, "whole"),
        ],
        [
            ((2,) + wide, bf16, "pair"),
            (wide, bf16, "seq"),
            (wide, bf16, "seq"),
            (edge, f32, "seq"),
            (edge, f32, "seq"),
            ((pad_rows, lanes), f32, "whole"),
        ],
        [pltpu.VMEM((piece, lanes), f32)] + [pltpu.VMEM((piece + pad_rows, lanes), f32)] * 2,
        gate_flops,
    )
    behind = lax.ppermute(
        head[:, : taps - 1].astype(bf16), "seq", [(i + 1, i) for i in range(n - 1)]
    ).astype(f32)
    beyond = jnp.concatenate([jnp.zeros_like(last), behind], axis=1)
    beyond = jnp.pad(beyond, ((0, 0), (0, 1), (0, 0)))
    for lag in range(1, taps):
        last = last + conv_w[lag] * beyond[:, lag : lag + pad_rows]
    grad_inner = lax.dynamic_update_slice(
        grad_inner, last.astype(bf16), (0, piece - pad_rows, 0)
    )
    back0 = grad_inner.reshape(rows, lanes)
    back1 = grad_gate_in.reshape(rows, lanes)
    back = ring.land(jnp.concatenate([back0, back1], axis=1))
    w_both = jnp.concatenate([jnp.concatenate(in0, axis=1), jnp.concatenate(in1, axis=1)], axis=0)
    grads = [
        Scatter(lambda k: down(back0, normed1[k]), 1, n, chunk),
        Scatter(lambda k: down(back1, normed1[k]), -1, n, chunk),
    ]
    ring.add(grads)
    ring.issue()
    late = []

    def hold_output(chip):
        late.append(after(mlp_out, chip))
        return ring.land(chip)

    grad_normed1 = tp_sum(
        lambda h: dot(half_of(back, h), w_both),
        chips=hold_output,
        totals=lambda v: lands(v, 4),
    )
    mlp_out = late[0]
    ring.drain()
    grads = [g.total() for g in grads]
    low_mixed = mixed.astype(bf16).reshape(rows, lanes)
    grad_matrix = []
    for k in range(2):
        dense = down(low_mixed, grad_gates[k].reshape(rows, lanes)).astype(bf16)
        for h in range(heads):
            at = slice(h * head_width, (h + 1) * head_width)
            grad_matrix.append(dense[at, at])
    packed = jnp.concatenate(
        grad_matrix + [sums.astype(bf16).reshape(-1, head_width)], axis=0
    )
    packed = lax.psum(packed, "seq")

    if tiled:
        output = by_rows(
            output_kernel,
            [middle, mlp_out.reshape(full)],
            [],
            [bf16],
            0,
            move,
            back=True,
            moved=(1,),
        )[0]
        grad_tokens = in_halves(
            start_back_kernel,
            [x, grad_middle],
            [g.reshape(part_full) for g in grad_normed1],
            [gain1],
            [f32],
            0,
            move,
            back=True,
        )[0]
    else:
        mlp_out = mlp_out.reshape(full)[sequence].astype(f32)
        output = own_order((middle + mlp_out).astype(bf16), move, True)
        grad_normed1_all = jnp.concatenate(grad_normed1, axis=0).reshape(full).astype(f32)
        grad_start = norm_back(x.astype(f32), grad_normed1_all, gain1)[0]
        grad_tokens = own_order(grad_middle + grad_start, move, True)
    mine = lax.axis_index("seq")
    slots = (me - jnp.asarray(place, jnp.int32)) % n
    scaled1 = start[:block] * inverse1[:block]
    sum_gain1 = jnp.sum(grad_normed1[0].astype(f32) * scaled1, axis=0)
    grad_gains = jnp.stack([sum_gain1, 0.5 * jnp.sum(sum_gain2, axis=0)])
    grad_gains = grad_gains + core_swap(grad_gains)
    grad_gains = seq_sum(grad_gains.reshape(2, n, part)[:, slots], n)
    grad_gains = lax.dynamic_index_in_dim(grad_gains, mine, 1, keepdims=False)

    packed, grad_gains = lax.optimization_barrier((packed, grad_gains))
    packed = packed.astype(f32)
    matrix_rows = 2 * heads * head_width
    grad_matrix = packed[:matrix_rows].reshape(gate_matrix.shape)
    small = packed[matrix_rows:].reshape(4 + taps, lanes)
    return (
        output,
        grad_tokens,
        grad_gains[0],
        jnp.transpose(jnp.stack(grads), (2, 0, 1)),
        small[4:],
        small[3],
        grad_matrix,
        small[1:3],
        small[0],
        grad_out.total(),
        grad_gains[1],
        grad_mlp.total().reshape(part, 2, units),
        grad_down.total(),
    )


def solution(mesh):
    in_specs = (
        P(None, "seq", None),
        P("seq"),
        P("seq", None, "tp"),
        P(None, "tp"),
        P("tp"),
        P(None, "tp", None, None),
        P(None, "tp"),
        P("tp"),
        P("tp", "seq"),
        P("seq"),
        P("seq", None, "tp"),
        P("tp", "seq"),
        P(None, "seq", None),
    )
    out_specs = (
        P(None, "seq", None),
        P(None, "seq", None),
        P("seq"),
        P("seq", None, "tp"),
        P(None, "tp"),
        P("tp"),
        P(None, "tp", None, None),
        P(None, "tp"),
        P("tp"),
        P("tp", "seq"),
        P("seq"),
        P("seq", None, "tp"),
        P("tp", "seq"),
    )
    return jax.shard_map(shards, mesh=mesh, in_specs=in_specs, out_specs=out_specs, check_vma=False)
```

```python
import functools
import math

import jax
import jax.numpy as jnp
from jax import lax
from jax.experimental import pallas as pl
from jax.experimental.pallas import tpu as pltpu
from jax.sharding import PartitionSpec as P

f32 = jnp.float32
bf16 = jnp.bfloat16
eps = 1e-06
gelu_scale = math.sqrt(2.0 / math.pi)
step_rows = 16
pad_rows = 8
vmem_bytes = 48 * 2**20
ring_most = 8
lane_depth = 2
norm_rows = 128


def ring_order(n):
    return [*range(0, n, 2), *range(n - 1 - n % 2, 0, -2)]


def after(values, *earlier):
    return lax.optimization_barrier((values, *earlier))[0]


class Ring:
    def __init__(self, order, depth):
        n = len(order)
        self.n = n
        self.depth = depth
        self.pairs = {w: [(order[i], order[(i + w) % n]) for i in range(n)] for w in (1, -1)}
        self.queue = {1: [], -1: []}
        self.flying = {1: [], -1: []}
        self.landed = {1: [], -1: []}
        self.sent = {1: 0, -1: 0}
        self.last = {1: None, -1: None}
        self.token = None

    def add(self, weights, delays=None):
        half = self.n // 2
        delays = delays or [0] * len(weights)
        left = {id(flow): flow.count for w in weights for flow in w.flows.values()}
        for turn in range(half + max(delays)):
            for late in (True, False):
                for weight, delay in zip(weights, delays):
                    if (delay > 0) != late or turn < delay:
                        continue
                    for way, flow in weight.flows.items():
                        if left[id(flow)]:
                            left[id(flow)] -= 1
                            self.queue[way].append(flow)

    def issue(self, most=None):
        for way in (1, -1):
            queue, flying, landed = self.queue[way], self.flying[way], self.landed[way]
            while queue and len(flying) < (most or self.depth) and not queue[0].busy:
                flow = queue.pop(0)
                message = flow.message()
                gate = self.sent[way] - self.depth
                if gate >= 0:
                    message = after(message, landed[gate])
                if self.token is not None:
                    message = after(message, self.token)
                flow.busy = True
                self.sent[way] += 1
                self.last[way] = message
                flying.append((flow, lax.ppermute(message, "seq", self.pairs[way])))

    def hold(self, values):
        last = [message for message in self.last.values() if message is not None]
        return after(values, *last) if last else values

    def resume(self, token):
        self.token = token
        self.issue()
        return token

    def quiet(self, values):
        waiting = {w: self.queue[w] for w in (1, -1)}
        self.queue = {1: [], -1: []}
        for _ in range(self.depth):
            values = self.land(values)
        self.queue = waiting
        return values

    def pause(self):
        waiting, self.queue = self.queue, {1: [], -1: []}
        return waiting

    def go(self, waiting, token):
        self.queue = waiting
        self.resume(token)

    def land(self, values=None, count=1):
        for turn in range(count):
            taken = [(w, *self.flying[w].pop(0)) for w in (1, -1) if self.flying[w]]
            arrived = [message for _, _, message in taken]
            if values is not None and taken and turn == count - 1:
                values, *arrived = lax.optimization_barrier((values, *arrived))
            for (way, flow, _), message in zip(taken, arrived):
                flow.arrive(message)
                flow.busy = False
                self.landed[way].append(message)
            self.issue()
        return values

    def drain(self):
        while self.queue[1] or self.queue[-1] or self.flying[1] or self.flying[-1]:
            self.land()


class Pieces:
    def __init__(self, own, count):
        self.value, self.count, self.busy, self.got = own, count, False, []

    def message(self):
        return self.value

    def arrive(self, message):
        self.value = message
        self.got.append(message)


class Totals:
    def __init__(self, part, slots):
        self.part, self.slots, self.count, self.busy = part, slots, len(slots), False
        self.got, self.at = None, 0

    def message(self):
        total = self.part(self.slots[self.at])
        if self.got is not None:
            total = total + self.got.astype(f32)
        self.at += 1
        return total.astype(bf16)

    def arrive(self, message):
        self.got = message


class Gather:
    def __init__(self, piece, far, n, chunk):
        half = n // 2
        self.piece, self.n, self.chunk, self.flows = piece, n, chunk, {}
        if n <= ring_most:
            self.flows = {w: Pieces(piece, half if w == far else half - 1) for w in (1, -1)}

    def slots(self):
        if not self.flows:
            pieces = lax.all_gather(self.piece, "seq")[self.chunk]
            return [pieces[k] for k in range(self.n)]
        return [self.piece, *self.flows[1].got, *self.flows[-1].got[::-1]]


class Scatter:
    def __init__(self, part, far, n, chunk):
        half = n // 2
        self.part, self.n, self.chunk, self.flows = part, n, chunk, {}
        if n <= ring_most:
            self.flows = {
                1: Totals(part, list(range(half if far == 1 else half + 1, n))),
                -1: Totals(part, list(range(half if far == -1 else half - 1, 0, -1))),
            }

    def total(self):
        if not self.flows:
            parts = jnp.stack([self.part(k).astype(bf16) for k in range(self.n)])
            parts = parts[jnp.argsort(self.chunk)]
            return lax.psum_scatter(parts, "seq", scatter_dimension=0).astype(f32)
        total = self.part(0)
        for flow in self.flows.values():
            if flow.got is not None:
                total = total + flow.got.astype(f32)
        return total


def core_swap(values):
    size = lax.axis_size("tp")
    return lax.ppermute(values, "tp", [(i, i ^ 1) for i in range(size)])


def chip_swap(values):
    size = lax.axis_size("tp")
    return lax.ppermute(values, "tp", [(i, i ^ 2) for i in range(size)])


def tp_sum(part, others=lambda v: v, chips=lambda v: v, totals=lambda v: v):
    got = core_swap(others(part(1).astype(bf16)))
    own = lax.optimization_barrier(part(0).astype(bf16))
    chip = chips((own.astype(f32) + got.astype(f32)).astype(bf16))
    far = chip_swap(chip)
    total = totals((chip.astype(f32) + far.astype(f32)).astype(bf16))
    return total, core_swap(total)


def gelu_parts(x):
    t = jnp.tanh(gelu_scale * (x + 0.044715 * x * x * x))
    value = 0.5 * x * (1.0 + t)
    slope = 0.5 * (1.0 + t) + 0.5 * x * (1.0 - t * t) * gelu_scale * (1.0 + 3 * 0.044715 * x * x)
    return value, slope


def drive_square(log_decay, decay):
    y = -2.0 * log_decay
    series = 1.0 - y * (1.0 / 9.0)
    for k in range(8, 1, -1):
        series = 1.0 - y * (1.0 / k) * series
    return jnp.where(y < 0.5, y * series, 1.0 - decay * decay)


def scan_block(a, b, rows, reverse):
    count = a.shape[0]
    by = 1
    while by < count:
        turn = count - by if reverse else by
        pa = pltpu.roll(a, turn, 0)
        pb = pltpu.roll(b, turn, 0)
        inside = rows < count - by if reverse else rows >= by
        b = jnp.where(inside, a * pb + b, b)
        a = jnp.where(inside, a * pa, a)
        by *= 2
    return a, b


def forward_kernel(
    inner, before, conv_w, conv_b, gate_m, gate_b, rate,
    mixed, recur, admit, decay, root, cum, local, ends, ext, gates,
):
    length, lanes = inner.shape
    ext[:pad_rows] = before[...]
    ext[pad_rows:] = inner[...].astype(f32)
    taps = conv_w.shape[0]
    total = jnp.broadcast_to(conv_b[...], (length, lanes))
    for lag in range(taps):
        total = total + conv_w[lag : lag + 1] * ext[pad_rows - lag : pad_rows - lag + length]
    mixed[...] = total
    low = total.astype(bf16)
    for k in range(2):
        gates[k] = jnp.dot(low, gate_m[k], preferred_element_type=f32) + gate_b[k : k + 1]
    rows = lax.broadcasted_iota(jnp.int32, (step_rows, lanes), 0)

    def step(i, carry):
        at = pl.ds(pl.multiple_of(i * step_rows, step_rows), step_rows)
        r = jax.nn.sigmoid(gates[0, at])
        g = jax.nn.sigmoid(gates[1, at])
        log_decay = -8.0 * r * rate[...]
        d = jnp.exp(log_decay)
        m = jnp.sqrt(drive_square(log_decay, d))
        drive = m * g * mixed[at]
        root[at] = m
        recur[at] = r
        admit[at] = g
        decay[at] = d
        a, b = scan_block(d, drive, rows, False)
        b = b + a * carry[1]
        a = a * carry[0]
        cum[at] = a
        local[at] = b
        return a[step_rows - 1 :], b[step_rows - 1 :]

    a, b = lax.fori_loop(
        0, length // step_rows, step, (jnp.ones((1, lanes), f32), jnp.zeros((1, lanes), f32))
    )
    ends[0:1] = a
    ends[1:2] = b
    ends[2:] = jnp.zeros((pad_rows - 2, lanes), f32)


def reverse_kernel(grad_product, act, decay, tail, grad, first, nexts):
    length, lanes = act.shape
    nexts[...] = pltpu.roll(decay[...], length - 1, 0)
    nexts[length - 1 :] = jnp.ones((1, lanes), f32)
    rows = lax.broadcasted_iota(jnp.int32, (step_rows, lanes), 0)
    steps = length // step_rows

    def step(i, carry):
        at = pl.ds(pl.multiple_of((steps - 1 - i) * step_rows, step_rows), step_rows)
        direct = grad_product[at] * act[at]
        a, b = scan_block(nexts[at], direct, rows, True)
        b = b + a * carry[1]
        a = a * carry[0]
        tail[at] = a
        grad[at] = b
        return a[:1], b[:1]

    a, b = lax.fori_loop(0, steps, step, (jnp.ones((1, lanes), f32), jnp.zeros((1, lanes), f32)))
    first[0:1] = decay[0:1] * a
    first[1:2] = decay[0:1] * b
    first[2:] = jnp.zeros((pad_rows - 2, lanes), f32)


def gates_back_kernel(
    grad_product, slope, tail, grad, incoming, states, entry, recur, admit, decay, root, mixed, inner, before,
    gate_m, rate, conv_w, grad_gates, grad_inner, grad_gate_in, head, last, sums, grad_mix, grad_ext, ext,
):
    length, lanes = inner.shape
    enter = entry[0:1]
    later = incoming[0:1]
    taps = conv_w.shape[0]

    def step(i, carry):
        at = pl.ds(pl.multiple_of(i * step_rows, step_rows), step_rows)
        state = states[at]
        rows = lax.broadcasted_iota(jnp.int32, (step_rows, lanes), 0)
        earlier = jnp.where(rows == 0, carry[3], pltpu.roll(state, 1, 0))
        grad_gate_in[at] = (slope[at] * (grad_product[at] * state)).astype(bf16)
        total = grad[at] + tail[at] * later
        r, g, d, m, mix = recur[at], admit[at], decay[at], root[at], mixed[at]
        grad_mix[at] = total * m * g
        both = total * mix
        gate1 = both * m * g * (1.0 - g)
        grad_log = total * earlier * d - both * g * d * d / m
        gate0 = -8.0 * rate[...] * grad_log * r * (1.0 - r)
        low0 = gate0.astype(bf16)
        low1 = gate1.astype(bf16)
        grad_gates[0, at] = low0
        grad_gates[1, at] = low1
        return (
            carry[0] - 8.0 * (grad_log * r),
            carry[1] + low0.astype(f32),
            carry[2] + low1.astype(f32),
            state[step_rows - 1 :],
        )

    zero = jnp.zeros((step_rows, lanes), f32)
    totals = lax.fori_loop(0, length // step_rows, step, (zero, zero, zero, enter))
    back = grad_mix[...]
    for k in range(2):
        back = back + lax.dot_general(
            grad_gates[k], gate_m[k], (((1,), (1,)), ((), ())), preferred_element_type=f32
        )
    back = back.astype(bf16).astype(f32)
    head[...] = back[:pad_rows]
    grad_ext[:length] = back
    grad_ext[length:] = jnp.zeros((pad_rows, lanes), f32)
    ext[:pad_rows] = before[...]
    ext[pad_rows:] = inner[...].astype(f32)

    @pl.when(pl.program_id(0) == 0)
    def _():
        sums[...] = jnp.zeros_like(sums)

    for k in range(3):
        sums[k : k + 1] += jnp.sum(totals[k], axis=0, keepdims=True)
    sums[3:4] += jnp.sum(back, axis=0, keepdims=True)
    total = jnp.zeros((length, lanes), f32)
    for lag in range(taps):
        total = total + conv_w[lag : lag + 1] * grad_ext[lag : lag + length]
        term = back * ext[pad_rows - lag : pad_rows - lag + length]
        sums[4 + lag : 5 + lag] += jnp.sum(term, axis=0, keepdims=True)
    grad_inner[...] = total.astype(bf16)
    last[...] = total[length - pad_rows :]


def hidden_back_kernel(cot, w_down, act, slope, grad_both):
    units = w_down.shape[0]
    cut = math.gcd(units, 512)
    for j in range(0, units, cut):
        grad = lax.dot_general(
            cot[...], w_down[j : j + cut], (((1,), (1,)), ((), ())), preferred_element_type=f32
        )
        grad_both[:, j : j + cut] = (grad * slope[:, j : j + cut].astype(f32)).astype(bf16)
        grad_both[:, units + j : units + j + cut] = (
            grad * act[:, j : j + cut].astype(f32)
        ).astype(bf16)


def per_sequence(kernel, seqs, inputs, outputs, scratch, flops):
    def spec(shape, kind):
        if kind == "whole":
            return pl.BlockSpec(shape, lambda s: (0,) * len(shape))
        if kind == "pair":
            return pl.BlockSpec((shape[0], None) + shape[2:], lambda s: (0, s, 0, 0))
        return pl.BlockSpec((None,) + shape[1:], lambda s: (s,) + (0,) * (len(shape) - 1))

    moved = sum(a.size * a.dtype.itemsize for a, _ in inputs)
    moved += sum(math.prod(shape) * jnp.dtype(t).itemsize for shape, t, _ in outputs)
    return pl.pallas_call(
        kernel,
        grid=(seqs,),
        in_specs=[spec(a.shape, kind) for a, kind in inputs],
        out_specs=[spec(shape, kind) for shape, _, kind in outputs],
        out_shape=[jax.ShapeDtypeStruct(shape, t) for shape, t, _ in outputs],
        scratch_shapes=scratch,
        compiler_params=pltpu.CompilerParams(vmem_limit_bytes=vmem_bytes),
        cost_estimate=pl.CostEstimate(flops=flops, bytes_accessed=moved, transcendentals=0),
    )(*[a for a, _ in inputs])


def moved_bytes(*arrays):
    return sum(math.prod(a.shape) * jnp.dtype(a.dtype).itemsize for a in arrays)


def by_rows(
    kernel, arrays, whole, outputs, sums, order=None, back=False, moved=(), half=None, earlier=()
):
    seqs, length, width = arrays[0].shape
    block = min(norm_rows, length)
    count = seqs if half is None else seqs // 2
    skip = count * (half or 0)
    moves = order is not None
    tile = (None, block, width)
    near = pl.BlockSpec(tile, lambda s, r, *_: (s + skip, r, 0))
    own = pl.BlockSpec(tile, lambda s, r, *_: (s, r, 0))
    far = pl.BlockSpec(tile, lambda s, r, sequence, chunk: (sequence[s + skip], r, 0))
    total = pl.BlockSpec((pad_rows, width), lambda s, r, *_: (0, 0))
    out_shape = [jax.ShapeDtypeStruct((seqs, length, width), t) for t in outputs]
    out_shape += [jax.ShapeDtypeStruct((pad_rows, width), f32)] * sums
    scalars = 2 if moves else 0
    given = scalars + len(arrays) + len(whole)

    def body(*refs):
        kernel(*refs[:given], *refs[given + len(earlier) :])

    return pl.pallas_call(
        body,
        grid_spec=pltpu.PrefetchScalarGridSpec(
            num_scalar_prefetch=scalars,
            grid=(count, length // block),
            in_specs=[
                own
                if a.shape[0] != seqs
                else far
                if moves and (not back or i in moved)
                else near
                for i, a in enumerate(arrays)
            ]
            + [pl.BlockSpec(w.shape, lambda s, r, *_: (0, 0)) for w in whole]
            + [pl.BlockSpec(memory_space=pl.ANY)] * len(earlier),
            out_specs=[far if moves and back else near] * len(outputs) + [total] * sums,
        ),
        out_shape=out_shape,
        input_output_aliases={given + i: i for i in range(len(earlier))},
        compiler_params=pltpu.CompilerParams(vmem_limit_bytes=vmem_bytes),
        cost_estimate=pl.CostEstimate(
            flops=8 * count * length * width,
            bytes_accessed=moved_bytes(*arrays, *out_shape) * count // seqs,
            transcendentals=0,
        ),
    )(*(order if moves else ()), *arrays, *whole, *earlier)


def in_halves(kernel, arrays, summed, whole, outputs, sums, order=None, back=False):
    ready = by_rows(
        kernel, [arrays[0], summed[0], *arrays[1:]], whole, outputs, sums, order, back, (), 0
    )
    count = len(outputs)
    done = by_rows(
        kernel,
        [arrays[0], summed[1], *arrays[1:]],
        whole,
        outputs,
        sums,
        order,
        back,
        (),
        1,
        tuple(ready[:count]),
    )
    return [*done[:count], *(a + b for a, b in zip(ready[count:], done[count:]))]


def enter_kernel(sequence, chunk, *refs):
    count = len(refs) // 2
    part = refs[0].shape[1] // chunk.shape[0]
    for k in range(chunk.shape[0]):
        at = pl.ds(pl.multiple_of(chunk[k] * part, part), part)
        for i in range(count):
            refs[count + i][:, k * part : (k + 1) * part] = refs[i][:, at]


def norm_kernel(x, added, gain, middle, normed):
    total = x[...].astype(f32) + added[...].astype(f32)
    middle[...] = total
    inverse = lax.rsqrt(jnp.mean(total * total, axis=-1, keepdims=True) + eps)
    normed[...] = (total * inverse * gain[...]).astype(bf16)


def norm_back(values, grad, gain):
    inverse = lax.rsqrt(jnp.mean(values * values, axis=-1, keepdims=True) + eps)
    scaled = values * inverse
    weighted = grad * gain
    inner = jnp.mean(weighted * scaled, axis=-1, keepdims=True)
    return inverse * (weighted - scaled * inner), grad * scaled


def add_rows(total, values):
    @pl.when((pl.program_id(0) == 0) & (pl.program_id(1) == 0))
    def _():
        total[...] = jnp.zeros_like(total)

    rows, width = values.shape
    total[...] += jnp.sum(values.reshape(rows // pad_rows, pad_rows, width), axis=0)


def middle_back_kernel(middle, grad_normed, cot, gain, grad_middle, grad_low, total):
    grad, terms = norm_back(middle[...], grad_normed[...].astype(f32), gain[...])
    grad = grad + cot[...].astype(f32)
    grad_middle[...] = grad
    grad_low[...] = grad.astype(bf16)
    add_rows(total, terms)


def put_chunks(chunk, target, values):
    part = values.shape[1] // chunk.shape[0]
    for k in range(chunk.shape[0]):
        at = pl.ds(pl.multiple_of(chunk[k] * part, part), part)
        target[:, at] = values[:, k * part : (k + 1) * part]


def start_back_kernel(sequence, chunk, x, grad_normed, grad_middle, gain, grad_tokens):
    grad = norm_back(x[...].astype(f32), grad_normed[...].astype(f32), gain[...])[0]
    put_chunks(chunk, grad_tokens, grad + grad_middle[...])


def output_kernel(sequence, chunk, middle, added, output):
    put_chunks(chunk, output, (middle[...] + added[...].astype(f32)).astype(bf16))


def own_order(array, order, back=False):
    sequence, chunk = order
    if back:
        sequence, chunk = jnp.argsort(sequence), jnp.argsort(chunk)
    seqs, length, width = array.shape
    chunks = chunk.shape[0]
    split = array[sequence].reshape(seqs, length, chunks, width // chunks)
    return split[:, :, chunk].reshape(array.shape)


def carried(ends, way, n, between=lambda v: v):
    def shifted(values, by):
        pairs = [(i, i + way * by) for i in range(n) if 0 <= i + way * by < n]
        return lax.ppermute(values, "seq", pairs)

    ends = ends[:, :2]
    by = 1
    while 2 * by < n:
        earlier = shifted(ends, by)
        ends = ends[:, :1] * earlier + jnp.concatenate(
            [jnp.zeros_like(ends[:, 1:]), ends[:, 1:]], axis=1
        )
        by *= 2
        if by == 2:
            ends = between(ends)
    near, far = shifted(ends, 1), shifted(ends, 1 + by)
    state = near[:, :1] * far[:, 1:] + near[:, 1:]
    return jnp.pad(state, ((0, 0), (0, pad_rows - 1), (0, 0)))


def seq_sum(values, n):
    by = 1
    while by < n:
        values = values + lax.ppermute(values, "seq", [(i, i ^ by) for i in range(n)])
        by *= 2
    return values


def dense_heads(matrix):
    kinds, heads, width, _ = matrix.shape
    rows = [
        jnp.pad(matrix[:, h], ((0, 0), (0, 0), (h * width, (heads - 1 - h) * width)))
        for h in range(heads)
    ]
    return jnp.concatenate(rows, axis=1)


def across(a, b):
    return lax.dot_general(a, b, (((1,), (1,)), ((), ())), preferred_element_type=f32)


def down(a, b):
    return lax.dot_general(a, b, (((0,), (0,)), ((), ())), preferred_element_type=f32)


def dot(a, b):
    return jnp.dot(a, b, preferred_element_type=f32)


def shards(
    tokens,
    norm1_gain,
    in_weight,
    conv_weight,
    conv_bias,
    gate_matrix,
    gate_bias,
    decay_rate,
    out_weight,
    norm2_gain,
    mlp_weight,
    down_weight,
    cotangent,
):
    seqs, piece, width = tokens.shape
    rows = seqs * piece
    lanes = in_weight.shape[2]
    units = mlp_weight.shape[2]
    heads, head_width = gate_matrix.shape[1:3]
    taps = conv_weight.shape[0]
    n = lax.axis_size("seq")
    part = width // n
    order = ring_order(n)
    place = [order.index(i) for i in range(n)]
    me = jnp.asarray(place, jnp.int32)[lax.axis_index("seq")]
    chunk = jnp.asarray(order, jnp.int32)[(me - jnp.arange(n, dtype=jnp.int32)) % n]
    odd = lax.axis_index("tp") % 2
    sequence = (jnp.arange(seqs, dtype=jnp.int32) + odd * (seqs // 2)) % seqs
    move = (sequence, chunk)
    ring = Ring(order, lane_depth)
    tiled = part % 128 == 0

    def sl(a, k):
        return a[:, k * part : (k + 1) * part]

    move = (sequence, chunk)
    w_in = jnp.transpose(in_weight, (1, 2, 0))
    half_lanes = lanes // 2
    own_gain = jnp.pad(jnp.stack([norm1_gain, norm2_gain]), ((0, 14), (0, 0)))
    first = Gather(jnp.concatenate([w_in[0], out_weight[:half_lanes]], axis=0), 1, n, chunk)
    second = Gather(
        jnp.concatenate([w_in[1], out_weight[half_lanes:], own_gain], axis=0), -1, n, chunk
    )
    mlp = [Gather(mlp_weight[:, 0], 1, n, chunk), Gather(mlp_weight[:, 1], -1, n, chunk)]
    downs = Gather(down_weight, 1, n, chunk)
    ring.add([first, second])
    ring.add([*mlp, downs], [0, 0, 2])
    ring.issue()

    tokens, cotangent = ring.land((tokens, cotangent))
    if tiled:
        x, cot = by_rows(enter_kernel, [tokens, cotangent], [], [bf16, bf16], 0, move)
    else:
        x, cot = own_order(tokens, move), own_order(cotangent, move)
    full = x.shape
    part_full = (seqs // 2, piece, width)
    x, cot = ring.land((x, cot))
    grad_low = cot.reshape(rows, width)
    start = x.reshape(rows, width).astype(f32)
    inverse1 = lax.rsqrt(jnp.mean(start * start, axis=-1, keepdims=True) + eps)
    for _ in range(n - 3):
        ring.land()
    first, second = first.slots(), second.slots()
    in0 = [p[:lanes] for p in first]
    in1 = [p[:lanes] for p in second]
    gains = [p[lanes + half_lanes : lanes + half_lanes + 2] for p in second]
    gain1, gain2 = (
        jnp.concatenate([g[i : i + 1] for g in gains], axis=1).astype(f32) for i in range(2)
    )
    normed1 = [
        (sl(start, k) * inverse1 * gains[k][:1].astype(f32)).astype(bf16) for k in range(n)
    ]
    inner = sum(across(normed1[k], in0[k]) for k in range(n)).astype(bf16)
    gate_in = sum(across(normed1[k], in1[k]) for k in range(n)).astype(bf16)
    inner = ring.land(inner)
    inner = inner.reshape(seqs, piece, lanes)
    gate_in = gate_in.reshape(seqs, piece, lanes)
    before = lax.ppermute(
        inner[:, piece - taps + 1 :], "seq", [(i, i + 1) for i in range(n - 1)]
    ).astype(f32)
    before = ring.land(jnp.pad(before, ((0, 0), (pad_rows - taps + 1, 0), (0, 0))))
    conv_w = conv_weight.astype(f32)
    rate = decay_rate.astype(f32)[None]
    gate_m = dense_heads(gate_matrix)
    wide = (seqs, piece, lanes)
    edge = (seqs, pad_rows, lanes)
    gate_flops = 4 * rows * lanes * lanes
    mixed, recur, admit, decay, root, cum, local, ends = per_sequence(
        forward_kernel,
        seqs,
        [
            (inner, "seq"),
            (before, "seq"),
            (conv_w, "whole"),
            (conv_bias.astype(f32)[None], "whole"),
            (gate_m, "whole"),
            (gate_bias.astype(f32), "whole"),
            (rate, "whole"),
        ],
        [(wide, f32, "seq")] * 7 + [(edge, f32, "seq")],
        [pltpu.VMEM((piece + pad_rows, lanes), f32), pltpu.VMEM((2, piece, lanes), f32)],
        gate_flops,
    )
    entry = ring.land(carried(ring.land(ends), 1, n, ring.land))
    states = local + cum * entry[:, :1]
    product = (states * gelu_parts(gate_in.astype(f32))[0]).astype(bf16).reshape(rows, lanes)
    w_out = jnp.concatenate(
        [
            jnp.concatenate([p[lanes : lanes + half_lanes] for p in pieces], axis=1)
            for pieces in (first, second)
        ],
        axis=0,
    )
    block = rows // 2

    def half_of(a, h):
        return a[h * block : (h + 1) * block]

    def lands(values, count):
        for _ in range(count):
            ring.land()
        return ring.resume(values)

    chips = []

    def keep(chip):
        chips.append(ring.land(chip))
        return chips[0]

    recurrent = tp_sum(
        lambda h: dot(half_of(product, h), w_out),
        chips=keep,
        totals=lambda v: lands(v, 3),
    )
    gate_act, gate_slope = gelu_parts(after(gate_in, chips[0]).astype(f32))

    middle, normed2 = in_halves(
        norm_kernel, [x], [r.reshape(part_full) for r in recurrent], [gain2], [f32, bf16], 0
    )
    normed2 = ring.land(normed2.reshape(rows, width))
    w_mlp = jnp.concatenate([jnp.concatenate(w.slots(), axis=0) for w in mlp], axis=1)
    both = dot(normed2, w_mlp).astype(bf16)
    both0, both1 = both[:, :units].astype(f32), both[:, units:].astype(f32)
    act, slope = gelu_parts(both0)
    hidden = (act * both1).astype(bf16)
    hidden, act, slope = ring.land((hidden, act.astype(bf16), (slope * both1).astype(bf16)))
    ring.drain()
    w_down = jnp.concatenate(downs.slots(), axis=1)
    ring.token = None
    grad_both = []
    grad_down = Scatter(lambda k: down(hidden, sl(grad_low, k)), 1, n, chunk)
    grad_mlp = Scatter(lambda k: down(sl(normed2, k), grad_both[0]), -1, n, chunk)
    ring.add([grad_down, grad_mlp])
    ring.issue(1)
    act, slope, w_down = ring.hold((act, slope, w_down))
    grad_both.append(
        pl.pallas_call(
            hidden_back_kernel,
            grid=(seqs,),
            in_specs=[
                pl.BlockSpec((piece, width), lambda s: (s, 0)),
                pl.BlockSpec((units, width), lambda s: (0, 0)),
                pl.BlockSpec((piece, units), lambda s: (s, 0)),
                pl.BlockSpec((piece, units), lambda s: (s, 0)),
            ],
            out_specs=pl.BlockSpec((piece, 2 * units), lambda s: (s, 0)),
            out_shape=jax.ShapeDtypeStruct((rows, 2 * units), bf16),
            compiler_params=pltpu.CompilerParams(vmem_limit_bytes=vmem_bytes),
            cost_estimate=pl.CostEstimate(
                flops=2 * rows * width * units,
                bytes_accessed=moved_bytes(grad_low, w_down, act, slope, both),
                transcendentals=0,
            ),
        )(grad_low, w_down, act, slope)
    )
    ring.issue()
    grad_normed2 = tp_sum(
        lambda h: across(half_of(grad_both[0], h), w_mlp),
        others=ring.land,
        totals=lambda v: ring.land((ring.land(), v)[1]),
    )
    turned = jnp.concatenate([half_of(hidden, 1), half_of(hidden, 0)], axis=0)
    turned = jnp.where(odd == 1, turned, hidden)

    grad_middle, grad_rec, sum_gain2 = in_halves(
        middle_back_kernel,
        [middle, cot],
        [g.reshape(part_full) for g in grad_normed2],
        [gain2],
        [f32, bf16],
        1,
    )
    grad_out = Scatter(lambda k: down(product, sl(grad_rec, k)), 1, n, chunk)
    ring.add([grad_out])
    waiting = ring.pause()
    grad_rec = ring.land(grad_rec.reshape(rows, width))

    grad_product = across(grad_rec, w_out).reshape(wide)
    tail, local_grad, early = per_sequence(
        reverse_kernel,
        seqs,
        [(grad_product, "seq"), (gate_act, "seq"), (decay, "seq")],
        [(wide, f32, "seq")] * 2 + [(edge, f32, "seq")],
        [pltpu.VMEM((piece, lanes), f32)],
        rows * lanes * 50,
    )
    rounds = []

    def keep_round(ends):
        rounds.append(ends)
        return ends

    incoming = carried(ring.land(early), -1, n, keep_round)
    ring.go(waiting, incoming)
    mlp_out = lax.psum(dot(after(turned, *rounds), w_down).astype(bf16), "tp")
    grad_gates, grad_inner, grad_gate_in, head, last, sums = per_sequence(
        gates_back_kernel,
        seqs,
        [
            (grad_product, "seq"),
            (gate_slope, "seq"),
            (tail, "seq"),
            (local_grad, "seq"),
            (incoming, "seq"),
            (states, "seq"),
            (entry, "seq"),
            (recur, "seq"),
            (admit, "seq"),
            (decay, "seq"),
            (root, "seq"),
            (mixed, "seq"),
            (inner, "seq"),
            (before, "seq"),
            (gate_m, "whole"),
            (rate, "whole"),
            (conv_w, "whole"),
        ],
        [
            ((2,) + wide, bf16, "pair"),
            (wide, bf16, "seq"),
            (wide, bf16, "seq"),
            (edge, f32, "seq"),
            (edge, f32, "seq"),
            ((pad_rows, lanes), f32, "whole"),
        ],
        [pltpu.VMEM((piece, lanes), f32)] + [pltpu.VMEM((piece + pad_rows, lanes), f32)] * 2,
        gate_flops,
    )
    behind = lax.ppermute(
        head[:, : taps - 1].astype(bf16), "seq", [(i + 1, i) for i in range(n - 1)]
    ).astype(f32)
    beyond = jnp.concatenate([jnp.zeros_like(last), behind], axis=1)
    beyond = jnp.pad(beyond, ((0, 0), (0, 1), (0, 0)))
    for lag in range(1, taps):
        last = last + conv_w[lag] * beyond[:, lag : lag + pad_rows]
    grad_inner = lax.dynamic_update_slice(
        grad_inner, last.astype(bf16), (0, piece - pad_rows, 0)
    )
    back0 = grad_inner.reshape(rows, lanes)
    back1 = grad_gate_in.reshape(rows, lanes)
    back = ring.land(jnp.concatenate([back0, back1], axis=1))
    w_both = jnp.concatenate([jnp.concatenate(in0, axis=1), jnp.concatenate(in1, axis=1)], axis=0)
    grads = [
        Scatter(lambda k: down(back0, normed1[k]), 1, n, chunk),
        Scatter(lambda k: down(back1, normed1[k]), -1, n, chunk),
    ]
    ring.add(grads)
    ring.issue()
    late = []

    def hold_output(chip):
        late.append(after(mlp_out, chip))
        return ring.land(chip)

    grad_normed1 = tp_sum(
        lambda h: dot(half_of(back, h), w_both),
        chips=hold_output,
        totals=lambda v: lands(v, 4),
    )
    mlp_out = late[0]
    ring.drain()
    grads = [g.total() for g in grads]
    low_mixed = mixed.astype(bf16).reshape(rows, lanes)
    grad_matrix = []
    for k in range(2):
        dense = down(low_mixed, grad_gates[k].reshape(rows, lanes)).astype(bf16)
        for h in range(heads):
            at = slice(h * head_width, (h + 1) * head_width)
            grad_matrix.append(dense[at, at])
    packed = jnp.concatenate(
        grad_matrix + [sums.astype(bf16).reshape(-1, head_width)], axis=0
    )
    packed = lax.psum(packed, "seq")

    if tiled:
        output = by_rows(
            output_kernel,
            [middle, mlp_out.reshape(full)],
            [],
            [bf16],
            0,
            move,
            back=True,
            moved=(1,),
        )[0]
        grad_tokens = in_halves(
            start_back_kernel,
            [x, grad_middle],
            [g.reshape(part_full) for g in grad_normed1],
            [gain1],
            [f32],
            0,
            move,
            back=True,
        )[0]
    else:
        mlp_out = mlp_out.reshape(full)[sequence].astype(f32)
        output = own_order((middle + mlp_out).astype(bf16), move, True)
        grad_normed1_all = jnp.concatenate(grad_normed1, axis=0).reshape(full).astype(f32)
        grad_start = norm_back(x.astype(f32), grad_normed1_all, gain1)[0]
        grad_tokens = own_order(grad_middle + grad_start, move, True)
    mine = lax.axis_index("seq")
    slots = (me - jnp.asarray(place, jnp.int32)) % n
    scaled1 = start[:block] * inverse1[:block]
    sum_gain1 = jnp.sum(grad_normed1[0].astype(f32) * scaled1, axis=0)
    grad_gains = jnp.stack([sum_gain1, 0.5 * jnp.sum(sum_gain2, axis=0)])
    grad_gains = grad_gains + core_swap(grad_gains)
    grad_gains = seq_sum(grad_gains.reshape(2, n, part)[:, slots], n)
    grad_gains = lax.dynamic_index_in_dim(grad_gains, mine, 1, keepdims=False)

    packed, grad_gains = lax.optimization_barrier((packed, grad_gains))
    packed = packed.astype(f32)
    matrix_rows = 2 * heads * head_width
    grad_matrix = packed[:matrix_rows].reshape(gate_matrix.shape)
    small = packed[matrix_rows:].reshape(4 + taps, lanes)
    return (
        output,
        grad_tokens,
        grad_gains[0],
        jnp.transpose(jnp.stack(grads), (2, 0, 1)),
        small[4:],
        small[3],
        grad_matrix,
        small[1:3],
        small[0],
        grad_out.total(),
        grad_gains[1],
        grad_mlp.total().reshape(part, 2, units),
        grad_down.total(),
    )


def solution(mesh):
    in_specs = (
        P(None, "seq", None),
        P("seq"),
        P("seq", None, "tp"),
        P(None, "tp"),
        P("tp"),
        P(None, "tp", None, None),
        P(None, "tp"),
        P("tp"),
        P("tp", "seq"),
        P("seq"),
        P("seq", None, "tp"),
        P("tp", "seq"),
        P(None, "seq", None),
    )
    out_specs = (
        P(None, "seq", None),
        P(None, "seq", None),
        P("seq"),
        P("seq", None, "tp"),
        P(None, "tp"),
        P("tp"),
        P(None, "tp", None, None),
        P(None, "tp"),
        P("tp"),
        P("tp", "seq"),
        P("seq"),
        P("seq", None, "tp"),
        P("tp", "seq"),
    )
    return jax.shard_map(shards, mesh=mesh, in_specs=in_specs, out_specs=out_specs, check_vma=False)
```

```python
import functools
import math

import jax
import jax.numpy as jnp
from jax import lax
from jax.experimental import pallas as pl
from jax.experimental.pallas import tpu as pltpu
from jax.sharding import PartitionSpec as P

f32 = jnp.float32
bf16 = jnp.bfloat16
eps = 1e-06
gelu_scale = math.sqrt(2.0 / math.pi)
step_rows = 16
pad_rows = 8
vmem_bytes = 48 * 2**20
ring_most = 8
lane_depth = 2
norm_rows = 128


def ring_order(n):
    return [*range(0, n, 2), *range(n - 1 - n % 2, 0, -2)]


def after(values, *earlier):
    return lax.optimization_barrier((values, *earlier))[0]


class Ring:
    def __init__(self, order, depth):
        n = len(order)
        self.n = n
        self.depth = depth
        self.pairs = {w: [(order[i], order[(i + w) % n]) for i in range(n)] for w in (1, -1)}
        self.queue = {1: [], -1: []}
        self.flying = {1: [], -1: []}
        self.landed = {1: [], -1: []}
        self.sent = {1: 0, -1: 0}
        self.last = {1: None, -1: None}
        self.token = None

    def add(self, weights, delays=None):
        half = self.n // 2
        delays = delays or [0] * len(weights)
        left = {id(flow): flow.count for w in weights for flow in w.flows.values()}
        for turn in range(half + max(delays)):
            for late in (True, False):
                for weight, delay in zip(weights, delays):
                    if (delay > 0) != late or turn < delay:
                        continue
                    for way, flow in weight.flows.items():
                        if left[id(flow)]:
                            left[id(flow)] -= 1
                            self.queue[way].append(flow)

    def issue(self, most=None):
        for way in (1, -1):
            queue, flying, landed = self.queue[way], self.flying[way], self.landed[way]
            while queue and len(flying) < (most or self.depth) and not queue[0].busy:
                flow = queue.pop(0)
                message = flow.message()
                gate = self.sent[way] - self.depth
                if gate >= 0:
                    message = after(message, landed[gate])
                if self.token is not None:
                    message = after(message, self.token)
                flow.busy = True
                self.sent[way] += 1
                self.last[way] = message
                flying.append((flow, lax.ppermute(message, "seq", self.pairs[way])))

    def hold(self, values):
        last = [message for message in self.last.values() if message is not None]
        return after(values, *last) if last else values

    def resume(self, token):
        self.token = token
        self.issue()
        return token

    def quiet(self, values):
        waiting = {w: self.queue[w] for w in (1, -1)}
        self.queue = {1: [], -1: []}
        for _ in range(self.depth):
            values = self.land(values)
        self.queue = waiting
        return values

    def pause(self):
        waiting, self.queue = self.queue, {1: [], -1: []}
        return waiting

    def go(self, waiting, token):
        self.queue = waiting
        self.resume(token)

    def land(self, values=None, count=1):
        for turn in range(count):
            taken = [(w, *self.flying[w].pop(0)) for w in (1, -1) if self.flying[w]]
            arrived = [message for _, _, message in taken]
            if values is not None and taken and turn == count - 1:
                values, *arrived = lax.optimization_barrier((values, *arrived))
            for (way, flow, _), message in zip(taken, arrived):
                flow.arrive(message)
                flow.busy = False
                self.landed[way].append(message)
            self.issue()
        return values

    def drain(self):
        while self.queue[1] or self.queue[-1] or self.flying[1] or self.flying[-1]:
            self.land()


class Pieces:
    def __init__(self, own, count):
        self.value, self.count, self.busy, self.got = own, count, False, []

    def message(self):
        return self.value

    def arrive(self, message):
        self.value = message
        self.got.append(message)


class Totals:
    def __init__(self, part, slots):
        self.part, self.slots, self.count, self.busy = part, slots, len(slots), False
        self.got, self.at = None, 0

    def message(self):
        total = self.part(self.slots[self.at])
        if self.got is not None:
            total = total + self.got.astype(f32)
        self.at += 1
        return total.astype(bf16)

    def arrive(self, message):
        self.got = message


class Gather:
    def __init__(self, piece, far, n, chunk):
        half = n // 2
        self.piece, self.n, self.chunk, self.flows = piece, n, chunk, {}
        if n <= ring_most:
            self.flows = {w: Pieces(piece, half if w == far else half - 1) for w in (1, -1)}

    def slots(self):
        if not self.flows:
            pieces = lax.all_gather(self.piece, "seq")[self.chunk]
            return [pieces[k] for k in range(self.n)]
        return [self.piece, *self.flows[1].got, *self.flows[-1].got[::-1]]


class Scatter:
    def __init__(self, part, far, n, chunk):
        half = n // 2
        self.part, self.n, self.chunk, self.flows = part, n, chunk, {}
        if n <= ring_most:
            self.flows = {
                1: Totals(part, list(range(half if far == 1 else half + 1, n))),
                -1: Totals(part, list(range(half if far == -1 else half - 1, 0, -1))),
            }

    def total(self):
        if not self.flows:
            parts = jnp.stack([self.part(k).astype(bf16) for k in range(self.n)])
            parts = parts[jnp.argsort(self.chunk)]
            return lax.psum_scatter(parts, "seq", scatter_dimension=0).astype(f32)
        total = self.part(0)
        for flow in self.flows.values():
            if flow.got is not None:
                total = total + flow.got.astype(f32)
        return total


def core_swap(values):
    size = lax.axis_size("tp")
    return lax.ppermute(values, "tp", [(i, i ^ 1) for i in range(size)])


def chip_swap(values):
    size = lax.axis_size("tp")
    return lax.ppermute(values, "tp", [(i, i ^ 2) for i in range(size)])


def tp_sum(part, others=lambda v: v, chips=lambda v: v, totals=lambda v: v):
    got = core_swap(others(part(1).astype(bf16)))
    own = lax.optimization_barrier(part(0).astype(bf16))
    chip = chips((own.astype(f32) + got.astype(f32)).astype(bf16))
    far = chip_swap(chip)
    total = totals((chip.astype(f32) + far.astype(f32)).astype(bf16))
    return total, core_swap(total)


def gelu_parts(x):
    t = jnp.tanh(gelu_scale * (x + 0.044715 * x * x * x))
    value = 0.5 * x * (1.0 + t)
    slope = 0.5 * (1.0 + t) + 0.5 * x * (1.0 - t * t) * gelu_scale * (1.0 + 3 * 0.044715 * x * x)
    return value, slope


def drive_square(log_decay, decay):
    y = -2.0 * log_decay
    series = 1.0 - y * (1.0 / 9.0)
    for k in range(8, 1, -1):
        series = 1.0 - y * (1.0 / k) * series
    return jnp.where(y < 0.5, y * series, 1.0 - decay * decay)


def scan_block(a, b, rows, reverse):
    count = a.shape[0]
    by = 1
    while by < count:
        turn = count - by if reverse else by
        pa = pltpu.roll(a, turn, 0)
        pb = pltpu.roll(b, turn, 0)
        inside = rows < count - by if reverse else rows >= by
        b = jnp.where(inside, a * pb + b, b)
        a = jnp.where(inside, a * pa, a)
        by *= 2
    return a, b


def forward_kernel(
    inner, before, conv_w, conv_b, gate_m, gate_b, rate,
    mixed, recur, admit, decay, root, cum, local, ends, ext, gates,
):
    length, lanes = inner.shape
    ext[:pad_rows] = before[...]
    ext[pad_rows:] = inner[...].astype(f32)
    taps = conv_w.shape[0]
    total = jnp.broadcast_to(conv_b[...], (length, lanes))
    for lag in range(taps):
        total = total + conv_w[lag : lag + 1] * ext[pad_rows - lag : pad_rows - lag + length]
    mixed[...] = total
    low = total.astype(bf16)
    for k in range(2):
        gates[k] = jnp.dot(low, gate_m[k], preferred_element_type=f32) + gate_b[k : k + 1]
    rows = lax.broadcasted_iota(jnp.int32, (step_rows, lanes), 0)

    def step(i, carry):
        at = pl.ds(pl.multiple_of(i * step_rows, step_rows), step_rows)
        r = jax.nn.sigmoid(gates[0, at])
        g = jax.nn.sigmoid(gates[1, at])
        log_decay = -8.0 * r * rate[...]
        d = jnp.exp(log_decay)
        m = jnp.sqrt(drive_square(log_decay, d))
        drive = m * g * mixed[at]
        root[at] = m
        recur[at] = r
        admit[at] = g
        decay[at] = d
        a, b = scan_block(d, drive, rows, False)
        b = b + a * carry[1]
        a = a * carry[0]
        cum[at] = a
        local[at] = b
        return a[step_rows - 1 :], b[step_rows - 1 :]

    a, b = lax.fori_loop(
        0, length // step_rows, step, (jnp.ones((1, lanes), f32), jnp.zeros((1, lanes), f32))
    )
    ends[0:1] = a
    ends[1:2] = b
    ends[2:] = jnp.zeros((pad_rows - 2, lanes), f32)


def reverse_kernel(grad_product, act, decay, tail, grad, first, nexts):
    length, lanes = act.shape
    nexts[...] = pltpu.roll(decay[...], length - 1, 0)
    nexts[length - 1 :] = jnp.ones((1, lanes), f32)
    rows = lax.broadcasted_iota(jnp.int32, (step_rows, lanes), 0)
    steps = length // step_rows

    def step(i, carry):
        at = pl.ds(pl.multiple_of((steps - 1 - i) * step_rows, step_rows), step_rows)
        direct = grad_product[at] * act[at]
        a, b = scan_block(nexts[at], direct, rows, True)
        b = b + a * carry[1]
        a = a * carry[0]
        tail[at] = a
        grad[at] = b
        return a[:1], b[:1]

    a, b = lax.fori_loop(0, steps, step, (jnp.ones((1, lanes), f32), jnp.zeros((1, lanes), f32)))
    first[0:1] = decay[0:1] * a
    first[1:2] = decay[0:1] * b
    first[2:] = jnp.zeros((pad_rows - 2, lanes), f32)


def gates_back_kernel(
    grad_product, slope, tail, grad, incoming, states, entry, recur, admit, decay, root, mixed, inner, before,
    gate_m, rate, conv_w, grad_gates, grad_inner, grad_gate_in, head, last, sums, grad_mix, grad_ext, ext,
):
    length, lanes = inner.shape
    enter = entry[0:1]
    later = incoming[0:1]
    taps = conv_w.shape[0]

    def step(i, carry):
        at = pl.ds(pl.multiple_of(i * step_rows, step_rows), step_rows)
        state = states[at]
        rows = lax.broadcasted_iota(jnp.int32, (step_rows, lanes), 0)
        earlier = jnp.where(rows == 0, carry[3], pltpu.roll(state, 1, 0))
        grad_gate_in[at] = (slope[at] * (grad_product[at] * state)).astype(bf16)
        total = grad[at] + tail[at] * later
        r, g, d, m, mix = recur[at], admit[at], decay[at], root[at], mixed[at]
        grad_mix[at] = total * m * g
        both = total * mix
        gate1 = both * m * g * (1.0 - g)
        grad_log = total * earlier * d - both * g * d * d / m
        gate0 = -8.0 * rate[...] * grad_log * r * (1.0 - r)
        low0 = gate0.astype(bf16)
        low1 = gate1.astype(bf16)
        grad_gates[0, at] = low0
        grad_gates[1, at] = low1
        return (
            carry[0] - 8.0 * (grad_log * r),
            carry[1] + low0.astype(f32),
            carry[2] + low1.astype(f32),
            state[step_rows - 1 :],
        )

    zero = jnp.zeros((step_rows, lanes), f32)
    totals = lax.fori_loop(0, length // step_rows, step, (zero, zero, zero, enter))
    back = grad_mix[...]
    for k in range(2):
        back = back + lax.dot_general(
            grad_gates[k], gate_m[k], (((1,), (1,)), ((), ())), preferred_element_type=f32
        )
    back = back.astype(bf16).astype(f32)
    head[...] = back[:pad_rows]
    grad_ext[:length] = back
    grad_ext[length:] = jnp.zeros((pad_rows, lanes), f32)
    ext[:pad_rows] = before[...]
    ext[pad_rows:] = inner[...].astype(f32)

    @pl.when(pl.program_id(0) == 0)
    def _():
        sums[...] = jnp.zeros_like(sums)

    for k in range(3):
        sums[k : k + 1] += jnp.sum(totals[k], axis=0, keepdims=True)
    sums[3:4] += jnp.sum(back, axis=0, keepdims=True)
    total = jnp.zeros((length, lanes), f32)
    for lag in range(taps):
        total = total + conv_w[lag : lag + 1] * grad_ext[lag : lag + length]
        term = back * ext[pad_rows - lag : pad_rows - lag + length]
        sums[4 + lag : 5 + lag] += jnp.sum(term, axis=0, keepdims=True)
    grad_inner[...] = total.astype(bf16)
    last[...] = total[length - pad_rows :]


def hidden_back_kernel(cot, w_down, act, slope, grad_both):
    units = w_down.shape[0]
    cut = math.gcd(units, 512)
    for j in range(0, units, cut):
        grad = lax.dot_general(
            cot[...], w_down[j : j + cut], (((1,), (1,)), ((), ())), preferred_element_type=f32
        )
        grad_both[:, j : j + cut] = (grad * slope[:, j : j + cut].astype(f32)).astype(bf16)
        grad_both[:, units + j : units + j + cut] = (
            grad * act[:, j : j + cut].astype(f32)
        ).astype(bf16)


def per_sequence(kernel, seqs, inputs, outputs, scratch, flops):
    def spec(shape, kind):
        if kind == "whole":
            return pl.BlockSpec(shape, lambda s: (0,) * len(shape))
        if kind == "pair":
            return pl.BlockSpec((shape[0], None) + shape[2:], lambda s: (0, s, 0, 0))
        return pl.BlockSpec((None,) + shape[1:], lambda s: (s,) + (0,) * (len(shape) - 1))

    moved = sum(a.size * a.dtype.itemsize for a, _ in inputs)
    moved += sum(math.prod(shape) * jnp.dtype(t).itemsize for shape, t, _ in outputs)
    return pl.pallas_call(
        kernel,
        grid=(seqs,),
        in_specs=[spec(a.shape, kind) for a, kind in inputs],
        out_specs=[spec(shape, kind) for shape, _, kind in outputs],
        out_shape=[jax.ShapeDtypeStruct(shape, t) for shape, t, _ in outputs],
        scratch_shapes=scratch,
        compiler_params=pltpu.CompilerParams(vmem_limit_bytes=vmem_bytes),
        cost_estimate=pl.CostEstimate(flops=flops, bytes_accessed=moved, transcendentals=0),
    )(*[a for a, _ in inputs])


def moved_bytes(*arrays):
    return sum(math.prod(a.shape) * jnp.dtype(a.dtype).itemsize for a in arrays)


def by_rows(
    kernel, arrays, whole, outputs, sums, order=None, back=False, moved=(), half=None, earlier=()
):
    seqs, length, width = arrays[0].shape
    block = min(norm_rows, length)
    count = seqs if half is None else seqs // 2
    skip = count * (half or 0)
    moves = order is not None
    tile = (None, block, width)
    near = pl.BlockSpec(tile, lambda s, r, *_: (s + skip, r, 0))
    own = pl.BlockSpec(tile, lambda s, r, *_: (s, r, 0))
    far = pl.BlockSpec(tile, lambda s, r, sequence, chunk: (sequence[s + skip], r, 0))
    total = pl.BlockSpec((pad_rows, width), lambda s, r, *_: (0, 0))
    out_shape = [jax.ShapeDtypeStruct((seqs, length, width), t) for t in outputs]
    out_shape += [jax.ShapeDtypeStruct((pad_rows, width), f32)] * sums
    scalars = 2 if moves else 0
    given = scalars + len(arrays) + len(whole)

    def body(*refs):
        kernel(*refs[:given], *refs[given + len(earlier) :])

    return pl.pallas_call(
        body,
        grid_spec=pltpu.PrefetchScalarGridSpec(
            num_scalar_prefetch=scalars,
            grid=(count, length // block),
            in_specs=[
                own
                if a.shape[0] != seqs
                else far
                if moves and (not back or i in moved)
                else near
                for i, a in enumerate(arrays)
            ]
            + [pl.BlockSpec(w.shape, lambda s, r, *_: (0, 0)) for w in whole]
            + [pl.BlockSpec(memory_space=pl.ANY)] * len(earlier),
            out_specs=[far if moves and back else near] * len(outputs) + [total] * sums,
        ),
        out_shape=out_shape,
        input_output_aliases={given + i: i for i in range(len(earlier))},
        compiler_params=pltpu.CompilerParams(vmem_limit_bytes=vmem_bytes),
        cost_estimate=pl.CostEstimate(
            flops=8 * count * length * width,
            bytes_accessed=moved_bytes(*arrays, *out_shape) * count // seqs,
            transcendentals=0,
        ),
    )(*(order if moves else ()), *arrays, *whole, *earlier)


def in_halves(kernel, arrays, summed, whole, outputs, sums, order=None, back=False):
    ready = by_rows(
        kernel, [arrays[0], summed[0], *arrays[1:]], whole, outputs, sums, order, back, (), 0
    )
    count = len(outputs)
    done = by_rows(
        kernel,
        [arrays[0], summed[1], *arrays[1:]],
        whole,
        outputs,
        sums,
        order,
        back,
        (),
        1,
        tuple(ready[:count]),
    )
    return [*done[:count], *(a + b for a, b in zip(ready[count:], done[count:]))]


def enter_kernel(sequence, chunk, *refs):
    count = len(refs) // 2
    part = refs[0].shape[1] // chunk.shape[0]
    for k in range(chunk.shape[0]):
        at = pl.ds(pl.multiple_of(chunk[k] * part, part), part)
        for i in range(count):
            refs[count + i][:, k * part : (k + 1) * part] = refs[i][:, at]


def norm_kernel(x, added, gain, middle, normed):
    total = x[...].astype(f32) + added[...].astype(f32)
    middle[...] = total
    inverse = lax.rsqrt(jnp.mean(total * total, axis=-1, keepdims=True) + eps)
    normed[...] = (total * inverse * gain[...]).astype(bf16)


def norm_back(values, grad, gain):
    inverse = lax.rsqrt(jnp.mean(values * values, axis=-1, keepdims=True) + eps)
    scaled = values * inverse
    weighted = grad * gain
    inner = jnp.mean(weighted * scaled, axis=-1, keepdims=True)
    return inverse * (weighted - scaled * inner), grad * scaled


def add_rows(total, values):
    @pl.when((pl.program_id(0) == 0) & (pl.program_id(1) == 0))
    def _():
        total[...] = jnp.zeros_like(total)

    rows, width = values.shape
    total[...] += jnp.sum(values.reshape(rows // pad_rows, pad_rows, width), axis=0)


def middle_back_kernel(middle, grad_normed, cot, gain, grad_middle, grad_low, total):
    grad, terms = norm_back(middle[...], grad_normed[...].astype(f32), gain[...])
    grad = grad + cot[...].astype(f32)
    grad_middle[...] = grad
    grad_low[...] = grad.astype(bf16)
    add_rows(total, terms)


def put_chunks(chunk, target, values):
    part = values.shape[1] // chunk.shape[0]
    for k in range(chunk.shape[0]):
        at = pl.ds(pl.multiple_of(chunk[k] * part, part), part)
        target[:, at] = values[:, k * part : (k + 1) * part]


def start_back_kernel(sequence, chunk, x, grad_normed, grad_middle, gain, grad_tokens):
    grad = norm_back(x[...].astype(f32), grad_normed[...].astype(f32), gain[...])[0]
    put_chunks(chunk, grad_tokens, grad + grad_middle[...])


def output_kernel(sequence, chunk, middle, added, output):
    put_chunks(chunk, output, (middle[...] + added[...].astype(f32)).astype(bf16))


def own_order(array, order, back=False):
    sequence, chunk = order
    if back:
        sequence, chunk = jnp.argsort(sequence), jnp.argsort(chunk)
    seqs, length, width = array.shape
    chunks = chunk.shape[0]
    split = array[sequence].reshape(seqs, length, chunks, width // chunks)
    return split[:, :, chunk].reshape(array.shape)


def carried(ends, way, n, between=lambda v: v):
    def shifted(values, by):
        pairs = [(i, i + way * by) for i in range(n) if 0 <= i + way * by < n]
        return lax.ppermute(values, "seq", pairs)

    ends = ends[:, :2]
    by = 1
    while 2 * by < n:
        earlier = shifted(ends, by)
        ends = ends[:, :1] * earlier + jnp.concatenate(
            [jnp.zeros_like(ends[:, 1:]), ends[:, 1:]], axis=1
        )
        by *= 2
        if by == 2:
            ends = between(ends)
    near, far = shifted(ends, 1), shifted(ends, 1 + by)
    state = near[:, :1] * far[:, 1:] + near[:, 1:]
    return jnp.pad(state, ((0, 0), (0, pad_rows - 1), (0, 0)))


def seq_sum(values, n):
    by = 1
    while by < n:
        values = values + lax.ppermute(values, "seq", [(i, i ^ by) for i in range(n)])
        by *= 2
    return values


def dense_heads(matrix):
    kinds, heads, width, _ = matrix.shape
    rows = [
        jnp.pad(matrix[:, h], ((0, 0), (0, 0), (h * width, (heads - 1 - h) * width)))
        for h in range(heads)
    ]
    return jnp.concatenate(rows, axis=1)


def across(a, b):
    return lax.dot_general(a, b, (((1,), (1,)), ((), ())), preferred_element_type=f32)


def down(a, b):
    return lax.dot_general(a, b, (((0,), (0,)), ((), ())), preferred_element_type=f32)


def dot(a, b):
    return jnp.dot(a, b, preferred_element_type=f32)


def shards(
    tokens,
    norm1_gain,
    in_weight,
    conv_weight,
    conv_bias,
    gate_matrix,
    gate_bias,
    decay_rate,
    out_weight,
    norm2_gain,
    mlp_weight,
    down_weight,
    cotangent,
):
    seqs, piece, width = tokens.shape
    rows = seqs * piece
    lanes = in_weight.shape[2]
    units = mlp_weight.shape[2]
    heads, head_width = gate_matrix.shape[1:3]
    taps = conv_weight.shape[0]
    n = lax.axis_size("seq")
    part = width // n
    order = ring_order(n)
    place = [order.index(i) for i in range(n)]
    me = jnp.asarray(place, jnp.int32)[lax.axis_index("seq")]
    chunk = jnp.asarray(order, jnp.int32)[(me - jnp.arange(n, dtype=jnp.int32)) % n]
    odd = lax.axis_index("tp") % 2
    sequence = (jnp.arange(seqs, dtype=jnp.int32) + odd * (seqs // 2)) % seqs
    move = (sequence, chunk)
    ring = Ring(order, lane_depth)
    tiled = part % 128 == 0

    def sl(a, k):
        return a[:, k * part : (k + 1) * part]

    move = (sequence, chunk)
    w_in = jnp.transpose(in_weight, (1, 2, 0))
    half_lanes = lanes // 2
    own_gain = jnp.pad(jnp.stack([norm1_gain, norm2_gain]), ((0, 14), (0, 0)))
    first = Gather(jnp.concatenate([w_in[0], out_weight[:half_lanes]], axis=0), 1, n, chunk)
    second = Gather(
        jnp.concatenate([w_in[1], out_weight[half_lanes:], own_gain], axis=0), -1, n, chunk
    )
    mlp = [Gather(mlp_weight[:, 0], 1, n, chunk), Gather(mlp_weight[:, 1], -1, n, chunk)]
    downs = Gather(down_weight, 1, n, chunk)
    ring.add([first, second])
    ring.add([*mlp, downs], [0, 0, 2])
    ring.issue()

    tokens, cotangent = ring.land((tokens, cotangent))
    if tiled:
        x, cot = by_rows(enter_kernel, [tokens, cotangent], [], [bf16, bf16], 0, move)
    else:
        x, cot = own_order(tokens, move), own_order(cotangent, move)
    full = x.shape
    part_full = (seqs // 2, piece, width)
    x, cot = ring.land((x, cot))
    grad_low = cot.reshape(rows, width)
    start = x.reshape(rows, width).astype(f32)
    inverse1 = lax.rsqrt(jnp.mean(start * start, axis=-1, keepdims=True) + eps)
    for _ in range(n - 3):
        ring.land()
    first, second = first.slots(), second.slots()
    in0 = [p[:lanes] for p in first]
    in1 = [p[:lanes] for p in second]
    gains = [p[lanes + half_lanes : lanes + half_lanes + 2] for p in second]
    gain1, gain2 = (
        jnp.concatenate([g[i : i + 1] for g in gains], axis=1).astype(f32) for i in range(2)
    )
    normed1 = [
        (sl(start, k) * inverse1 * gains[k][:1].astype(f32)).astype(bf16) for k in range(n)
    ]
    inner = sum(across(normed1[k], in0[k]) for k in range(n)).astype(bf16)
    gate_in = sum(across(normed1[k], in1[k]) for k in range(n)).astype(bf16)
    inner = inner.reshape(seqs, piece, lanes)
    gate_in = gate_in.reshape(seqs, piece, lanes)
    before = lax.ppermute(
        inner[:, piece - taps + 1 :], "seq", [(i, i + 1) for i in range(n - 1)]
    ).astype(f32)
    before = jnp.pad(before, ((0, 0), (pad_rows - taps + 1, 0), (0, 0)))
    before, inner = ring.land((before, inner), 2)
    conv_w = conv_weight.astype(f32)
    rate = decay_rate.astype(f32)[None]
    gate_m = dense_heads(gate_matrix)
    wide = (seqs, piece, lanes)
    edge = (seqs, pad_rows, lanes)
    gate_flops = 4 * rows * lanes * lanes
    mixed, recur, admit, decay, root, cum, local, ends = per_sequence(
        forward_kernel,
        seqs,
        [
            (inner, "seq"),
            (before, "seq"),
            (conv_w, "whole"),
            (conv_bias.astype(f32)[None], "whole"),
            (gate_m, "whole"),
            (gate_bias.astype(f32), "whole"),
            (rate, "whole"),
        ],
        [(wide, f32, "seq")] * 7 + [(edge, f32, "seq")],
        [pltpu.VMEM((piece + pad_rows, lanes), f32), pltpu.VMEM((2, piece, lanes), f32)],
        gate_flops,
    )
    entry = ring.land(carried(ring.land(ends), 1, n, ring.land))
    states = local + cum * entry[:, :1]
    product = (states * gelu_parts(gate_in.astype(f32))[0]).astype(bf16).reshape(rows, lanes)
    w_out = jnp.concatenate(
        [
            jnp.concatenate([p[lanes : lanes + half_lanes] for p in pieces], axis=1)
            for pieces in (first, second)
        ],
        axis=0,
    )
    block = rows // 2

    def half_of(a, h):
        return a[h * block : (h + 1) * block]

    def lands(values, count):
        for _ in range(count):
            ring.land()
        return ring.resume(values)

    chips = []

    def keep(chip):
        chips.append(ring.land(chip))
        return chips[0]

    recurrent = tp_sum(
        lambda h: dot(half_of(product, h), w_out),
        chips=keep,
        totals=lambda v: lands(v, 3),
    )
    gate_act, gate_slope = gelu_parts(after(gate_in, chips[0]).astype(f32))

    middle, normed2 = in_halves(
        norm_kernel, [x], [r.reshape(part_full) for r in recurrent], [gain2], [f32, bf16], 0
    )
    normed2 = ring.land(normed2.reshape(rows, width))
    w_mlp = jnp.concatenate([jnp.concatenate(w.slots(), axis=0) for w in mlp], axis=1)
    both = dot(normed2, w_mlp).astype(bf16)
    both0, both1 = both[:, :units].astype(f32), both[:, units:].astype(f32)
    act, slope = gelu_parts(both0)
    hidden = (act * both1).astype(bf16)
    hidden, act, slope = ring.land((hidden, act.astype(bf16), (slope * both1).astype(bf16)))
    ring.drain()
    w_down = jnp.concatenate(downs.slots(), axis=1)
    ring.token = None
    grad_both = []
    grad_down = Scatter(lambda k: down(hidden, sl(grad_low, k)), 1, n, chunk)
    grad_mlp = Scatter(lambda k: down(sl(normed2, k), grad_both[0]), -1, n, chunk)
    ring.add([grad_down, grad_mlp])
    ring.issue(1)
    act, slope, w_down = ring.hold((act, slope, w_down))
    grad_both.append(
        pl.pallas_call(
            hidden_back_kernel,
            grid=(seqs,),
            in_specs=[
                pl.BlockSpec((piece, width), lambda s: (s, 0)),
                pl.BlockSpec((units, width), lambda s: (0, 0)),
                pl.BlockSpec((piece, units), lambda s: (s, 0)),
                pl.BlockSpec((piece, units), lambda s: (s, 0)),
            ],
            out_specs=pl.BlockSpec((piece, 2 * units), lambda s: (s, 0)),
            out_shape=jax.ShapeDtypeStruct((rows, 2 * units), bf16),
            compiler_params=pltpu.CompilerParams(vmem_limit_bytes=vmem_bytes),
            cost_estimate=pl.CostEstimate(
                flops=2 * rows * width * units,
                bytes_accessed=moved_bytes(grad_low, w_down, act, slope, both),
                transcendentals=0,
            ),
        )(grad_low, w_down, act, slope)
    )
    ring.issue()
    grad_normed2 = tp_sum(
        lambda h: across(half_of(grad_both[0], h), w_mlp),
        others=ring.land,
        totals=lambda v: ring.land((ring.land(), v)[1]),
    )
    turned = jnp.concatenate([half_of(hidden, 1), half_of(hidden, 0)], axis=0)
    turned = jnp.where(odd == 1, turned, hidden)

    grad_middle, grad_rec, sum_gain2 = in_halves(
        middle_back_kernel,
        [middle, cot],
        [g.reshape(part_full) for g in grad_normed2],
        [gain2],
        [f32, bf16],
        1,
    )
    grad_out = Scatter(lambda k: down(product, sl(grad_rec, k)), 1, n, chunk)
    ring.add([grad_out])
    waiting = ring.pause()
    grad_rec = ring.land(grad_rec.reshape(rows, width))

    grad_product = across(grad_rec, w_out).reshape(wide)
    tail, local_grad, early = per_sequence(
        reverse_kernel,
        seqs,
        [(grad_product, "seq"), (gate_act, "seq"), (decay, "seq")],
        [(wide, f32, "seq")] * 2 + [(edge, f32, "seq")],
        [pltpu.VMEM((piece, lanes), f32)],
        rows * lanes * 50,
    )
    rounds = []

    def keep_round(ends):
        rounds.append(ends)
        return ends

    incoming = carried(ring.land(early), -1, n, keep_round)
    ring.go(waiting, incoming)
    mlp_out = lax.psum(dot(after(turned, *rounds), w_down).astype(bf16), "tp")
    grad_gates, grad_inner, grad_gate_in, head, last, sums = per_sequence(
        gates_back_kernel,
        seqs,
        [
            (grad_product, "seq"),
            (gate_slope, "seq"),
            (tail, "seq"),
            (local_grad, "seq"),
            (incoming, "seq"),
            (states, "seq"),
            (entry, "seq"),
            (recur, "seq"),
            (admit, "seq"),
            (decay, "seq"),
            (root, "seq"),
            (mixed, "seq"),
            (inner, "seq"),
            (before, "seq"),
            (gate_m, "whole"),
            (rate, "whole"),
            (conv_w, "whole"),
        ],
        [
            ((2,) + wide, bf16, "pair"),
            (wide, bf16, "seq"),
            (wide, bf16, "seq"),
            (edge, f32, "seq"),
            (edge, f32, "seq"),
            ((pad_rows, lanes), f32, "whole"),
        ],
        [pltpu.VMEM((piece, lanes), f32)] + [pltpu.VMEM((piece + pad_rows, lanes), f32)] * 2,
        gate_flops,
    )
    behind = lax.ppermute(
        head[:, : taps - 1].astype(bf16), "seq", [(i + 1, i) for i in range(n - 1)]
    ).astype(f32)
    beyond = jnp.concatenate([jnp.zeros_like(last), behind], axis=1)
    beyond = jnp.pad(beyond, ((0, 0), (0, 1), (0, 0)))
    for lag in range(1, taps):
        last = last + conv_w[lag] * beyond[:, lag : lag + pad_rows]
    grad_inner = lax.dynamic_update_slice(
        grad_inner, last.astype(bf16), (0, piece - pad_rows, 0)
    )
    back0 = grad_inner.reshape(rows, lanes)
    back1 = grad_gate_in.reshape(rows, lanes)
    back = ring.land(jnp.concatenate([back0, back1], axis=1))
    w_both = jnp.concatenate([jnp.concatenate(in0, axis=1), jnp.concatenate(in1, axis=1)], axis=0)
    grads = [
        Scatter(lambda k: down(back, normed1[k]), -1, n, chunk),
    ]
    ring.add(grads)
    ring.issue()
    late = []

    def hold_output(chip):
        late.append(after(mlp_out, chip))
        return ring.land(chip)

    grad_normed1 = tp_sum(
        lambda h: dot(half_of(back, h), w_both),
        chips=hold_output,
        totals=lambda v: lands(v, 4),
    )
    mlp_out = late[0]
    ring.drain()
    grads = [g.total() for g in grads]
    low_mixed = mixed.astype(bf16).reshape(rows, lanes)
    grad_matrix = []
    for k in range(2):
        dense = down(low_mixed, grad_gates[k].reshape(rows, lanes)).astype(bf16)
        for h in range(heads):
            at = slice(h * head_width, (h + 1) * head_width)
            grad_matrix.append(dense[at, at])
    packed = jnp.concatenate(
        grad_matrix + [sums.astype(bf16).reshape(-1, head_width)], axis=0
    )
    packed = lax.psum(packed, "seq")

    if tiled:
        output = by_rows(
            output_kernel,
            [middle, mlp_out.reshape(full)],
            [],
            [bf16],
            0,
            move,
            back=True,
            moved=(1,),
        )[0]
        grad_tokens = in_halves(
            start_back_kernel,
            [x, grad_middle],
            [g.reshape(part_full) for g in grad_normed1],
            [gain1],
            [f32],
            0,
            move,
            back=True,
        )[0]
    else:
        mlp_out = mlp_out.reshape(full)[sequence].astype(f32)
        output = own_order((middle + mlp_out).astype(bf16), move, True)
        grad_normed1_all = jnp.concatenate(grad_normed1, axis=0).reshape(full).astype(f32)
        grad_start = norm_back(x.astype(f32), grad_normed1_all, gain1)[0]
        grad_tokens = own_order(grad_middle + grad_start, move, True)
    mine = lax.axis_index("seq")
    slots = (me - jnp.asarray(place, jnp.int32)) % n
    scaled1 = start[:block] * inverse1[:block]
    sum_gain1 = jnp.sum(grad_normed1[0].astype(f32) * scaled1, axis=0)
    grad_gains = jnp.stack([sum_gain1, 0.5 * jnp.sum(sum_gain2, axis=0)])
    grad_gains = grad_gains + core_swap(grad_gains)
    grad_gains = seq_sum(grad_gains.reshape(2, n, part)[:, slots], n)
    grad_gains = lax.dynamic_index_in_dim(grad_gains, mine, 1, keepdims=False)

    packed, grad_gains = lax.optimization_barrier((packed, grad_gains))
    packed = packed.astype(f32)
    matrix_rows = 2 * heads * head_width
    grad_matrix = packed[:matrix_rows].reshape(gate_matrix.shape)
    small = packed[matrix_rows:].reshape(4 + taps, lanes)
    return (
        output,
        grad_tokens,
        grad_gains[0],
        jnp.transpose(grads[0].reshape(2, lanes, part), (2, 0, 1)),
        small[4:],
        small[3],
        grad_matrix,
        small[1:3],
        small[0],
        grad_out.total(),
        grad_gains[1],
        grad_mlp.total().reshape(part, 2, units),
        grad_down.total(),
    )


def solution(mesh):
    in_specs = (
        P(None, "seq", None),
        P("seq"),
        P("seq", None, "tp"),
        P(None, "tp"),
        P("tp"),
        P(None, "tp", None, None),
        P(None, "tp"),
        P("tp"),
        P("tp", "seq"),
        P("seq"),
        P("seq", None, "tp"),
        P("tp", "seq"),
        P(None, "seq", None),
    )
    out_specs = (
        P(None, "seq", None),
        P(None, "seq", None),
        P("seq"),
        P("seq", None, "tp"),
        P(None, "tp"),
        P("tp"),
        P(None, "tp", None, None),
        P(None, "tp"),
        P("tp"),
        P("tp", "seq"),
        P("seq"),
        P("seq", None, "tp"),
        P("tp", "seq"),
    )
    return jax.shard_map(shards, mesh=mesh, in_specs=in_specs, out_specs=out_specs, check_vma=False)
```

```python
import functools
import math

import jax
import jax.numpy as jnp
from jax import lax
from jax.experimental import pallas as pl
from jax.experimental.pallas import tpu as pltpu
from jax.sharding import PartitionSpec as P

f32 = jnp.float32
bf16 = jnp.bfloat16
eps = 1e-06
gelu_scale = math.sqrt(2.0 / math.pi)
step_rows = 16
pad_rows = 8
vmem_bytes = 48 * 2**20
ring_most = 8
lane_depth = 2
norm_rows = 128


def ring_order(n):
    return [*range(0, n, 2), *range(n - 1 - n % 2, 0, -2)]


def after(values, *earlier):
    return lax.optimization_barrier((values, *earlier))[0]


class Ring:
    def __init__(self, order, depth):
        n = len(order)
        self.n = n
        self.depth = depth
        self.pairs = {w: [(order[i], order[(i + w) % n]) for i in range(n)] for w in (1, -1)}
        self.queue = {1: [], -1: []}
        self.flying = {1: [], -1: []}
        self.landed = {1: [], -1: []}
        self.sent = {1: 0, -1: 0}
        self.last = {1: None, -1: None}
        self.token = None

    def add(self, weights, delays=None):
        half = self.n // 2
        delays = delays or [0] * len(weights)
        left = {id(flow): flow.count for w in weights for flow in w.flows.values()}
        for turn in range(half + max(delays)):
            for late in (True, False):
                for weight, delay in zip(weights, delays):
                    if (delay > 0) != late or turn < delay:
                        continue
                    for way, flow in weight.flows.items():
                        if left[id(flow)]:
                            left[id(flow)] -= 1
                            self.queue[way].append(flow)

    def issue(self, most=None):
        for way in (1, -1):
            queue, flying, landed = self.queue[way], self.flying[way], self.landed[way]
            while queue and len(flying) < (most or self.depth) and not queue[0].busy:
                flow = queue.pop(0)
                message = flow.message()
                gate = self.sent[way] - self.depth
                if gate >= 0:
                    message = after(message, landed[gate])
                if self.token is not None:
                    message = after(message, self.token)
                flow.busy = True
                self.sent[way] += 1
                self.last[way] = message
                flying.append((flow, lax.ppermute(message, "seq", self.pairs[way])))

    def hold(self, values):
        last = [message for message in self.last.values() if message is not None]
        return after(values, *last) if last else values

    def resume(self, token):
        self.token = token
        self.issue()
        return token

    def quiet(self, values):
        waiting = {w: self.queue[w] for w in (1, -1)}
        self.queue = {1: [], -1: []}
        for _ in range(self.depth):
            values = self.land(values)
        self.queue = waiting
        return values

    def pause(self):
        waiting, self.queue = self.queue, {1: [], -1: []}
        return waiting

    def go(self, waiting, token):
        self.queue = waiting
        self.resume(token)

    def land(self, values=None, count=1):
        for turn in range(count):
            taken = [(w, *self.flying[w].pop(0)) for w in (1, -1) if self.flying[w]]
            arrived = [message for _, _, message in taken]
            if values is not None and taken and turn == count - 1:
                values, *arrived = lax.optimization_barrier((values, *arrived))
            for (way, flow, _), message in zip(taken, arrived):
                flow.arrive(message)
                flow.busy = False
                self.landed[way].append(message)
            self.issue()
        return values

    def drain(self):
        while self.queue[1] or self.queue[-1] or self.flying[1] or self.flying[-1]:
            self.land()


class Pieces:
    def __init__(self, own, count):
        self.value, self.count, self.busy, self.got = own, count, False, []

    def message(self):
        return self.value

    def arrive(self, message):
        self.value = message
        self.got.append(message)


class Totals:
    def __init__(self, part, slots):
        self.part, self.slots, self.count, self.busy = part, slots, len(slots), False
        self.got, self.at = None, 0

    def message(self):
        total = self.part(self.slots[self.at])
        if self.got is not None:
            total = total + self.got.astype(f32)
        self.at += 1
        return total.astype(bf16)

    def arrive(self, message):
        self.got = message


class Gather:
    def __init__(self, piece, far, n, chunk):
        half = n // 2
        self.piece, self.n, self.chunk, self.flows = piece, n, chunk, {}
        if n <= ring_most:
            self.flows = {w: Pieces(piece, half if w == far else half - 1) for w in (1, -1)}

    def slots(self):
        if not self.flows:
            pieces = lax.all_gather(self.piece, "seq")[self.chunk]
            return [pieces[k] for k in range(self.n)]
        return [self.piece, *self.flows[1].got, *self.flows[-1].got[::-1]]


class Scatter:
    def __init__(self, part, far, n, chunk):
        half = n // 2
        self.part, self.n, self.chunk, self.flows = part, n, chunk, {}
        if n <= ring_most:
            self.flows = {
                1: Totals(part, list(range(half if far == 1 else half + 1, n))),
                -1: Totals(part, list(range(half if far == -1 else half - 1, 0, -1))),
            }

    def total(self):
        if not self.flows:
            parts = jnp.stack([self.part(k).astype(bf16) for k in range(self.n)])
            parts = parts[jnp.argsort(self.chunk)]
            return lax.psum_scatter(parts, "seq", scatter_dimension=0).astype(f32)
        total = self.part(0)
        for flow in self.flows.values():
            if flow.got is not None:
                total = total + flow.got.astype(f32)
        return total


def core_swap(values):
    size = lax.axis_size("tp")
    return lax.ppermute(values, "tp", [(i, i ^ 1) for i in range(size)])


def chip_swap(values):
    size = lax.axis_size("tp")
    return lax.ppermute(values, "tp", [(i, i ^ 2) for i in range(size)])


def tp_sum(part, others=lambda v: v, chips=lambda v: v, totals=lambda v: v):
    got = core_swap(others(part(1).astype(bf16)))
    own = lax.optimization_barrier(part(0).astype(bf16))
    chip = chips((own.astype(f32) + got.astype(f32)).astype(bf16))
    far = chip_swap(chip)
    total = totals((chip.astype(f32) + far.astype(f32)).astype(bf16))
    return total, core_swap(total)


def gelu_parts(x):
    t = jnp.tanh(gelu_scale * (x + 0.044715 * x * x * x))
    value = 0.5 * x * (1.0 + t)
    slope = 0.5 * (1.0 + t) + 0.5 * x * (1.0 - t * t) * gelu_scale * (1.0 + 3 * 0.044715 * x * x)
    return value, slope


def drive_square(log_decay, decay):
    y = -2.0 * log_decay
    series = 1.0 - y * (1.0 / 9.0)
    for k in range(8, 1, -1):
        series = 1.0 - y * (1.0 / k) * series
    return jnp.where(y < 0.5, y * series, 1.0 - decay * decay)


def scan_block(a, b, rows, reverse):
    count = a.shape[0]
    by = 1
    while by < count:
        turn = count - by if reverse else by
        pa = pltpu.roll(a, turn, 0)
        pb = pltpu.roll(b, turn, 0)
        inside = rows < count - by if reverse else rows >= by
        b = jnp.where(inside, a * pb + b, b)
        a = jnp.where(inside, a * pa, a)
        by *= 2
    return a, b


def forward_kernel(
    inner, before, conv_w, conv_b, gate_m, gate_b, rate,
    mixed, recur, admit, decay, root, cum, local, ends, ext, gates,
):
    length, lanes = inner.shape
    ext[:pad_rows] = before[...]
    ext[pad_rows:] = inner[...].astype(f32)
    taps = conv_w.shape[0]
    total = jnp.broadcast_to(conv_b[...], (length, lanes))
    for lag in range(taps):
        total = total + conv_w[lag : lag + 1] * ext[pad_rows - lag : pad_rows - lag + length]
    mixed[...] = total
    low = total.astype(bf16)
    for k in range(2):
        gates[k] = jnp.dot(low, gate_m[k], preferred_element_type=f32) + gate_b[k : k + 1]
    rows = lax.broadcasted_iota(jnp.int32, (step_rows, lanes), 0)

    def step(i, carry):
        at = pl.ds(pl.multiple_of(i * step_rows, step_rows), step_rows)
        r = jax.nn.sigmoid(gates[0, at])
        g = jax.nn.sigmoid(gates[1, at])
        log_decay = -8.0 * r * rate[...]
        d = jnp.exp(log_decay)
        m = jnp.sqrt(drive_square(log_decay, d))
        drive = m * g * mixed[at]
        root[at] = m
        recur[at] = r
        admit[at] = g
        decay[at] = d
        a, b = scan_block(d, drive, rows, False)
        b = b + a * carry[1]
        a = a * carry[0]
        cum[at] = a
        local[at] = b
        return a[step_rows - 1 :], b[step_rows - 1 :]

    a, b = lax.fori_loop(
        0, length // step_rows, step, (jnp.ones((1, lanes), f32), jnp.zeros((1, lanes), f32))
    )
    ends[0:1] = a
    ends[1:2] = b
    ends[2:] = jnp.zeros((pad_rows - 2, lanes), f32)


def reverse_kernel(grad_product, act, decay, tail, grad, first, nexts):
    length, lanes = act.shape
    nexts[...] = pltpu.roll(decay[...], length - 1, 0)
    nexts[length - 1 :] = jnp.ones((1, lanes), f32)
    rows = lax.broadcasted_iota(jnp.int32, (step_rows, lanes), 0)
    steps = length // step_rows

    def step(i, carry):
        at = pl.ds(pl.multiple_of((steps - 1 - i) * step_rows, step_rows), step_rows)
        direct = grad_product[at] * act[at]
        a, b = scan_block(nexts[at], direct, rows, True)
        b = b + a * carry[1]
        a = a * carry[0]
        tail[at] = a
        grad[at] = b
        return a[:1], b[:1]

    a, b = lax.fori_loop(0, steps, step, (jnp.ones((1, lanes), f32), jnp.zeros((1, lanes), f32)))
    first[0:1] = decay[0:1] * a
    first[1:2] = decay[0:1] * b
    first[2:] = jnp.zeros((pad_rows - 2, lanes), f32)


def gates_back_kernel(
    grad_product, slope, tail, grad, incoming, states, entry, recur, admit, decay, root, mixed, inner, before,
    gate_m, rate, conv_w, grad_gates, grad_inner, grad_gate_in, head, last, sums, grad_mix, grad_ext, ext,
):
    length, lanes = inner.shape
    enter = entry[0:1]
    later = incoming[0:1]
    taps = conv_w.shape[0]

    def step(i, carry):
        at = pl.ds(pl.multiple_of(i * step_rows, step_rows), step_rows)
        state = states[at]
        rows = lax.broadcasted_iota(jnp.int32, (step_rows, lanes), 0)
        earlier = jnp.where(rows == 0, carry[3], pltpu.roll(state, 1, 0))
        grad_gate_in[at] = (slope[at] * (grad_product[at] * state)).astype(bf16)
        total = grad[at] + tail[at] * later
        r, g, d, m, mix = recur[at], admit[at], decay[at], root[at], mixed[at]
        grad_mix[at] = total * m * g
        both = total * mix
        gate1 = both * m * g * (1.0 - g)
        grad_log = total * earlier * d - both * g * d * d / m
        gate0 = -8.0 * rate[...] * grad_log * r * (1.0 - r)
        low0 = gate0.astype(bf16)
        low1 = gate1.astype(bf16)
        grad_gates[0, at] = low0
        grad_gates[1, at] = low1
        return (
            carry[0] - 8.0 * (grad_log * r),
            carry[1] + low0.astype(f32),
            carry[2] + low1.astype(f32),
            state[step_rows - 1 :],
        )

    zero = jnp.zeros((step_rows, lanes), f32)
    totals = lax.fori_loop(0, length // step_rows, step, (zero, zero, zero, enter))
    back = grad_mix[...]
    for k in range(2):
        back = back + lax.dot_general(
            grad_gates[k], gate_m[k], (((1,), (1,)), ((), ())), preferred_element_type=f32
        )
    back = back.astype(bf16).astype(f32)
    head[...] = back[:pad_rows]
    grad_ext[:length] = back
    grad_ext[length:] = jnp.zeros((pad_rows, lanes), f32)
    ext[:pad_rows] = before[...]
    ext[pad_rows:] = inner[...].astype(f32)

    @pl.when(pl.program_id(0) == 0)
    def _():
        sums[...] = jnp.zeros_like(sums)

    for k in range(3):
        sums[k : k + 1] += jnp.sum(totals[k], axis=0, keepdims=True)
    sums[3:4] += jnp.sum(back, axis=0, keepdims=True)
    total = jnp.zeros((length, lanes), f32)
    for lag in range(taps):
        total = total + conv_w[lag : lag + 1] * grad_ext[lag : lag + length]
        term = back * ext[pad_rows - lag : pad_rows - lag + length]
        sums[4 + lag : 5 + lag] += jnp.sum(term, axis=0, keepdims=True)
    grad_inner[...] = total.astype(bf16)
    last[...] = total[length - pad_rows :]


def hidden_back_kernel(cot, w_down, act, slope, grad_both):
    units = w_down.shape[0]
    cut = math.gcd(units, 512)
    for j in range(0, units, cut):
        grad = lax.dot_general(
            cot[...], w_down[j : j + cut], (((1,), (1,)), ((), ())), preferred_element_type=f32
        )
        grad_both[:, j : j + cut] = (grad * slope[:, j : j + cut].astype(f32)).astype(bf16)
        grad_both[:, units + j : units + j + cut] = (
            grad * act[:, j : j + cut].astype(f32)
        ).astype(bf16)


def per_sequence(kernel, seqs, inputs, outputs, scratch, flops):
    def spec(shape, kind):
        if kind == "whole":
            return pl.BlockSpec(shape, lambda s: (0,) * len(shape))
        if kind == "pair":
            return pl.BlockSpec((shape[0], None) + shape[2:], lambda s: (0, s, 0, 0))
        return pl.BlockSpec((None,) + shape[1:], lambda s: (s,) + (0,) * (len(shape) - 1))

    moved = sum(a.size * a.dtype.itemsize for a, _ in inputs)
    moved += sum(math.prod(shape) * jnp.dtype(t).itemsize for shape, t, _ in outputs)
    return pl.pallas_call(
        kernel,
        grid=(seqs,),
        in_specs=[spec(a.shape, kind) for a, kind in inputs],
        out_specs=[spec(shape, kind) for shape, _, kind in outputs],
        out_shape=[jax.ShapeDtypeStruct(shape, t) for shape, t, _ in outputs],
        scratch_shapes=scratch,
        compiler_params=pltpu.CompilerParams(vmem_limit_bytes=vmem_bytes),
        cost_estimate=pl.CostEstimate(flops=flops, bytes_accessed=moved, transcendentals=0),
    )(*[a for a, _ in inputs])


def moved_bytes(*arrays):
    return sum(math.prod(a.shape) * jnp.dtype(a.dtype).itemsize for a in arrays)


def by_rows(
    kernel, arrays, whole, outputs, sums, order=None, back=False, moved=(), half=None, earlier=()
):
    seqs, length, width = arrays[0].shape
    block = min(norm_rows, length)
    count = seqs if half is None else seqs // 2
    skip = count * (half or 0)
    moves = order is not None
    tile = (None, block, width)
    near = pl.BlockSpec(tile, lambda s, r, *_: (s + skip, r, 0))
    own = pl.BlockSpec(tile, lambda s, r, *_: (s, r, 0))
    far = pl.BlockSpec(tile, lambda s, r, sequence, chunk: (sequence[s + skip], r, 0))
    total = pl.BlockSpec((pad_rows, width), lambda s, r, *_: (0, 0))
    out_shape = [jax.ShapeDtypeStruct((seqs, length, width), t) for t in outputs]
    out_shape += [jax.ShapeDtypeStruct((pad_rows, width), f32)] * sums
    scalars = 2 if moves else 0
    given = scalars + len(arrays) + len(whole)

    def body(*refs):
        kernel(*refs[:given], *refs[given + len(earlier) :])

    return pl.pallas_call(
        body,
        grid_spec=pltpu.PrefetchScalarGridSpec(
            num_scalar_prefetch=scalars,
            grid=(count, length // block),
            in_specs=[
                own
                if a.shape[0] != seqs
                else far
                if moves and (not back or i in moved)
                else near
                for i, a in enumerate(arrays)
            ]
            + [pl.BlockSpec(w.shape, lambda s, r, *_: (0, 0)) for w in whole]
            + [pl.BlockSpec(memory_space=pl.ANY)] * len(earlier),
            out_specs=[far if moves and back else near] * len(outputs) + [total] * sums,
        ),
        out_shape=out_shape,
        input_output_aliases={given + i: i for i in range(len(earlier))},
        compiler_params=pltpu.CompilerParams(vmem_limit_bytes=vmem_bytes),
        cost_estimate=pl.CostEstimate(
            flops=8 * count * length * width,
            bytes_accessed=moved_bytes(*arrays, *out_shape) * count // seqs,
            transcendentals=0,
        ),
    )(*(order if moves else ()), *arrays, *whole, *earlier)


def in_halves(kernel, arrays, summed, whole, outputs, sums, order=None, back=False):
    ready = by_rows(
        kernel, [arrays[0], summed[0], *arrays[1:]], whole, outputs, sums, order, back, (), 0
    )
    count = len(outputs)
    done = by_rows(
        kernel,
        [arrays[0], summed[1], *arrays[1:]],
        whole,
        outputs,
        sums,
        order,
        back,
        (),
        1,
        tuple(ready[:count]),
    )
    return [*done[:count], *(a + b for a, b in zip(ready[count:], done[count:]))]


def enter_kernel(sequence, chunk, *refs):
    count = len(refs) // 2
    part = refs[0].shape[1] // chunk.shape[0]
    for k in range(chunk.shape[0]):
        at = pl.ds(pl.multiple_of(chunk[k] * part, part), part)
        for i in range(count):
            refs[count + i][:, k * part : (k + 1) * part] = refs[i][:, at]


def norm_kernel(x, added, gain, middle, normed):
    total = x[...].astype(f32) + added[...].astype(f32)
    middle[...] = total
    inverse = lax.rsqrt(jnp.mean(total * total, axis=-1, keepdims=True) + eps)
    normed[...] = (total * inverse * gain[...]).astype(bf16)


def norm_back(values, grad, gain):
    inverse = lax.rsqrt(jnp.mean(values * values, axis=-1, keepdims=True) + eps)
    scaled = values * inverse
    weighted = grad * gain
    inner = jnp.mean(weighted * scaled, axis=-1, keepdims=True)
    return inverse * (weighted - scaled * inner), grad * scaled


def add_rows(total, values):
    @pl.when((pl.program_id(0) == 0) & (pl.program_id(1) == 0))
    def _():
        total[...] = jnp.zeros_like(total)

    rows, width = values.shape
    total[...] += jnp.sum(values.reshape(rows // pad_rows, pad_rows, width), axis=0)


def middle_back_kernel(middle, grad_normed, cot, gain, grad_middle, grad_low, total):
    grad, terms = norm_back(middle[...], grad_normed[...].astype(f32), gain[...])
    grad = grad + cot[...].astype(f32)
    grad_middle[...] = grad
    grad_low[...] = grad.astype(bf16)
    add_rows(total, terms)


def put_chunks(chunk, target, values):
    part = values.shape[1] // chunk.shape[0]
    for k in range(chunk.shape[0]):
        at = pl.ds(pl.multiple_of(chunk[k] * part, part), part)
        target[:, at] = values[:, k * part : (k + 1) * part]


def start_back_kernel(sequence, chunk, x, grad_normed, grad_middle, gain, grad_tokens):
    grad = norm_back(x[...].astype(f32), grad_normed[...].astype(f32), gain[...])[0]
    put_chunks(chunk, grad_tokens, grad + grad_middle[...])


def output_kernel(sequence, chunk, middle, added, output):
    put_chunks(chunk, output, (middle[...] + added[...].astype(f32)).astype(bf16))


def own_order(array, order, back=False):
    sequence, chunk = order
    if back:
        sequence, chunk = jnp.argsort(sequence), jnp.argsort(chunk)
    seqs, length, width = array.shape
    chunks = chunk.shape[0]
    split = array[sequence].reshape(seqs, length, chunks, width // chunks)
    return split[:, :, chunk].reshape(array.shape)


def carried(ends, way, n, between=lambda v: v):
    def shifted(values, by):
        pairs = [(i, i + way * by) for i in range(n) if 0 <= i + way * by < n]
        return lax.ppermute(values, "seq", pairs)

    ends = ends[:, :2]
    by = 1
    while 2 * by < n:
        earlier = shifted(ends, by)
        ends = ends[:, :1] * earlier + jnp.concatenate(
            [jnp.zeros_like(ends[:, 1:]), ends[:, 1:]], axis=1
        )
        by *= 2
        if by == 2:
            ends = between(ends)
    near, far = shifted(ends, 1), shifted(ends, 1 + by)
    state = near[:, :1] * far[:, 1:] + near[:, 1:]
    return jnp.pad(state, ((0, 0), (0, pad_rows - 1), (0, 0)))


def seq_sum(values, n):
    by = 1
    while by < n:
        values = values + lax.ppermute(values, "seq", [(i, i ^ by) for i in range(n)])
        by *= 2
    return values


def dense_heads(matrix):
    kinds, heads, width, _ = matrix.shape
    rows = [
        jnp.pad(matrix[:, h], ((0, 0), (0, 0), (h * width, (heads - 1 - h) * width)))
        for h in range(heads)
    ]
    return jnp.concatenate(rows, axis=1)


def across(a, b):
    return lax.dot_general(a, b, (((1,), (1,)), ((), ())), preferred_element_type=f32)


def down(a, b):
    return lax.dot_general(a, b, (((0,), (0,)), ((), ())), preferred_element_type=f32)


def dot(a, b):
    return jnp.dot(a, b, preferred_element_type=f32)


def shards(
    tokens,
    norm1_gain,
    in_weight,
    conv_weight,
    conv_bias,
    gate_matrix,
    gate_bias,
    decay_rate,
    out_weight,
    norm2_gain,
    mlp_weight,
    down_weight,
    cotangent,
):
    seqs, piece, width = tokens.shape
    rows = seqs * piece
    lanes = in_weight.shape[2]
    units = mlp_weight.shape[2]
    heads, head_width = gate_matrix.shape[1:3]
    taps = conv_weight.shape[0]
    n = lax.axis_size("seq")
    part = width // n
    order = ring_order(n)
    place = [order.index(i) for i in range(n)]
    me = jnp.asarray(place, jnp.int32)[lax.axis_index("seq")]
    chunk = jnp.asarray(order, jnp.int32)[(me - jnp.arange(n, dtype=jnp.int32)) % n]
    odd = lax.axis_index("tp") % 2
    sequence = (jnp.arange(seqs, dtype=jnp.int32) + odd * (seqs // 2)) % seqs
    move = (sequence, chunk)
    ring = Ring(order, lane_depth)
    tiled = part % 128 == 0

    def sl(a, k):
        return a[:, k * part : (k + 1) * part]

    move = (sequence, chunk)
    w_in = jnp.transpose(in_weight, (1, 2, 0))
    half_lanes = lanes // 2
    own_gain = jnp.pad(jnp.stack([norm1_gain, norm2_gain]), ((0, 14), (0, 0)))
    first = Gather(jnp.concatenate([w_in[0], out_weight[:half_lanes]], axis=0), 1, n, chunk)
    second = Gather(
        jnp.concatenate([w_in[1], out_weight[half_lanes:], own_gain], axis=0), -1, n, chunk
    )
    mlp = [Gather(mlp_weight[:, 0], 1, n, chunk), Gather(mlp_weight[:, 1], -1, n, chunk)]
    downs = Gather(down_weight, 1, n, chunk)
    ring.add([first, second])
    ring.add([*mlp, downs], [0, 0, 3])
    ring.issue()

    tokens, cotangent = ring.land((tokens, cotangent))
    if tiled:
        x, cot = by_rows(enter_kernel, [tokens, cotangent], [], [bf16, bf16], 0, move)
    else:
        x, cot = own_order(tokens, move), own_order(cotangent, move)
    full = x.shape
    part_full = (seqs // 2, piece, width)
    x, cot = ring.land((x, cot))
    grad_low = cot.reshape(rows, width)
    start = x.reshape(rows, width).astype(f32)
    inverse1 = lax.rsqrt(jnp.mean(start * start, axis=-1, keepdims=True) + eps)
    for _ in range(n - 3):
        ring.land()
    first, second = first.slots(), second.slots()
    in0 = [p[:lanes] for p in first]
    in1 = [p[:lanes] for p in second]
    gains = [p[lanes + half_lanes : lanes + half_lanes + 2] for p in second]
    gain1, gain2 = (
        jnp.concatenate([g[i : i + 1] for g in gains], axis=1).astype(f32) for i in range(2)
    )
    normed1 = [
        (sl(start, k) * inverse1 * gains[k][:1].astype(f32)).astype(bf16) for k in range(n)
    ]
    inner = sum(across(normed1[k], in0[k]) for k in range(n)).astype(bf16)
    gate_in = sum(across(normed1[k], in1[k]) for k in range(n)).astype(bf16)
    inner = ring.land(inner)
    inner = inner.reshape(seqs, piece, lanes)
    gate_in = gate_in.reshape(seqs, piece, lanes)
    before = lax.ppermute(
        inner[:, piece - taps + 1 :], "seq", [(i, i + 1) for i in range(n - 1)]
    ).astype(f32)
    before = ring.land(jnp.pad(before, ((0, 0), (pad_rows - taps + 1, 0), (0, 0))))
    conv_w = conv_weight.astype(f32)
    rate = decay_rate.astype(f32)[None]
    gate_m = dense_heads(gate_matrix)
    wide = (seqs, piece, lanes)
    edge = (seqs, pad_rows, lanes)
    gate_flops = 4 * rows * lanes * lanes
    mixed, recur, admit, decay, root, cum, local, ends = per_sequence(
        forward_kernel,
        seqs,
        [
            (inner, "seq"),
            (before, "seq"),
            (conv_w, "whole"),
            (conv_bias.astype(f32)[None], "whole"),
            (gate_m, "whole"),
            (gate_bias.astype(f32), "whole"),
            (rate, "whole"),
        ],
        [(wide, f32, "seq")] * 7 + [(edge, f32, "seq")],
        [pltpu.VMEM((piece + pad_rows, lanes), f32), pltpu.VMEM((2, piece, lanes), f32)],
        gate_flops,
    )
    entry = ring.land(carried(ring.land(ends), 1, n, ring.land))
    states = local + cum * entry[:, :1]
    product = (states * gelu_parts(gate_in.astype(f32))[0]).astype(bf16).reshape(rows, lanes)
    w_out = jnp.concatenate(
        [
            jnp.concatenate([p[lanes : lanes + half_lanes] for p in pieces], axis=1)
            for pieces in (first, second)
        ],
        axis=0,
    )
    block = rows // 2

    def half_of(a, h):
        return a[h * block : (h + 1) * block]

    def lands(values, count):
        for _ in range(count):
            ring.land()
        return ring.resume(values)

    chips = []

    def keep(chip):
        chips.append(ring.land(chip))
        return chips[0]

    recurrent = tp_sum(
        lambda h: dot(half_of(product, h), w_out),
        chips=keep,
        totals=lambda v: lands(v, 3),
    )
    gate_act, gate_slope = gelu_parts(after(gate_in, chips[0]).astype(f32))

    middle, normed2 = in_halves(
        norm_kernel, [x], [r.reshape(part_full) for r in recurrent], [gain2], [f32, bf16], 0
    )
    normed2 = ring.land(normed2.reshape(rows, width))
    w_mlp = jnp.concatenate([jnp.concatenate(w.slots(), axis=0) for w in mlp], axis=1)
    both = dot(normed2, w_mlp).astype(bf16)
    both0, both1 = both[:, :units].astype(f32), both[:, units:].astype(f32)
    act, slope = gelu_parts(both0)
    hidden = (act * both1).astype(bf16)
    hidden, act, slope = ring.land((hidden, act.astype(bf16), (slope * both1).astype(bf16)))
    ring.drain()
    w_down = jnp.concatenate(downs.slots(), axis=1)
    ring.token = None
    grad_both = []
    grad_down = Scatter(lambda k: down(hidden, sl(grad_low, k)), 1, n, chunk)
    grad_mlp = Scatter(lambda k: down(sl(normed2, k), grad_both[0]), -1, n, chunk)
    ring.add([grad_down, grad_mlp])
    ring.issue(1)
    act, slope, w_down = ring.hold((act, slope, w_down))
    grad_both.append(
        pl.pallas_call(
            hidden_back_kernel,
            grid=(seqs,),
            in_specs=[
                pl.BlockSpec((piece, width), lambda s: (s, 0)),
                pl.BlockSpec((units, width), lambda s: (0, 0)),
                pl.BlockSpec((piece, units), lambda s: (s, 0)),
                pl.BlockSpec((piece, units), lambda s: (s, 0)),
            ],
            out_specs=pl.BlockSpec((piece, 2 * units), lambda s: (s, 0)),
            out_shape=jax.ShapeDtypeStruct((rows, 2 * units), bf16),
            compiler_params=pltpu.CompilerParams(vmem_limit_bytes=vmem_bytes),
            cost_estimate=pl.CostEstimate(
                flops=2 * rows * width * units,
                bytes_accessed=moved_bytes(grad_low, w_down, act, slope, both),
                transcendentals=0,
            ),
        )(grad_low, w_down, act, slope)
    )
    ring.issue()
    grad_normed2 = tp_sum(
        lambda h: across(half_of(grad_both[0], h), w_mlp),
        others=ring.land,
        totals=lambda v: ring.land((ring.land(), v)[1]),
    )
    turned = jnp.concatenate([half_of(hidden, 1), half_of(hidden, 0)], axis=0)
    turned = jnp.where(odd == 1, turned, hidden)

    grad_middle, grad_rec, sum_gain2 = in_halves(
        middle_back_kernel,
        [middle, cot],
        [g.reshape(part_full) for g in grad_normed2],
        [gain2],
        [f32, bf16],
        1,
    )
    grad_out = Scatter(lambda k: down(product, sl(grad_rec, k)), 1, n, chunk)
    ring.add([grad_out])
    waiting = ring.pause()
    grad_rec = ring.land(grad_rec.reshape(rows, width))

    grad_product = across(grad_rec, w_out).reshape(wide)
    tail, local_grad, early = per_sequence(
        reverse_kernel,
        seqs,
        [(grad_product, "seq"), (gate_act, "seq"), (decay, "seq")],
        [(wide, f32, "seq")] * 2 + [(edge, f32, "seq")],
        [pltpu.VMEM((piece, lanes), f32)],
        rows * lanes * 50,
    )
    rounds = []

    def keep_round(ends):
        rounds.append(ends)
        return ends

    incoming = carried(ring.land(early), -1, n, keep_round)
    ring.go(waiting, incoming)
    mlp_out = lax.psum(dot(after(turned, *rounds), w_down).astype(bf16), "tp")
    grad_gates, grad_inner, grad_gate_in, head, last, sums = per_sequence(
        gates_back_kernel,
        seqs,
        [
            (grad_product, "seq"),
            (gate_slope, "seq"),
            (tail, "seq"),
            (local_grad, "seq"),
            (incoming, "seq"),
            (states, "seq"),
            (entry, "seq"),
            (recur, "seq"),
            (admit, "seq"),
            (decay, "seq"),
            (root, "seq"),
            (mixed, "seq"),
            (inner, "seq"),
            (before, "seq"),
            (gate_m, "whole"),
            (rate, "whole"),
            (conv_w, "whole"),
        ],
        [
            ((2,) + wide, bf16, "pair"),
            (wide, bf16, "seq"),
            (wide, bf16, "seq"),
            (edge, f32, "seq"),
            (edge, f32, "seq"),
            ((pad_rows, lanes), f32, "whole"),
        ],
        [pltpu.VMEM((piece, lanes), f32)] + [pltpu.VMEM((piece + pad_rows, lanes), f32)] * 2,
        gate_flops,
    )
    behind = lax.ppermute(
        head[:, : taps - 1].astype(bf16), "seq", [(i + 1, i) for i in range(n - 1)]
    ).astype(f32)
    beyond = jnp.concatenate([jnp.zeros_like(last), behind], axis=1)
    beyond = jnp.pad(beyond, ((0, 0), (0, 1), (0, 0)))
    for lag in range(1, taps):
        last = last + conv_w[lag] * beyond[:, lag : lag + pad_rows]
    grad_inner = lax.dynamic_update_slice(
        grad_inner, last.astype(bf16), (0, piece - pad_rows, 0)
    )
    back0 = grad_inner.reshape(rows, lanes)
    back1 = grad_gate_in.reshape(rows, lanes)
    back = ring.land(jnp.concatenate([back0, back1], axis=1))
    w_both = jnp.concatenate([jnp.concatenate(in0, axis=1), jnp.concatenate(in1, axis=1)], axis=0)
    grads = [
        Scatter(lambda k: down(back0, normed1[k]), 1, n, chunk),
        Scatter(lambda k: down(back1, normed1[k]), -1, n, chunk),
    ]
    ring.add(grads)
    ring.issue()
    late = []

    def hold_output(chip):
        late.append(after(mlp_out, chip))
        return ring.land(chip)

    grad_normed1 = tp_sum(
        lambda h: dot(half_of(back, h), w_both),
        chips=hold_output,
        totals=lambda v: lands(v, 4),
    )
    mlp_out = late[0]
    ring.drain()
    grads = [g.total() for g in grads]
    low_mixed = mixed.astype(bf16).reshape(rows, lanes)
    grad_matrix = []
    for k in range(2):
        dense = down(low_mixed, grad_gates[k].reshape(rows, lanes)).astype(bf16)
        for h in range(heads):
            at = slice(h * head_width, (h + 1) * head_width)
            grad_matrix.append(dense[at, at])
    packed = jnp.concatenate(
        grad_matrix + [sums.astype(bf16).reshape(-1, head_width)], axis=0
    )
    packed = lax.psum(packed, "seq")

    if tiled:
        output = by_rows(
            output_kernel,
            [middle, mlp_out.reshape(full)],
            [],
            [bf16],
            0,
            move,
            back=True,
            moved=(1,),
        )[0]
        grad_tokens = in_halves(
            start_back_kernel,
            [x, grad_middle],
            [g.reshape(part_full) for g in grad_normed1],
            [gain1],
            [f32],
            0,
            move,
            back=True,
        )[0]
    else:
        mlp_out = mlp_out.reshape(full)[sequence].astype(f32)
        output = own_order((middle + mlp_out).astype(bf16), move, True)
        grad_normed1_all = jnp.concatenate(grad_normed1, axis=0).reshape(full).astype(f32)
        grad_start = norm_back(x.astype(f32), grad_normed1_all, gain1)[0]
        grad_tokens = own_order(grad_middle + grad_start, move, True)
    mine = lax.axis_index("seq")
    slots = (me - jnp.asarray(place, jnp.int32)) % n
    scaled1 = start[:block] * inverse1[:block]
    sum_gain1 = jnp.sum(grad_normed1[0].astype(f32) * scaled1, axis=0)
    grad_gains = jnp.stack([sum_gain1, 0.5 * jnp.sum(sum_gain2, axis=0)])
    grad_gains = grad_gains + core_swap(grad_gains)
    grad_gains = seq_sum(grad_gains.reshape(2, n, part)[:, slots], n)
    grad_gains = lax.dynamic_index_in_dim(grad_gains, mine, 1, keepdims=False)

    packed, grad_gains = lax.optimization_barrier((packed, grad_gains))
    packed = packed.astype(f32)
    matrix_rows = 2 * heads * head_width
    grad_matrix = packed[:matrix_rows].reshape(gate_matrix.shape)
    small = packed[matrix_rows:].reshape(4 + taps, lanes)
    return (
        output,
        grad_tokens,
        grad_gains[0],
        jnp.transpose(jnp.stack(grads), (2, 0, 1)),
        small[4:],
        small[3],
        grad_matrix,
        small[1:3],
        small[0],
        grad_out.total(),
        grad_gains[1],
        grad_mlp.total().reshape(part, 2, units),
        grad_down.total(),
    )


def solution(mesh):
    in_specs = (
        P(None, "seq", None),
        P("seq"),
        P("seq", None, "tp"),
        P(None, "tp"),
        P("tp"),
        P(None, "tp", None, None),
        P(None, "tp"),
        P("tp"),
        P("tp", "seq"),
        P("seq"),
        P("seq", None, "tp"),
        P("tp", "seq"),
        P(None, "seq", None),
    )
    out_specs = (
        P(None, "seq", None),
        P(None, "seq", None),
        P("seq"),
        P("seq", None, "tp"),
        P(None, "tp"),
        P("tp"),
        P(None, "tp", None, None),
        P(None, "tp"),
        P("tp"),
        P("tp", "seq"),
        P("seq"),
        P("seq", None, "tp"),
        P("tp", "seq"),
    )
    return jax.shard_map(shards, mesh=mesh, in_specs=in_specs, out_specs=out_specs, check_vma=False)
```

```python
import functools
import math

import jax
import jax.numpy as jnp
from jax import lax
from jax.experimental import pallas as pl
from jax.experimental.pallas import tpu as pltpu
from jax.sharding import PartitionSpec as P

f32 = jnp.float32
bf16 = jnp.bfloat16
eps = 1e-06
gelu_scale = math.sqrt(2.0 / math.pi)
step_rows = 16
pad_rows = 8
vmem_bytes = 48 * 2**20
ring_most = 8
lane_depth = 2
norm_rows = 128


def ring_order(n):
    return [*range(0, n, 2), *range(n - 1 - n % 2, 0, -2)]


def after(values, *earlier):
    return lax.optimization_barrier((values, *earlier))[0]


class Ring:
    def __init__(self, order, depth):
        n = len(order)
        self.n = n
        self.depth = depth
        self.pairs = {w: [(order[i], order[(i + w) % n]) for i in range(n)] for w in (1, -1)}
        self.queue = {1: [], -1: []}
        self.flying = {1: [], -1: []}
        self.landed = {1: [], -1: []}
        self.sent = {1: 0, -1: 0}
        self.last = {1: None, -1: None}
        self.token = None

    def add(self, weights, delays=None):
        half = self.n // 2
        delays = delays or [0] * len(weights)
        left = {id(flow): flow.count for w in weights for flow in w.flows.values()}
        for turn in range(half + max(delays)):
            for late in (True, False):
                for weight, delay in zip(weights, delays):
                    if (delay > 0) != late or turn < delay:
                        continue
                    for way, flow in weight.flows.items():
                        if left[id(flow)]:
                            left[id(flow)] -= 1
                            self.queue[way].append(flow)

    def issue(self, most=None):
        for way in (1, -1):
            queue, flying, landed = self.queue[way], self.flying[way], self.landed[way]
            while queue and len(flying) < (most or self.depth) and not queue[0].busy:
                flow = queue.pop(0)
                message = flow.message()
                gate = self.sent[way] - self.depth
                if gate >= 0:
                    message = after(message, landed[gate])
                if self.token is not None:
                    message = after(message, self.token)
                flow.busy = True
                self.sent[way] += 1
                self.last[way] = message
                flying.append((flow, lax.ppermute(message, "seq", self.pairs[way])))

    def hold(self, values):
        last = [message for message in self.last.values() if message is not None]
        return after(values, *last) if last else values

    def resume(self, token):
        self.token = token
        self.issue()
        return token

    def quiet(self, values):
        waiting = {w: self.queue[w] for w in (1, -1)}
        self.queue = {1: [], -1: []}
        for _ in range(self.depth):
            values = self.land(values)
        self.queue = waiting
        return values

    def pause(self):
        waiting, self.queue = self.queue, {1: [], -1: []}
        return waiting

    def go(self, waiting, token):
        self.queue = waiting
        self.resume(token)

    def land(self, values=None, count=1):
        for turn in range(count):
            taken = [(w, *self.flying[w].pop(0)) for w in (1, -1) if self.flying[w]]
            arrived = [message for _, _, message in taken]
            if values is not None and taken and turn == count - 1:
                values, *arrived = lax.optimization_barrier((values, *arrived))
            for (way, flow, _), message in zip(taken, arrived):
                flow.arrive(message)
                flow.busy = False
                self.landed[way].append(message)
            self.issue()
        return values

    def drain(self):
        while self.queue[1] or self.queue[-1] or self.flying[1] or self.flying[-1]:
            self.land()


class Pieces:
    def __init__(self, own, count):
        self.value, self.count, self.busy, self.got = own, count, False, []

    def message(self):
        return self.value

    def arrive(self, message):
        self.value = message
        self.got.append(message)


class Totals:
    def __init__(self, part, slots):
        self.part, self.slots, self.count, self.busy = part, slots, len(slots), False
        self.got, self.at = None, 0

    def message(self):
        total = self.part(self.slots[self.at])
        if self.got is not None:
            total = total + self.got.astype(f32)
        self.at += 1
        return total.astype(bf16)

    def arrive(self, message):
        self.got = message


class Gather:
    def __init__(self, piece, far, n, chunk):
        half = n // 2
        self.piece, self.n, self.chunk, self.flows = piece, n, chunk, {}
        if n <= ring_most:
            self.flows = {w: Pieces(piece, half if w == far else half - 1) for w in (1, -1)}

    def slots(self):
        if not self.flows:
            pieces = lax.all_gather(self.piece, "seq")[self.chunk]
            return [pieces[k] for k in range(self.n)]
        return [self.piece, *self.flows[1].got, *self.flows[-1].got[::-1]]


class Scatter:
    def __init__(self, part, far, n, chunk):
        half = n // 2
        self.part, self.n, self.chunk, self.flows = part, n, chunk, {}
        if n <= ring_most:
            self.flows = {
                1: Totals(part, list(range(half if far == 1 else half + 1, n))),
                -1: Totals(part, list(range(half if far == -1 else half - 1, 0, -1))),
            }

    def total(self):
        if not self.flows:
            parts = jnp.stack([self.part(k).astype(bf16) for k in range(self.n)])
            parts = parts[jnp.argsort(self.chunk)]
            return lax.psum_scatter(parts, "seq", scatter_dimension=0).astype(f32)
        total = self.part(0)
        for flow in self.flows.values():
            if flow.got is not None:
                total = total + flow.got.astype(f32)
        return total


def core_swap(values):
    size = lax.axis_size("tp")
    return lax.ppermute(values, "tp", [(i, i ^ 1) for i in range(size)])


def chip_swap(values):
    size = lax.axis_size("tp")
    return lax.ppermute(values, "tp", [(i, i ^ 2) for i in range(size)])


def tp_sum(part, others=lambda v: v, chips=lambda v: v, totals=lambda v: v):
    got = core_swap(others(part(1).astype(bf16)))
    own = lax.optimization_barrier(part(0).astype(bf16))
    chip = chips((own.astype(f32) + got.astype(f32)).astype(bf16))
    far = chip_swap(chip)
    total = totals((chip.astype(f32) + far.astype(f32)).astype(bf16))
    return total, core_swap(total)


def gelu_parts(x):
    t = jnp.tanh(gelu_scale * (x + 0.044715 * x * x * x))
    value = 0.5 * x * (1.0 + t)
    slope = 0.5 * (1.0 + t) + 0.5 * x * (1.0 - t * t) * gelu_scale * (1.0 + 3 * 0.044715 * x * x)
    return value, slope


def drive_square(log_decay, decay):
    y = -2.0 * log_decay
    series = 1.0 - y * (1.0 / 9.0)
    for k in range(8, 1, -1):
        series = 1.0 - y * (1.0 / k) * series
    return jnp.where(y < 0.5, y * series, 1.0 - decay * decay)


def scan_block(a, b, rows, reverse):
    count = a.shape[0]
    by = 1
    while by < count:
        turn = count - by if reverse else by
        pa = pltpu.roll(a, turn, 0)
        pb = pltpu.roll(b, turn, 0)
        inside = rows < count - by if reverse else rows >= by
        b = jnp.where(inside, a * pb + b, b)
        a = jnp.where(inside, a * pa, a)
        by *= 2
    return a, b


def forward_kernel(
    inner, before, conv_w, conv_b, gate_m, gate_b, rate,
    mixed, recur, admit, decay, root, cum, local, ends, ext, gates,
):
    length, lanes = inner.shape
    ext[:pad_rows] = before[...]
    ext[pad_rows:] = inner[...].astype(f32)
    taps = conv_w.shape[0]
    total = jnp.broadcast_to(conv_b[...], (length, lanes))
    for lag in range(taps):
        total = total + conv_w[lag : lag + 1] * ext[pad_rows - lag : pad_rows - lag + length]
    mixed[...] = total
    low = total.astype(bf16)
    for k in range(2):
        gates[k] = jnp.dot(low, gate_m[k], preferred_element_type=f32) + gate_b[k : k + 1]
    rows = lax.broadcasted_iota(jnp.int32, (step_rows, lanes), 0)

    def step(i, carry):
        at = pl.ds(pl.multiple_of(i * step_rows, step_rows), step_rows)
        r = jax.nn.sigmoid(gates[0, at])
        g = jax.nn.sigmoid(gates[1, at])
        log_decay = -8.0 * r * rate[...]
        d = jnp.exp(log_decay)
        m = jnp.sqrt(drive_square(log_decay, d))
        drive = m * g * mixed[at]
        root[at] = m
        recur[at] = r
        admit[at] = g
        decay[at] = d
        a, b = scan_block(d, drive, rows, False)
        b = b + a * carry[1]
        a = a * carry[0]
        cum[at] = a
        local[at] = b
        return a[step_rows - 1 :], b[step_rows - 1 :]

    a, b = lax.fori_loop(
        0, length // step_rows, step, (jnp.ones((1, lanes), f32), jnp.zeros((1, lanes), f32))
    )
    ends[0:1] = a
    ends[1:2] = b
    ends[2:] = jnp.zeros((pad_rows - 2, lanes), f32)


def reverse_kernel(grad_product, act, decay, tail, grad, first, nexts):
    length, lanes = act.shape
    nexts[...] = pltpu.roll(decay[...], length - 1, 0)
    nexts[length - 1 :] = jnp.ones((1, lanes), f32)
    rows = lax.broadcasted_iota(jnp.int32, (step_rows, lanes), 0)
    steps = length // step_rows

    def step(i, carry):
        at = pl.ds(pl.multiple_of((steps - 1 - i) * step_rows, step_rows), step_rows)
        direct = grad_product[at] * act[at]
        a, b = scan_block(nexts[at], direct, rows, True)
        b = b + a * carry[1]
        a = a * carry[0]
        tail[at] = a
        grad[at] = b
        return a[:1], b[:1]

    a, b = lax.fori_loop(0, steps, step, (jnp.ones((1, lanes), f32), jnp.zeros((1, lanes), f32)))
    first[0:1] = decay[0:1] * a
    first[1:2] = decay[0:1] * b
    first[2:] = jnp.zeros((pad_rows - 2, lanes), f32)


def gates_back_kernel(
    grad_product, slope, tail, grad, incoming, states, entry, recur, admit, decay, root, mixed, inner, before,
    gate_m, rate, conv_w, grad_gates, grad_inner, grad_gate_in, head, last, sums, grad_mix, grad_ext, ext,
):
    length, lanes = inner.shape
    enter = entry[0:1]
    later = incoming[0:1]
    taps = conv_w.shape[0]

    def step(i, carry):
        at = pl.ds(pl.multiple_of(i * step_rows, step_rows), step_rows)
        state = states[at]
        rows = lax.broadcasted_iota(jnp.int32, (step_rows, lanes), 0)
        earlier = jnp.where(rows == 0, carry[3], pltpu.roll(state, 1, 0))
        grad_gate_in[at] = (slope[at] * (grad_product[at] * state)).astype(bf16)
        total = grad[at] + tail[at] * later
        r, g, d, m, mix = recur[at], admit[at], decay[at], root[at], mixed[at]
        grad_mix[at] = total * m * g
        both = total * mix
        gate1 = both * m * g * (1.0 - g)
        grad_log = total * earlier * d - both * g * d * d / m
        gate0 = -8.0 * rate[...] * grad_log * r * (1.0 - r)
        low0 = gate0.astype(bf16)
        low1 = gate1.astype(bf16)
        grad_gates[0, at] = low0
        grad_gates[1, at] = low1
        return (
            carry[0] - 8.0 * (grad_log * r),
            carry[1] + low0.astype(f32),
            carry[2] + low1.astype(f32),
            state[step_rows - 1 :],
        )

    zero = jnp.zeros((step_rows, lanes), f32)
    totals = lax.fori_loop(0, length // step_rows, step, (zero, zero, zero, enter))
    back = grad_mix[...]
    for k in range(2):
        back = back + lax.dot_general(
            grad_gates[k], gate_m[k], (((1,), (1,)), ((), ())), preferred_element_type=f32
        )
    back = back.astype(bf16).astype(f32)
    head[...] = back[:pad_rows]
    grad_ext[:length] = back
    grad_ext[length:] = jnp.zeros((pad_rows, lanes), f32)
    ext[:pad_rows] = before[...]
    ext[pad_rows:] = inner[...].astype(f32)

    @pl.when(pl.program_id(0) == 0)
    def _():
        sums[...] = jnp.zeros_like(sums)

    for k in range(3):
        sums[k : k + 1] += jnp.sum(totals[k], axis=0, keepdims=True)
    sums[3:4] += jnp.sum(back, axis=0, keepdims=True)
    total = jnp.zeros((length, lanes), f32)
    for lag in range(taps):
        total = total + conv_w[lag : lag + 1] * grad_ext[lag : lag + length]
        term = back * ext[pad_rows - lag : pad_rows - lag + length]
        sums[4 + lag : 5 + lag] += jnp.sum(term, axis=0, keepdims=True)
    grad_inner[...] = total.astype(bf16)
    last[...] = total[length - pad_rows :]


def hidden_back_kernel(cot, w_down, act, slope, grad_both):
    units = w_down.shape[0]
    cut = math.gcd(units, 512)
    for j in range(0, units, cut):
        grad = lax.dot_general(
            cot[...], w_down[j : j + cut], (((1,), (1,)), ((), ())), preferred_element_type=f32
        )
        grad_both[:, j : j + cut] = (grad * slope[:, j : j + cut].astype(f32)).astype(bf16)
        grad_both[:, units + j : units + j + cut] = (
            grad * act[:, j : j + cut].astype(f32)
        ).astype(bf16)


def per_sequence(kernel, seqs, inputs, outputs, scratch, flops):
    def spec(shape, kind):
        if kind == "whole":
            return pl.BlockSpec(shape, lambda s: (0,) * len(shape))
        if kind == "pair":
            return pl.BlockSpec((shape[0], None) + shape[2:], lambda s: (0, s, 0, 0))
        return pl.BlockSpec((None,) + shape[1:], lambda s: (s,) + (0,) * (len(shape) - 1))

    moved = sum(a.size * a.dtype.itemsize for a, _ in inputs)
    moved += sum(math.prod(shape) * jnp.dtype(t).itemsize for shape, t, _ in outputs)
    return pl.pallas_call(
        kernel,
        grid=(seqs,),
        in_specs=[spec(a.shape, kind) for a, kind in inputs],
        out_specs=[spec(shape, kind) for shape, _, kind in outputs],
        out_shape=[jax.ShapeDtypeStruct(shape, t) for shape, t, _ in outputs],
        scratch_shapes=scratch,
        compiler_params=pltpu.CompilerParams(vmem_limit_bytes=vmem_bytes),
        cost_estimate=pl.CostEstimate(flops=flops, bytes_accessed=moved, transcendentals=0),
    )(*[a for a, _ in inputs])


def moved_bytes(*arrays):
    return sum(math.prod(a.shape) * jnp.dtype(a.dtype).itemsize for a in arrays)


def by_rows(
    kernel, arrays, whole, outputs, sums, order=None, back=False, moved=(), half=None, earlier=()
):
    seqs, length, width = arrays[0].shape
    block = min(norm_rows, length)
    count = seqs if half is None else seqs // 2
    skip = count * (half or 0)
    moves = order is not None
    tile = (None, block, width)
    near = pl.BlockSpec(tile, lambda s, r, *_: (s + skip, r, 0))
    own = pl.BlockSpec(tile, lambda s, r, *_: (s, r, 0))
    far = pl.BlockSpec(tile, lambda s, r, sequence, chunk: (sequence[s + skip], r, 0))
    total = pl.BlockSpec((pad_rows, width), lambda s, r, *_: (0, 0))
    out_shape = [jax.ShapeDtypeStruct((seqs, length, width), t) for t in outputs]
    out_shape += [jax.ShapeDtypeStruct((pad_rows, width), f32)] * sums
    scalars = 2 if moves else 0
    given = scalars + len(arrays) + len(whole)

    def body(*refs):
        kernel(*refs[:given], *refs[given + len(earlier) :])

    return pl.pallas_call(
        body,
        grid_spec=pltpu.PrefetchScalarGridSpec(
            num_scalar_prefetch=scalars,
            grid=(count, length // block),
            in_specs=[
                own
                if a.shape[0] != seqs
                else far
                if moves and (not back or i in moved)
                else near
                for i, a in enumerate(arrays)
            ]
            + [pl.BlockSpec(w.shape, lambda s, r, *_: (0, 0)) for w in whole]
            + [pl.BlockSpec(memory_space=pl.ANY)] * len(earlier),
            out_specs=[far if moves and back else near] * len(outputs) + [total] * sums,
        ),
        out_shape=out_shape,
        input_output_aliases={given + i: i for i in range(len(earlier))},
        compiler_params=pltpu.CompilerParams(vmem_limit_bytes=vmem_bytes),
        cost_estimate=pl.CostEstimate(
            flops=8 * count * length * width,
            bytes_accessed=moved_bytes(*arrays, *out_shape) * count // seqs,
            transcendentals=0,
        ),
    )(*(order if moves else ()), *arrays, *whole, *earlier)


def in_halves(kernel, arrays, summed, whole, outputs, sums, order=None, back=False):
    ready = by_rows(
        kernel, [arrays[0], summed[0], *arrays[1:]], whole, outputs, sums, order, back, (), 0
    )
    count = len(outputs)
    done = by_rows(
        kernel,
        [arrays[0], summed[1], *arrays[1:]],
        whole,
        outputs,
        sums,
        order,
        back,
        (),
        1,
        tuple(ready[:count]),
    )
    return [*done[:count], *(a + b for a, b in zip(ready[count:], done[count:]))]


def enter_kernel(sequence, chunk, *refs):
    count = len(refs) // 2
    part = refs[0].shape[1] // chunk.shape[0]
    for k in range(chunk.shape[0]):
        at = pl.ds(pl.multiple_of(chunk[k] * part, part), part)
        for i in range(count):
            refs[count + i][:, k * part : (k + 1) * part] = refs[i][:, at]


def norm_kernel(x, added, gain, middle, normed):
    total = x[...].astype(f32) + added[...].astype(f32)
    middle[...] = total
    inverse = lax.rsqrt(jnp.mean(total * total, axis=-1, keepdims=True) + eps)
    normed[...] = (total * inverse * gain[...]).astype(bf16)


def norm_back(values, grad, gain):
    inverse = lax.rsqrt(jnp.mean(values * values, axis=-1, keepdims=True) + eps)
    scaled = values * inverse
    weighted = grad * gain
    inner = jnp.mean(weighted * scaled, axis=-1, keepdims=True)
    return inverse * (weighted - scaled * inner), grad * scaled


def add_rows(total, values):
    @pl.when((pl.program_id(0) == 0) & (pl.program_id(1) == 0))
    def _():
        total[...] = jnp.zeros_like(total)

    rows, width = values.shape
    total[...] += jnp.sum(values.reshape(rows // pad_rows, pad_rows, width), axis=0)


def middle_back_kernel(middle, grad_normed, cot, gain, grad_middle, grad_low, total):
    grad, terms = norm_back(middle[...], grad_normed[...].astype(f32), gain[...])
    grad = grad + cot[...].astype(f32)
    grad_middle[...] = grad
    grad_low[...] = grad.astype(bf16)
    add_rows(total, terms)


def put_chunks(chunk, target, values):
    part = values.shape[1] // chunk.shape[0]
    for k in range(chunk.shape[0]):
        at = pl.ds(pl.multiple_of(chunk[k] * part, part), part)
        target[:, at] = values[:, k * part : (k + 1) * part]


def start_back_kernel(sequence, chunk, x, grad_normed, grad_middle, gain, grad_tokens):
    grad = norm_back(x[...].astype(f32), grad_normed[...].astype(f32), gain[...])[0]
    put_chunks(chunk, grad_tokens, grad + grad_middle[...])


def output_kernel(sequence, chunk, middle, added, output):
    put_chunks(chunk, output, (middle[...] + added[...].astype(f32)).astype(bf16))


def own_order(array, order, back=False):
    sequence, chunk = order
    if back:
        sequence, chunk = jnp.argsort(sequence), jnp.argsort(chunk)
    seqs, length, width = array.shape
    chunks = chunk.shape[0]
    split = array[sequence].reshape(seqs, length, chunks, width // chunks)
    return split[:, :, chunk].reshape(array.shape)


def carried(ends, way, n, between=lambda v: v):
    def shifted(values, by):
        pairs = [(i, i + way * by) for i in range(n) if 0 <= i + way * by < n]
        return lax.ppermute(values, "seq", pairs)

    ends = ends[:, :2]
    by = 1
    while 2 * by < n:
        earlier = shifted(ends, by)
        ends = ends[:, :1] * earlier + jnp.concatenate(
            [jnp.zeros_like(ends[:, 1:]), ends[:, 1:]], axis=1
        )
        by *= 2
        if by == 2:
            ends = between(ends)
    near, far = shifted(ends, 1), shifted(ends, 1 + by)
    state = near[:, :1] * far[:, 1:] + near[:, 1:]
    return jnp.pad(state, ((0, 0), (0, pad_rows - 1), (0, 0)))


def seq_sum(values, n):
    by = 1
    while by < n:
        values = values + lax.ppermute(values, "seq", [(i, i ^ by) for i in range(n)])
        by *= 2
    return values


def dense_heads(matrix):
    kinds, heads, width, _ = matrix.shape
    rows = [
        jnp.pad(matrix[:, h], ((0, 0), (0, 0), (h * width, (heads - 1 - h) * width)))
        for h in range(heads)
    ]
    return jnp.concatenate(rows, axis=1)


def across(a, b):
    return lax.dot_general(a, b, (((1,), (1,)), ((), ())), preferred_element_type=f32)


def down(a, b):
    return lax.dot_general(a, b, (((0,), (0,)), ((), ())), preferred_element_type=f32)


def dot(a, b):
    return jnp.dot(a, b, preferred_element_type=f32)


def shards(
    tokens,
    norm1_gain,
    in_weight,
    conv_weight,
    conv_bias,
    gate_matrix,
    gate_bias,
    decay_rate,
    out_weight,
    norm2_gain,
    mlp_weight,
    down_weight,
    cotangent,
):
    seqs, piece, width = tokens.shape
    rows = seqs * piece
    lanes = in_weight.shape[2]
    units = mlp_weight.shape[2]
    heads, head_width = gate_matrix.shape[1:3]
    taps = conv_weight.shape[0]
    n = lax.axis_size("seq")
    part = width // n
    order = ring_order(n)
    place = [order.index(i) for i in range(n)]
    me = jnp.asarray(place, jnp.int32)[lax.axis_index("seq")]
    chunk = jnp.asarray(order, jnp.int32)[(me - jnp.arange(n, dtype=jnp.int32)) % n]
    odd = lax.axis_index("tp") % 2
    sequence = (jnp.arange(seqs, dtype=jnp.int32) + odd * (seqs // 2)) % seqs
    move = (sequence, chunk)
    ring = Ring(order, lane_depth)
    tiled = part % 128 == 0

    def sl(a, k):
        return a[:, k * part : (k + 1) * part]

    move = (sequence, chunk)
    w_in = jnp.transpose(in_weight, (1, 2, 0))
    half_lanes = lanes // 2
    own_gain = jnp.pad(jnp.stack([norm1_gain, norm2_gain]), ((0, 14), (0, 0)))
    first = Gather(jnp.concatenate([w_in[0], out_weight[:half_lanes]], axis=0), 1, n, chunk)
    second = Gather(
        jnp.concatenate([w_in[1], out_weight[half_lanes:], own_gain], axis=0), -1, n, chunk
    )
    mlp = [Gather(mlp_weight[:, 0], 1, n, chunk), Gather(mlp_weight[:, 1], -1, n, chunk)]
    downs = Gather(down_weight, 1, n, chunk)
    ring.add([first, second])
    ring.add([*mlp, downs], [0, 0, 3])
    ring.issue()

    tokens, cotangent = ring.land((tokens, cotangent))
    if tiled:
        x, cot = by_rows(enter_kernel, [tokens, cotangent], [], [bf16, bf16], 0, move)
    else:
        x, cot = own_order(tokens, move), own_order(cotangent, move)
    full = x.shape
    part_full = (seqs // 2, piece, width)
    x, cot = ring.land((x, cot))
    grad_low = cot.reshape(rows, width)
    start = x.reshape(rows, width).astype(f32)
    inverse1 = lax.rsqrt(jnp.mean(start * start, axis=-1, keepdims=True) + eps)
    for _ in range(n - 3):
        ring.land()
    first, second = first.slots(), second.slots()
    in0 = [p[:lanes] for p in first]
    in1 = [p[:lanes] for p in second]
    gains = [p[lanes + half_lanes : lanes + half_lanes + 2] for p in second]
    gain1, gain2 = (
        jnp.concatenate([g[i : i + 1] for g in gains], axis=1).astype(f32) for i in range(2)
    )
    normed1 = [
        (sl(start, k) * inverse1 * gains[k][:1].astype(f32)).astype(bf16) for k in range(n)
    ]
    inner = sum(across(normed1[k], in0[k]) for k in range(n)).astype(bf16)
    gate_in = sum(across(normed1[k], in1[k]) for k in range(n)).astype(bf16)
    inner = ring.land(inner)
    inner = inner.reshape(seqs, piece, lanes)
    gate_in = gate_in.reshape(seqs, piece, lanes)
    before = lax.ppermute(
        inner[:, piece - taps + 1 :], "seq", [(i, i + 1) for i in range(n - 1)]
    ).astype(f32)
    before = ring.land(jnp.pad(before, ((0, 0), (pad_rows - taps + 1, 0), (0, 0))))
    conv_w = conv_weight.astype(f32)
    rate = decay_rate.astype(f32)[None]
    gate_m = dense_heads(gate_matrix)
    wide = (seqs, piece, lanes)
    edge = (seqs, pad_rows, lanes)
    gate_flops = 4 * rows * lanes * lanes
    mixed, recur, admit, decay, root, cum, local, ends = per_sequence(
        forward_kernel,
        seqs,
        [
            (inner, "seq"),
            (before, "seq"),
            (conv_w, "whole"),
            (conv_bias.astype(f32)[None], "whole"),
            (gate_m, "whole"),
            (gate_bias.astype(f32), "whole"),
            (rate, "whole"),
        ],
        [(wide, f32, "seq")] * 7 + [(edge, f32, "seq")],
        [pltpu.VMEM((piece + pad_rows, lanes), f32), pltpu.VMEM((2, piece, lanes), f32)],
        gate_flops,
    )
    entry = ring.land(carried(ring.land(ends), 1, n, ring.land))
    states = local + cum * entry[:, :1]
    product = (states * gelu_parts(gate_in.astype(f32))[0]).astype(bf16).reshape(rows, lanes)
    w_out = jnp.concatenate(
        [
            jnp.concatenate([p[lanes : lanes + half_lanes] for p in pieces], axis=1)
            for pieces in (first, second)
        ],
        axis=0,
    )
    block = rows // 2

    def half_of(a, h):
        return a[h * block : (h + 1) * block]

    def lands(values, count):
        for _ in range(count):
            ring.land()
        return ring.resume(values)

    chips = []

    def keep(chip):
        chips.append(ring.land(chip))
        return chips[0]

    recurrent = tp_sum(
        lambda h: dot(half_of(product, h), w_out),
        chips=keep,
        totals=lambda v: lands(v, 3),
    )
    gate_act, gate_slope = gelu_parts(after(gate_in, chips[0]).astype(f32))

    middle, normed2 = in_halves(
        norm_kernel, [x], [r.reshape(part_full) for r in recurrent], [gain2], [f32, bf16], 0
    )
    normed2 = ring.land(normed2.reshape(rows, width))
    w_mlp = jnp.concatenate([jnp.concatenate(w.slots(), axis=0) for w in mlp], axis=1)
    both = dot(normed2, w_mlp).astype(bf16)
    both0, both1 = both[:, :units].astype(f32), both[:, units:].astype(f32)
    act, slope = gelu_parts(both0)
    hidden = (act * both1).astype(bf16)
    hidden, act, slope = ring.land((hidden, act.astype(bf16), (slope * both1).astype(bf16)))
    ring.drain()
    w_down = jnp.concatenate(downs.slots(), axis=1)
    ring.token = None
    grad_both = []
    grad_down = Scatter(lambda k: down(hidden, sl(grad_low, k)), 1, n, chunk)
    grad_mlp = Scatter(lambda k: down(sl(normed2, k), grad_both[0]), -1, n, chunk)
    ring.add([grad_down, grad_mlp])
    ring.issue(1)
    act, slope, w_down = ring.hold((act, slope, w_down))
    grad_both.append(
        pl.pallas_call(
            hidden_back_kernel,
            grid=(seqs,),
            in_specs=[
                pl.BlockSpec((piece, width), lambda s: (s, 0)),
                pl.BlockSpec((units, width), lambda s: (0, 0)),
                pl.BlockSpec((piece, units), lambda s: (s, 0)),
                pl.BlockSpec((piece, units), lambda s: (s, 0)),
            ],
            out_specs=pl.BlockSpec((piece, 2 * units), lambda s: (s, 0)),
            out_shape=jax.ShapeDtypeStruct((rows, 2 * units), bf16),
            compiler_params=pltpu.CompilerParams(vmem_limit_bytes=vmem_bytes),
            cost_estimate=pl.CostEstimate(
                flops=2 * rows * width * units,
                bytes_accessed=moved_bytes(grad_low, w_down, act, slope, both),
                transcendentals=0,
            ),
        )(grad_low, w_down, act, slope)
    )
    ring.issue()
    grad_normed2 = tp_sum(
        lambda h: across(half_of(grad_both[0], h), w_mlp),
        others=ring.land,
        totals=lambda v: ring.land((ring.land(), v)[1]),
    )
    turned = jnp.concatenate([half_of(hidden, 1), half_of(hidden, 0)], axis=0)
    turned = jnp.where(odd == 1, turned, hidden)

    grad_middle, grad_rec, sum_gain2 = in_halves(
        middle_back_kernel,
        [middle, cot],
        [g.reshape(part_full) for g in grad_normed2],
        [gain2],
        [f32, bf16],
        1,
    )
    grad_out = Scatter(lambda k: down(product, sl(grad_rec, k)), 1, n, chunk)
    ring.add([grad_out])
    waiting = ring.pause()
    grad_rec = ring.land(grad_rec.reshape(rows, width))

    grad_product = across(grad_rec, w_out).reshape(wide)
    tail, local_grad, early = per_sequence(
        reverse_kernel,
        seqs,
        [(grad_product, "seq"), (gate_act, "seq"), (decay, "seq")],
        [(wide, f32, "seq")] * 2 + [(edge, f32, "seq")],
        [pltpu.VMEM((piece, lanes), f32)],
        rows * lanes * 50,
    )
    rounds = []

    def keep_round(ends):
        rounds.append(ends)
        return ends

    incoming = carried(ring.land(early), -1, n, keep_round)
    ring.go(waiting, incoming)
    mlp_out = lax.psum(dot(after(turned, *rounds), w_down).astype(bf16), "tp")
    grad_gates, grad_inner, grad_gate_in, head, last, sums = per_sequence(
        gates_back_kernel,
        seqs,
        [
            (grad_product, "seq"),
            (gate_slope, "seq"),
            (tail, "seq"),
            (local_grad, "seq"),
            (incoming, "seq"),
            (states, "seq"),
            (entry, "seq"),
            (recur, "seq"),
            (admit, "seq"),
            (decay, "seq"),
            (root, "seq"),
            (mixed, "seq"),
            (inner, "seq"),
            (before, "seq"),
            (gate_m, "whole"),
            (rate, "whole"),
            (conv_w, "whole"),
        ],
        [
            ((2,) + wide, bf16, "pair"),
            (wide, bf16, "seq"),
            (wide, bf16, "seq"),
            (edge, f32, "seq"),
            (edge, f32, "seq"),
            ((pad_rows, lanes), f32, "whole"),
        ],
        [pltpu.VMEM((piece, lanes), f32)] + [pltpu.VMEM((piece + pad_rows, lanes), f32)] * 2,
        gate_flops,
    )
    behind = lax.ppermute(
        head[:, : taps - 1].astype(bf16), "seq", [(i + 1, i) for i in range(n - 1)]
    ).astype(f32)
    beyond = jnp.concatenate([jnp.zeros_like(last), behind], axis=1)
    beyond = jnp.pad(beyond, ((0, 0), (0, 1), (0, 0)))
    for lag in range(1, taps):
        last = last + conv_w[lag] * beyond[:, lag : lag + pad_rows]
    grad_inner = lax.dynamic_update_slice(
        grad_inner, last.astype(bf16), (0, piece - pad_rows, 0)
    )
    back0 = grad_inner.reshape(rows, lanes)
    back1 = grad_gate_in.reshape(rows, lanes)
    back = ring.land(jnp.concatenate([back0, back1], axis=1))
    w_both = jnp.concatenate([jnp.concatenate(in0, axis=1), jnp.concatenate(in1, axis=1)], axis=0)
    grads = [
        Scatter(lambda k: down(back0, normed1[k]), 1, n, chunk),
        Scatter(lambda k: down(back1, normed1[k]), -1, n, chunk),
    ]
    ring.add(grads)
    ring.issue()
    late = []

    def hold_output(chip):
        late.append(after(mlp_out, chip))
        return ring.land(chip)

    grad_normed1 = tp_sum(
        lambda h: dot(half_of(back, h), w_both),
        chips=hold_output,
        totals=lambda v: lands(v, 5),
    )
    mlp_out = late[0]
    ring.drain()
    grads = [g.total() for g in grads]
    low_mixed = mixed.astype(bf16).reshape(rows, lanes)
    grad_matrix = []
    for k in range(2):
        dense = down(low_mixed, grad_gates[k].reshape(rows, lanes)).astype(bf16)
        for h in range(heads):
            at = slice(h * head_width, (h + 1) * head_width)
            grad_matrix.append(dense[at, at])
    packed = jnp.concatenate(
        grad_matrix + [sums.astype(bf16).reshape(-1, head_width)], axis=0
    )
    packed = lax.psum(packed, "seq")

    if tiled:
        output = by_rows(
            output_kernel,
            [middle, mlp_out.reshape(full)],
            [],
            [bf16],
            0,
            move,
            back=True,
            moved=(1,),
        )[0]
        grad_tokens = in_halves(
            start_back_kernel,
            [x, grad_middle],
            [g.reshape(part_full) for g in grad_normed1],
            [gain1],
            [f32],
            0,
            move,
            back=True,
        )[0]
    else:
        mlp_out = mlp_out.reshape(full)[sequence].astype(f32)
        output = own_order((middle + mlp_out).astype(bf16), move, True)
        grad_normed1_all = jnp.concatenate(grad_normed1, axis=0).reshape(full).astype(f32)
        grad_start = norm_back(x.astype(f32), grad_normed1_all, gain1)[0]
        grad_tokens = own_order(grad_middle + grad_start, move, True)
    mine = lax.axis_index("seq")
    slots = (me - jnp.asarray(place, jnp.int32)) % n
    scaled1 = start[:block] * inverse1[:block]
    sum_gain1 = jnp.sum(grad_normed1[0].astype(f32) * scaled1, axis=0)
    grad_gains = jnp.stack([sum_gain1, 0.5 * jnp.sum(sum_gain2, axis=0)])
    grad_gains = grad_gains + core_swap(grad_gains)
    grad_gains = seq_sum(grad_gains.reshape(2, n, part)[:, slots], n)
    grad_gains = lax.dynamic_index_in_dim(grad_gains, mine, 1, keepdims=False)

    packed, grad_gains = lax.optimization_barrier((packed, grad_gains))
    packed = packed.astype(f32)
    matrix_rows = 2 * heads * head_width
    grad_matrix = packed[:matrix_rows].reshape(gate_matrix.shape)
    small = packed[matrix_rows:].reshape(4 + taps, lanes)
    return (
        output,
        grad_tokens,
        grad_gains[0],
        jnp.transpose(jnp.stack(grads), (2, 0, 1)),
        small[4:],
        small[3],
        grad_matrix,
        small[1:3],
        small[0],
        grad_out.total(),
        grad_gains[1],
        grad_mlp.total().reshape(part, 2, units),
        grad_down.total(),
    )


def solution(mesh):
    in_specs = (
        P(None, "seq", None),
        P("seq"),
        P("seq", None, "tp"),
        P(None, "tp"),
        P("tp"),
        P(None, "tp", None, None),
        P(None, "tp"),
        P("tp"),
        P("tp", "seq"),
        P("seq"),
        P("seq", None, "tp"),
        P("tp", "seq"),
        P(None, "seq", None),
    )
    out_specs = (
        P(None, "seq", None),
        P(None, "seq", None),
        P("seq"),
        P("seq", None, "tp"),
        P(None, "tp"),
        P("tp"),
        P(None, "tp", None, None),
        P(None, "tp"),
        P("tp"),
        P("tp", "seq"),
        P("seq"),
        P("seq", None, "tp"),
        P("tp", "seq"),
    )
    return jax.shard_map(shards, mesh=mesh, in_specs=in_specs, out_specs=out_specs, check_vma=False)
```
